32 devices in a mesh: section: 2 (over core), dp: 4 (over z), tensor: 4 (over y, x).
Axes of the slice: x: 2, y: 2, z: 4, core: 2. Of those that a mesh axis runs over, the one named last changes fastest.
Arguments:
- ends_in: bfloat16 [2, 2, 8, 2048, 1024], P('section', None, 'dp', 'tensor'), may hold values from -6 to 6
- lengths: int32 [2, 8], P(None, 'dp'), may hold values from 32 to 2048, as said below
- ln_gains: float32 [2, 2, 1024], P('section'), may hold values from 0.5 to 1.5
- ln_biases: float32 [2, 2, 1024], P('section'), may hold values from -1.5 to 1.5
- w_qkv: bfloat16 [2, 3, 1024, 1024], P('section', None, None, 'tensor'), may hold values from -0.1875 to 0.1875
- qv_bias: float32 [2, 2, 1024], P('section', None, 'tensor'), may hold values from -1.5 to 1.5
- w_out: bfloat16 [2, 1024, 1024], P('section', 'tensor'), may hold values from -0.75 to 0.75
- w_up: bfloat16 [2, 1024, 4096], P('section', None, 'tensor'), may hold values from -0.1875 to 0.1875
- up_bias: float32 [2, 4096], P('section', 'tensor'), may hold values from -1.5 to 1.5
- w_down: bfloat16 [2, 4096, 1024], P('section', 'tensor'), may hold values from -0.09375 to 0.09375
- out_biases: float32 [2, 2, 1024], P('section'), may hold values from -1.5 to 1.5
Outputs:
- ends_out: float32 [2, 2, 8, 2048, 1024], P('section', None, 'dp', 'tensor')
- grad_ln_gains: float32 [2, 2, 1024], P('section')
- grad_ln_biases: float32 [2, 2, 1024], P('section')
- grad_qkv: float32 [2, 3, 1024, 1024], P('section', None, None, 'tensor')
- grad_qv_bias: float32 [2, 2, 1024], P('section', None, 'tensor')
- grad_out: float32 [2, 1024, 1024], P('section', 'tensor')
- grad_up: float32 [2, 1024, 4096], P('section', None, 'tensor')
- grad_up_bias: float32 [2, 4096], P('section', 'tensor')
- grad_down: float32 [2, 4096, 1024], P('section', 'tensor')
- grad_out_biases: float32 [2, 2, 1024], P('section')
The draws below stay inside these ranges and needn't reach their ends.
Inputs may be any that keep to these rules, and one draw needn't show every extreme that they name: `lengths`: in every micro-batch each aligned block of 2 rows (the rows of one index of dp) holds one row of length 2048.
All inputs are finite; a program needn't handle non-finite values.
Results may differ from the reference program's by a relative error of at most 0.017.
Values may be sent and summed in bfloat16 or wider, within the bound.
No kernel may reach another device: no remote copies, remote signals or barrier semaphores. Data moves between devices by JAX's collectives and lax.ppermute only.
A program may use at most 512 MiB of HBM per device.

```python
import jax
import jax.numpy as jnp
from jax import lax

D = 1024
HEADS = 16
FF = 4096
SEQ_LEN = 2048
MB = 2
ROWS = 2
BATCH = 8


def draw_lengths(key, part):
    key = jax.random.fold_in(key, 11)
    first_key, second_key, third_key = jax.random.split(key, 3)
    first_step = jax.random.randint(first_key, (MB, BATCH), 1, 65)
    second_step = jax.random.randint(second_key, (MB, BATCH), 1, 65)
    steps_used = jnp.maximum(first_step, second_step)
    drawn = SEQ_LEN * steps_used // 64
    groups = BATCH // ROWS
    chosen = jax.random.randint(third_key, (MB, groups), 0, ROWS)
    full_row = (jnp.arange(ROWS)[None, None, :] == chosen[:, :, None]).reshape(MB, BATCH)
    return jnp.where(full_row, SEQ_LEN, drawn).astype(jnp.int32)


def steps_of(rng, dims, shards, least, high):
    loudness, own = 1.0, jax.random.fold_in(rng, 6)
    for position, shards_of in shards:
        heights = jnp.exp(jax.random.uniform(jax.random.fold_in(own, position), (shards_of,), jnp.float32, least / len(shards), high / len(shards)))
        loudness = loudness * jnp.repeat(heights, dims[position] // shards_of).reshape([-1 if axis == position else 1 for axis in range(len(dims))])
    return loudness


def scatter_about(own_key, shape, scale, bound, cuts=(), held_as=jnp.bfloat16):
    level = steps_of(own_key, shape, cuts, -0.22, 0.18) if cuts else 1.0
    array = jax.random.normal(own_key, shape, jnp.float32) * scale * level
    return jnp.minimum(jnp.maximum(array, -bound), bound).astype(held_as)


def setup_inputs(seed: int = 0) -> dict:
    splits = jax.random.split(jax.random.key(seed), 12)
    ends_in = scatter_about(splits[0], (2, MB, BATCH, SEQ_LEN, D), 1.0, 6.0, ((0, 2), (2, 4), (3, 4)))
    lengths = draw_lengths(jax.random.fold_in(splits[11], 71), 0)
    ln_gains = jnp.clip(1.0 + 0.1 * jax.random.normal(splits[2], (2, 2, D), jnp.float32), 0.5, 1.5)
    ln_biases = scatter_about(splits[3], (2, 2, D), 0.3, 1.5, ((0, 2),), jnp.float32)
    w_qkv = scatter_about(splits[4], (2, 3, D, D), D ** -0.5, 0.1875, ((0, 2), (3, 4)))
    qv_bias = scatter_about(splits[5], (2, 2, D), 0.3, 1.5, ((0, 2), (2, 4)), jnp.float32)
    w_out = scatter_about(splits[6], (2, D, D), (D // 16) ** -0.5, 0.75, ((0, 2), (1, 4)))
    w_up = scatter_about(splits[7], (2, D, FF), D ** -0.5, 0.1875, ((0, 2), (2, 4)))
    up_bias = scatter_about(splits[8], (2, FF), 0.3, 1.5, ((0, 2), (1, 4)), jnp.float32)
    w_down = scatter_about(splits[9], (2, FF, D), FF ** -0.5, 0.09375, ((0, 2), (1, 4)))
    out_biases = scatter_about(splits[10], (2, 2, D), 0.3, 1.5, ((0, 2),), jnp.float32)
    return {"ends_in": ends_in, "lengths": lengths, "ln_gains": ln_gains, "ln_biases": ln_biases, "w_qkv": w_qkv, "qv_bias": qv_bias, "w_out": w_out, "w_up": w_up, "up_bias": up_bias, "w_down": w_down, "out_biases": out_biases}


@jax.custom_vjp
def low(v):
    return lax.optimization_barrier(v.astype(jnp.bfloat16)).astype(jnp.float32)

@jax.custom_vjp
def low_back(v):
    return v

def low_keep(v):
    return (low(v), None)

def low_pass(kept, grad):
    return (grad,)

def back_keep(v):
    return (v, None)

def back_low(kept, grad):
    return (low(grad),)
low.defvjp(low_keep, low_pass)
low_back.defvjp(back_keep, back_low)
highest = lax.Precision.HIGHEST
eps = 1e-05

def product(left, right):
    return jnp.dot(left, right, precision=highest, preferred_element_type=jnp.float32)

def layer_norm(inputs, gain, bias):
    center = lax.optimization_barrier(jnp.mean(inputs, axis=-1, keepdims=True))
    centred = inputs - center
    spread = lax.optimization_barrier(jnp.mean(centred * centred, axis=-1, keepdims=True))
    return centred * lax.rsqrt(spread + eps) * gain + bias

def attend(queries, key_rows, value_rows, length):
    block_rows = min(512, SEQ_LEN)
    head_size = D // HEADS
    scale = head_size ** (-0.5)
    slopes_all = jnp.exp2(-8.0 * (jnp.arange(HEADS).astype(jnp.float32) + 1.0) / HEADS)
    keypos = jnp.arange(SEQ_LEN).astype(jnp.int32)
    query_heads = queries.reshape(SEQ_LEN, HEADS, head_size)
    key_heads = key_rows.reshape(SEQ_LEN, HEADS, head_size)
    value_heads = value_rows.reshape(SEQ_LEN, HEADS, head_size)

    @jax.checkpoint
    def one_block(row_start):
        query_block = lax.dynamic_slice_in_dim(query_heads, row_start, block_rows, 0)
        rowpos = row_start + jnp.arange(block_rows).astype(jnp.int32)
        scores = jnp.einsum('qhd,khd->hqk', query_block, key_heads, precision=highest) * scale
        distance = (rowpos[:, None] - keypos[None, :]).astype(jnp.float32)
        scores = scores - slopes_all[:, None, None] * distance[None]
        allowed = (keypos[None, :] <= rowpos[:, None]) & (keypos[None, :] < length)
        scores = low_back(jnp.where(allowed[None], scores, -1e+30))
        row_max = lax.optimization_barrier(jnp.max(scores, axis=-1, keepdims=True))
        powers = jnp.exp(scores - row_max)
        probs = low(powers / lax.optimization_barrier(jnp.sum(powers, axis=-1, keepdims=True)))
        return jnp.einsum('hqk,khd->qhd', probs, value_heads, precision=highest)
    starts = (jnp.arange(SEQ_LEN // block_rows) * block_rows).astype(jnp.int32)
    blocks_out = lax.map(one_block, starts)
    return blocks_out.reshape(SEQ_LEN, D)

def layer(inputs, row_lengths, params):
    gains, biases, w_proj, proj_bias, w_attn, w_first, first_bias, w_second, end_biases = params
    normed = low(layer_norm(inputs, gains[0], biases[0]))
    queries = low(low_back(product(normed, w_proj[0]) + proj_bias[0]))
    key_rows = low(low_back(product(normed, w_proj[1])))
    value_rows = low(low_back(product(normed, w_proj[2]) + proj_bias[1]))
    attended = lax.map(lambda parts: attend(parts[0], parts[1], parts[2], parts[3]), (queries, key_rows, value_rows, row_lengths))
    attended = low(low_back(attended))
    after_attn = inputs + low_back(product(attended, w_attn)) + end_biases[0]
    middle = low(layer_norm(after_attn, gains[1], biases[1]))
    pre_act = low_back(product(middle, w_first) + first_bias)
    hidden = low(jax.nn.gelu(pre_act, approximate=True))
    return after_attn + low_back(product(hidden, w_second)) + end_biases[1]

def reference(ends_in, lengths, ln_gains, ln_biases, w_qkv, qv_bias, w_out, w_up, up_bias, w_down, out_biases):
    inputs = ends_in[0].astype(jnp.float32)
    cotangent = ends_in[1].astype(jnp.float32)
    params = (ln_gains, ln_biases, w_qkv.astype(jnp.float32), qv_bias, w_out.astype(jnp.float32), w_up.astype(jnp.float32), up_bias, w_down.astype(jnp.float32), out_biases)

    def network(first_in, weights):
        lower = tuple((stored[0] for stored in weights))
        upper = tuple((stored[1] for stored in weights))

        def micro_batch(pair):
            block_in, block_lengths = pair
            middle_out = layer(block_in, block_lengths, lower)
            return layer(low(low_back(middle_out)), block_lengths, upper)
        return lax.map(micro_batch, (first_in, lengths))
    outputs, pullback = jax.vjp(network, inputs, params)
    grad_in, grads = pullback(cotangent)
    return (jnp.stack([grad_in, outputs]), grads[0], grads[1], grads[2], grads[3], grads[4], grads[5], grads[6], grads[7], grads[8])
```

```python
from functools import partial

import jax
import jax.numpy as jnp
from jax import lax
from jax.experimental import pallas as pl
from jax.experimental.pallas import tpu as pltpu
from jax.sharding import PartitionSpec as P

D = 1024
HEADS = 16


eps = 1e-05
widest = 512


def shifted(shard, axis, by):
    devices = lax.axis_size(axis)
    pairs = [(i, i + by) for i in range(devices) if 0 <= i + by < devices]
    return lax.ppermute(shard, axis, pairs)


def layer_norm(inputs, gain, bias):
    center = jnp.mean(inputs, axis=-1, keepdims=True)
    centred = inputs - center
    spread = jnp.mean(centred * centred, axis=-1, keepdims=True)
    factor = lax.rsqrt(spread + eps)
    normal = centred * factor
    return (normal * gain + bias, normal, factor)


def norm_back(grad_norm, normal, factor, gain):
    scaled = grad_norm * gain
    first_mean = jnp.mean(scaled, axis=-1, keepdims=True)
    second_mean = jnp.mean(scaled * normal, axis=-1, keepdims=True)
    return factor * (scaled - first_mean - normal * second_mean)


def gather_tokens(values):
    return lax.all_gather(values, "tensor", axis=1, tiled=True)


def scatter_tokens(values):
    return lax.psum_scatter(values, "tensor", scatter_dimension=1, tiled=True)


def gather_grads(values):
    return lax.all_gather(values, "tensor", axis=1, tiled=True)


def scatter_grads(values):
    return lax.psum_scatter(
        values.astype(jnp.bfloat16), "tensor", scatter_dimension=1, tiled=True
    ).astype(jnp.float32)


def project(whole_rows, w_proj, proj_bias):
    combined = jnp.einsum("rld,cde->crle", whole_rows, w_proj, preferred_element_type=jnp.float32)
    queries = (combined[0] + proj_bias[0]).astype(jnp.bfloat16)
    key_rows = combined[1].astype(jnp.bfloat16)
    value_rows = (combined[2] + proj_bias[1]).astype(jnp.bfloat16)
    return (queries, key_rows, value_rows)


def score_block(query_block, key_heads, row_start, row_lengths, slopes_here):
    block_rows = query_block.shape[1]
    seq_len = key_heads.shape[1]
    head_size = key_heads.shape[-1]
    scores = jnp.einsum(
        "rqhd,rkhd->rhqk", query_block, key_heads, preferred_element_type=jnp.float32
    ) * head_size ** (-0.5)
    rowpos = row_start + jnp.arange(block_rows)
    keypos = jnp.arange(seq_len)
    distance = (rowpos[:, None] - keypos[None, :]).astype(jnp.float32)
    scores = scores - slopes_here[None, :, None, None] * distance[None, None]
    causal = keypos[None, :] <= rowpos[:, None]
    inside = keypos[None, :] < row_lengths[:, None]
    allowed = causal[None, None] & inside[:, None, None, :]
    return jnp.where(allowed, scores, -1e30)


def attention(queries, key_rows, value_rows, row_lengths, slopes_here):
    row_count, seq_len, width = queries.shape
    head_count = slopes_here.shape[0]
    head_size = width // head_count
    block_rows = min(widest, seq_len)
    query_heads = queries.reshape(row_count, seq_len, head_count, head_size)
    key_heads = key_rows.reshape(row_count, seq_len, head_count, head_size)
    value_heads = value_rows.reshape(row_count, seq_len, head_count, head_size)

    def one_block(row_start):
        query_block = lax.dynamic_slice_in_dim(query_heads, row_start, block_rows, 1)
        scores = score_block(query_block, key_heads, row_start, row_lengths, slopes_here)
        row_max = jnp.max(scores, axis=-1, keepdims=True)
        powers = jnp.exp(scores - row_max)
        row_total = jnp.sum(powers, axis=-1, keepdims=True)
        probs = (powers / row_total).astype(jnp.bfloat16)
        block_out = jnp.einsum(
            "rhqk,rkhd->rqhd", probs, value_heads, preferred_element_type=jnp.float32
        )
        return (block_out.astype(jnp.bfloat16), (row_max + jnp.log(row_total))[..., 0])

    starts = jnp.arange(seq_len // block_rows) * block_rows
    blocks_out, log_totals = lax.map(one_block, starts)
    attended = jnp.moveaxis(blocks_out, 0, 1).reshape(row_count, seq_len, width)
    log_totals = jnp.moveaxis(log_totals, 0, 2).reshape(row_count, head_count, seq_len)
    return (attended, log_totals)


def attention_back(
    queries, key_rows, value_rows, grad_attended, log_totals, row_lengths, slopes_here
):
    row_count, seq_len, width = queries.shape
    head_count = slopes_here.shape[0]
    head_size = width // head_count
    scale = head_size ** (-0.5)
    block_rows = min(widest, seq_len)
    query_heads = queries.reshape(row_count, seq_len, head_count, head_size)
    key_heads = key_rows.reshape(row_count, seq_len, head_count, head_size)
    value_heads = value_rows.reshape(row_count, seq_len, head_count, head_size)
    grad_heads = grad_attended.reshape(row_count, seq_len, head_count, head_size)

    def one_block(carry, row_start):
        grad_keys, grad_values = carry
        query_block = lax.dynamic_slice_in_dim(query_heads, row_start, block_rows, 1)
        grad_block = lax.dynamic_slice_in_dim(grad_heads, row_start, block_rows, 1)
        scores = score_block(query_block, key_heads, row_start, row_lengths, slopes_here)
        block_logs = lax.dynamic_slice_in_dim(log_totals, row_start, block_rows, 2)
        probs = jnp.exp(scores - block_logs[..., None])
        grad_values = grad_values + jnp.einsum(
            "rhqk,rqhd->rkhd",
            probs.astype(jnp.bfloat16),
            grad_block,
            preferred_element_type=jnp.float32,
        )
        grad_probs = jnp.einsum(
            "rqhd,rkhd->rhqk", grad_block, value_heads, preferred_element_type=jnp.float32
        )
        inner = jnp.sum(probs * grad_probs, axis=-1, keepdims=True)
        grad_scores = (probs * (grad_probs - inner)).astype(jnp.bfloat16)
        grad_query = (
            jnp.einsum(
                "rhqk,rkhd->rqhd", grad_scores, key_heads, preferred_element_type=jnp.float32
            )
            * scale
        )
        grad_keys = (
            grad_keys
            + jnp.einsum(
                "rhqk,rqhd->rkhd", grad_scores, query_block, preferred_element_type=jnp.float32
            )
            * scale
        )
        return ((grad_keys, grad_values), grad_query.astype(jnp.bfloat16))

    zeros_heads = jnp.zeros((row_count, seq_len, head_count, head_size), jnp.float32)
    starts = jnp.arange(seq_len // block_rows) * block_rows
    (grad_keys, grad_values), grad_queries = lax.scan(one_block, (zeros_heads, zeros_heads), starts)
    grad_queries = jnp.moveaxis(grad_queries, 0, 1).reshape(row_count, seq_len, width)
    grad_keys = grad_keys.reshape(row_count, seq_len, width).astype(jnp.bfloat16)
    grad_values = grad_values.reshape(row_count, seq_len, width).astype(jnp.bfloat16)
    return (grad_queries, grad_keys, grad_values)


def layer_forward(inputs, row_lengths, weights, slopes_here):
    gains, biases, w_proj, proj_bias, w_attn, w_first, first_bias, w_second, end_biases = weights
    normed, _, _ = layer_norm(inputs, gains[0], biases[0])
    whole_rows = gather_tokens(normed.astype(jnp.bfloat16))
    queries, key_rows, value_rows = project(whole_rows, w_proj, proj_bias)
    attended, log_totals = attention(queries, key_rows, value_rows, row_lengths, slopes_here)
    attn_part = jnp.dot(attended, w_attn, preferred_element_type=jnp.float32)
    after_attn = inputs + scatter_tokens(attn_part) + end_biases[0]
    middle, _, _ = layer_norm(after_attn, gains[1], biases[1])
    middle_rows = gather_tokens(middle.astype(jnp.bfloat16))
    pre_act = jnp.dot(middle_rows, w_first, preferred_element_type=jnp.float32) + first_bias
    hidden = jax.nn.gelu(pre_act, approximate=True).astype(jnp.bfloat16)
    ffn_part = jnp.dot(hidden, w_second, preferred_element_type=jnp.float32)
    result = after_attn + scatter_tokens(ffn_part) + end_biases[1]
    return (result, after_attn, attended, log_totals, whole_rows, middle_rows)


def layer_backward(grad_result, stored, row_lengths, weights, slopes_here):
    gains, biases, w_proj, proj_bias, w_attn, w_first, first_bias, w_second, end_biases = weights
    inputs = stored[0].astype(jnp.float32)
    after_attn = stored[1]
    attended = stored[2]
    log_totals = stored[3]
    normed, normal_one, factor_one = layer_norm(inputs, gains[0], biases[0])
    middle, normal_two, factor_two = layer_norm(after_attn, gains[1], biases[1])
    whole_rows = gather_tokens(normed.astype(jnp.bfloat16))
    middle_rows = gather_tokens(middle.astype(jnp.bfloat16))
    pre_act = jnp.dot(middle_rows, w_first, preferred_element_type=jnp.float32) + first_bias
    hidden, gelu_pull = jax.vjp(partial(jax.nn.gelu, approximate=True), pre_act)
    hidden = hidden.astype(jnp.bfloat16)
    grad_end_two = jnp.sum(grad_result, axis=(0, 1))
    grad_branch = gather_grads(grad_result.astype(jnp.bfloat16))
    grad_second = jnp.einsum("rlf,rld->fd", hidden, grad_branch, preferred_element_type=jnp.float32)
    grad_hidden = jnp.einsum(
        "rld,fd->rlf", grad_branch, w_second, preferred_element_type=jnp.float32
    )
    grad_pre = gelu_pull(grad_hidden)[0].astype(jnp.bfloat16)
    grad_first_bias = jnp.sum(grad_pre, axis=(0, 1), dtype=jnp.float32)
    grad_first = jnp.einsum(
        "rld,rlf->df", middle_rows, grad_pre, preferred_element_type=jnp.float32
    )
    grad_middle = scatter_grads(
        jnp.einsum("rlf,df->rld", grad_pre, w_first, preferred_element_type=jnp.float32)
    )
    grad_gain_two = jnp.sum(grad_middle * normal_two, axis=(0, 1))
    grad_bias_two = jnp.sum(grad_middle, axis=(0, 1))
    grad_after = grad_result + norm_back(grad_middle, normal_two, factor_two, gains[1])
    grad_end_one = jnp.sum(grad_after, axis=(0, 1))
    grad_attn_rows = gather_grads(grad_after.astype(jnp.bfloat16))
    grad_attn = jnp.einsum(
        "rle,rld->ed", attended, grad_attn_rows, preferred_element_type=jnp.float32
    )
    grad_attended = jnp.einsum(
        "rld,ed->rle", grad_attn_rows, w_attn, preferred_element_type=jnp.float32
    ).astype(jnp.bfloat16)
    queries, key_rows, value_rows = project(whole_rows, w_proj, proj_bias)
    grad_queries, grad_keys, grad_values = attention_back(
        queries, key_rows, value_rows, grad_attended, log_totals, row_lengths, slopes_here
    )
    stacked = jnp.stack([grad_queries, grad_keys, grad_values])
    grad_proj = jnp.einsum("rld,crle->cde", whole_rows, stacked, preferred_element_type=jnp.float32)
    grad_proj_bias = jnp.stack(
        [
            jnp.sum(grad_queries, axis=(0, 1), dtype=jnp.float32),
            jnp.sum(grad_values, axis=(0, 1), dtype=jnp.float32),
        ]
    )
    grad_normed = scatter_grads(
        jnp.einsum("crle,cde->rld", stacked, w_proj, preferred_element_type=jnp.float32)
    )
    grad_gain_one = jnp.sum(grad_normed * normal_one, axis=(0, 1))
    grad_bias_one = jnp.sum(grad_normed, axis=(0, 1))
    grad_inputs = grad_after + norm_back(grad_normed, normal_one, factor_one, gains[0])
    sharded = (grad_proj, grad_proj_bias, grad_attn, grad_first, grad_first_bias, grad_second)
    shared = (
        jnp.stack([grad_gain_one, grad_gain_two]),
        jnp.stack([grad_bias_one, grad_bias_two]),
        jnp.stack([grad_end_one, grad_end_two]),
    )
    return (grad_inputs, sharded, shared)


def on_device(
    ends_in, lengths, ln_gains, ln_biases, w_qkv, qv_bias, w_out, w_up, up_bias, w_down, out_biases
):
    section_index = lax.axis_index("section")
    weights = tuple(
        (
            stored[0]
            for stored in (
                ln_gains,
                ln_biases,
                w_qkv,
                qv_bias,
                w_out,
                w_up,
                up_bias,
                w_down,
                out_biases,
            )
        )
    )
    local_ends = ends_in[0]
    micro_count = local_ends.shape[0]
    heads_here = w_qkv.shape[-1] // (D // HEADS)
    first_head = lax.axis_index("tensor") * heads_here
    slopes_here = jnp.exp2(
        -8.0 * (first_head + jnp.arange(heads_here) + 1).astype(jnp.float32) / HEADS
    )
    padded = jnp.concatenate([local_ends, jnp.zeros_like(local_ends[:1])], axis=0)
    tick_list = jnp.arange(micro_count + 1)

    def forward_tick(received, item):
        arriving, tick_index = item
        entering = jnp.where(section_index == 0, arriving, received)
        slot_index = jnp.clip(tick_index - section_index, 0, micro_count - 1)
        row_lengths = lax.dynamic_index_in_dim(lengths, slot_index, 0, keepdims=False)
        result, after_attn, attended, log_totals, whole_rows, middle_rows = layer_forward(
            entering.astype(jnp.float32), row_lengths, weights, slopes_here
        )
        outgoing = shifted(result.astype(jnp.bfloat16), "section", 1)
        stored = (entering, after_attn, attended, log_totals)
        return (outgoing, (result, stored))

    _, (results, kept_all) = lax.scan(
        forward_tick, jnp.zeros_like(local_ends[0]), (padded, tick_list)
    )
    sharded_zero = (
        jnp.zeros(w_qkv.shape[1:], jnp.float32),
        jnp.zeros(qv_bias.shape[1:], jnp.float32),
        jnp.zeros(w_out.shape[1:], jnp.float32),
        jnp.zeros(w_up.shape[1:], jnp.float32),
        jnp.zeros(up_bias.shape[1:], jnp.float32),
        jnp.zeros(w_down.shape[1:], jnp.float32),
    )
    shared_zero = (
        jnp.zeros(ln_gains.shape[1:], jnp.float32),
        jnp.zeros(ln_biases.shape[1:], jnp.float32),
        jnp.zeros(out_biases.shape[1:], jnp.float32),
    )

    def backward_tick(carry, item):
        received, sharded_total, shared_total = carry
        arriving, tick_index = item
        grad_result = jnp.where(section_index == 1, arriving, received).astype(jnp.float32)
        slot_index = tick_index - 1 + section_index
        is_valid = ((slot_index >= 0) & (slot_index < micro_count)).astype(jnp.float32)
        slot_index = jnp.clip(slot_index, 0, micro_count - 1)
        stored = tuple(
            (
                lax.dynamic_index_in_dim(kept, slot_index + section_index, 0, keepdims=False)
                for kept in kept_all
            )
        )
        row_lengths = lax.dynamic_index_in_dim(lengths, slot_index, 0, keepdims=False)
        grad_inputs, sharded, shared = layer_backward(
            grad_result, stored, row_lengths, weights, slopes_here
        )
        outgoing = shifted(grad_inputs.astype(jnp.bfloat16), "section", -1)
        sharded = tuple((value * is_valid for value in sharded))
        shared = tuple((value * is_valid for value in shared))
        sharded_total = tuple((left + right for left, right in zip(sharded_total, sharded)))
        shared_total = tuple((left + right for left, right in zip(shared_total, shared)))
        return ((outgoing, sharded_total, shared_total), grad_inputs)

    start_carry = (jnp.zeros_like(local_ends[0]), sharded_zero, shared_zero)
    (_, sharded_total, shared_total), grads_in = lax.scan(
        backward_tick, start_carry, (padded, tick_list)
    )
    sharded_total = (
        lax.psum(sharded_total[0].astype(jnp.bfloat16), "dp").astype(jnp.float32),
        lax.psum(sharded_total[1].astype(jnp.bfloat16), "dp").astype(jnp.float32),
        lax.psum(sharded_total[2].astype(jnp.bfloat16), "dp").astype(jnp.float32),
        lax.psum(sharded_total[3].astype(jnp.bfloat16), "dp").astype(jnp.float32),
        lax.psum(sharded_total[4].astype(jnp.bfloat16), "dp").astype(jnp.float32),
        lax.psum(sharded_total[5].astype(jnp.bfloat16), "dp").astype(jnp.float32),
    )
    shared_total = lax.psum((shared_total[0], shared_total[1], shared_total[2]), ("dp", "tensor"))
    ends_local = jnp.where(section_index == 0, grads_in[1:], results[1:])
    return (
        ends_local[None],
        shared_total[0][None],
        shared_total[1][None],
        sharded_total[0][None],
        sharded_total[1][None],
        sharded_total[2][None],
        sharded_total[3][None],
        sharded_total[4][None],
        sharded_total[5][None],
        shared_total[2][None],
    )


bf16, f32 = jnp.bfloat16, jnp.float32
HEAD = D // HEADS
LOG2E = 1.4426950408889634
GROUP = 4
ST = ("section", "tensor")
MIB = 2**20


def one_row_a_chip(mesh):
    return mesh.shape["section"] == 2 and mesh.shape["tensor"] == GROUP


def core_of(segment):
    return (segment & 1) ^ (segment >> 1)


def place(core, chip):
    return core * GROUP + chip


CHIPS = range(GROUP)
FIRST_HOP = [(place(0, t), place(0, t ^ 1)) for t in CHIPS] + [(place(1, t), place(1, t ^ 2)) for t in CHIPS]
SECOND_HOP = [(place(0, t), place(0, t ^ 2)) for t in CHIPS] + [(place(1, t), place(1, t ^ 1)) for t in CHIPS]


def hop(value, pairs):
    return lax.ppermute(value, ST, pairs)


def swap(value):
    return lax.ppermute(value, "section", [(0, 1), (1, 0)])


def half_of(value, axis, index):
    size = value.shape[axis] // 2
    return lax.dynamic_slice_in_dim(value, index * size, size, axis)


def dot_nn(left, right):
    return lax.dot_general(left, right, (((1,), (0,)), ((), ())), preferred_element_type=f32)


def dot_nt(left, right):
    return lax.dot_general(left, right, (((1,), (1,)), ((), ())), preferred_element_type=f32)


def dot_tn(left, right):
    return lax.dot_general(left, right, (((0,), (0,)), ((), ())), preferred_element_type=f32)


def three_parts(value):
    first = value.astype(bf16)
    rest = value - first.astype(f32)
    second = rest.astype(bf16)
    third = (rest - second.astype(f32)).astype(bf16)
    return first, second, third


def key_columns(positions, length):
    high = (positions // 8 * 8).astype(f32)
    low = (positions % 8).astype(f32)
    mask = jnp.where(positions < length, 0.0, -1e30).astype(f32)
    one = jnp.ones_like(high)
    columns = jnp.stack([high, high, high, low, low, low, mask, one, one, one], axis=1)
    half = jnp.pad(columns, ((0, 0), (0, HEAD - 10)))
    return jnp.concatenate([half, half], axis=1).astype(bf16)


def query_columns(slopes):
    first, second, third = three_parts(slopes * 8.0)
    one = jnp.ones_like(first)
    columns = jnp.stack([first, second, third, first, second, third, one], axis=1)
    half = jnp.pad(columns, ((0, 0), (0, HEAD - 7))).reshape(-1, 2, HEAD)
    row = jnp.concatenate([half[:, 1], half[:, 0]], axis=1).astype(f32)
    return jnp.broadcast_to(row[:, None, :], (row.shape[0], 8, 2 * HEAD))


def attend_kernel(seg, meta, q, kv, kvo, kcol, qcol, o, qx, qp, kp, vp, st_m, st_a):
    other = 1 - meta[0]
    lane = lax.broadcasted_iota(jnp.int32, (1, 128), 1)
    low = lane < 64
    base = qcol[0, 0:1, :].astype(bf16)
    scale = LOG2E / 8
    one = jnp.ones((1, 128), bf16)
    for h in range(2):
        mine = low if h == 0 else ~low
        qp[h] = jnp.where(mine, q[...], base)
        kp[h, 0 : 2 * seg] = jnp.where(mine, kv[0], kcol[0 : 2 * seg])
        kp[h, 2 * seg :] = jnp.where(mine, kvo[0], kcol[2 * seg :])
        vp[h, 0 : 2 * seg] = jnp.where(mine, kv[1], one)
        vp[h, 2 * seg :] = jnp.where(mine, kvo[1], one)

    def scores_of(h, start, keys, masked):
        queries = qp[h, pl.ds(start, seg)]
        scores = []
        for n, (key_start, key_count) in enumerate(keys):
            part = dot_nt(queries, kp[h, pl.ds(key_start, key_count)])
            if masked and n == len(keys) - 1:
                row = lax.broadcasted_iota(jnp.int32, (seg, key_count), 0)
                column = lax.broadcasted_iota(jnp.int32, (seg, key_count), 1)
                part = jnp.where(column <= row, part, -1e30)
            scores.append(part)
        top = scores[0].max(axis=1, keepdims=True)
        for part in scores[1:]:
            top = jnp.maximum(top, part.max(axis=1, keepdims=True))
        return scores, top

    def weigh(h, scores, top, keys):
        total = None
        for part, (key_start, key_count) in zip(scores, keys):
            powers = jnp.exp2((part - top) * scale).astype(bf16)
            term = dot_nn(powers, vp[h, pl.ds(key_start, key_count)])
            total = term if total is None else total + term
        return total

    for h in range(2):
        start = pl.multiple_of(other * seg, seg)
        keys = [(pl.multiple_of(2 * seg + other * seg, seg), seg)]
        scores, top = scores_of(h, start, keys, False)
        st_a[h] = weigh(h, scores, top, keys)
        st_m[h] = jnp.broadcast_to(top, (seg, 128))
    for segment in range(2):
        use = other == segment
        rows = slice(segment * seg, (segment + 1) * seg)
        totals, tops = [], []
        for h in range(2):
            keys = [(segment * seg, seg)]
            if segment == 1:
                keys = [(0, seg), (2 * seg, seg)] + keys
            scores, top = scores_of(h, segment * seg, keys, True)
            fifth = jnp.where(use, st_m[h][:, 0:1], -1e30)
            top = jnp.maximum(top, fifth)
            weight = jnp.where(use, jnp.exp2((fifth - top) * scale), 0.0)
            totals.append(weigh(h, scores, top, keys) + weight * st_a[h])
            tops.append(top)
        number = jnp.where(low, totals[0], totals[1])
        sums = jnp.where(low, totals[1], totals[0])
        o[rows] = (number / pltpu.roll(sums, 64, 1)).astype(bf16)
        logs = jnp.where(low, tops[1], tops[0]) + jnp.log(sums) * 8.0
        first, second, third = three_parts(logs)
        at = lane & 63
        qx[rows] = jnp.where(at == 7, -first, jnp.where(at == 8, -second, jnp.where(at == 9, -third, base)))


def attend(meta, q, kv, kvo, kcol, qcol):
    rows, width = q.shape
    seg = rows // 2
    pairs = width // 128
    block = pl.BlockSpec((rows, 128), lambda i, m: (0, i))
    return pl.pallas_call(
        partial(attend_kernel, seg),
        grid_spec=pltpu.PrefetchScalarGridSpec(
            num_scalar_prefetch=1,
            grid=(pairs,),
            in_specs=[
                block,
                pl.BlockSpec((2, rows, 128), lambda i, m: (0, 0, i)),
                pl.BlockSpec((2, rows, 128), lambda i, m: (0, 0, m[1 + i])),
                pl.BlockSpec((2 * rows, 128), lambda i, m: (0, 0)),
                pl.BlockSpec((1, 8, 128), lambda i, m: (i, 0, 0)),
            ],
            out_specs=[block, block],
            scratch_shapes=[
                pltpu.VMEM((2, rows, 128), bf16),
                pltpu.VMEM((2, 2 * rows, 128), bf16),
                pltpu.VMEM((2, 2 * rows, 128), bf16),
                pltpu.VMEM((2, seg, 128), f32),
                pltpu.VMEM((2, seg, 128), f32),
            ],
        ),
        out_shape=[jax.ShapeDtypeStruct((rows, width), bf16)] * 2,
        compiler_params=pltpu.CompilerParams(vmem_limit_bytes=40 * MIB),
        cost_estimate=pl.CostEstimate(
            flops=40 * 256 * seg * seg * pairs, bytes_accessed=rows * width * 14, transcendentals=10 * seg * seg * pairs
        ),
        name="attend",
    )(meta, q, kv, kvo, kcol, qcol)


def attend_back_kernel(
    seg, meta, q, kv, kvo, kcol, qx, do, o, dq, dkv, dkvo, qp, kp, vp, dp, kt, qm, dm, aq, ak, av
):
    other = 1 - meta[0]
    lane = lax.broadcasted_iota(jnp.int32, (1, 128), 1)
    low = lane < 64
    at = lane & 63
    scale = LOG2E / 8
    zero = jnp.zeros((1, 128), bf16)
    product = do[...].astype(f32) * o[...].astype(f32)
    for h in range(2):
        mine = low if h == 0 else ~low
        qp[h] = jnp.where(mine, q[...], qx[...])
        kp[h, 0 : 2 * seg] = jnp.where(mine, kv[0], kcol[0 : 2 * seg])
        kp[h, 2 * seg :] = jnp.where(mine, kvo[0], kcol[2 * seg :])
        vp[h, 0 : 2 * seg] = jnp.where(mine, kv[1], kcol[0 : 2 * seg])
        vp[h, 2 * seg :] = jnp.where(mine, kvo[1], kcol[2 * seg :])
        first, second, third = three_parts(jnp.sum(jnp.where(mine, product, 0.0), axis=1, keepdims=True))
        extra = jnp.where(at == 7, -first, jnp.where(at == 8, -second, jnp.where(at == 9, -third, zero)))
        dp[h] = jnp.where(mine, do[...], extra)
        qm[h] = jnp.where(mine, q[...], zero)
        dm[h] = jnp.where(mine, do[...], zero)
    kt[:, 0 : 2 * seg] = kv[0].T
    kt[:, 2 * seg :] = kvo[0].T
    aq[...] = jnp.zeros_like(aq)
    ak[...] = jnp.zeros_like(ak)
    av[...] = jnp.zeros_like(av)

    def block(query_start, query_count, key_start, key_count, masked):
        queries, keys = pl.ds(query_start, query_count), pl.ds(key_start, key_count)
        for h in range(2):
            probs = jnp.exp2(dot_nt(kp[h, keys], qp[h, queries]) * scale)
            if masked:
                row = lax.broadcasted_iota(jnp.int32, (key_count, query_count), 0)
                column = lax.broadcasted_iota(jnp.int32, (key_count, query_count), 1)
                probs = jnp.where(row <= column, probs, 0.0)
            grads = (probs * dot_nt(vp[h, keys], dp[h, queries])).astype(bf16)
            av[keys] += dot_nn(probs.astype(bf16), dm[h, queries])
            ak[keys] += dot_nn(grads, qm[h, queries])
            aq[h * 64 : (h + 1) * 64, queries] += dot_nn(kt[h * 64 : (h + 1) * 64, keys], grads)

    half = seg // 2
    for segment in range(2):
        start = segment * seg
        block(start, half, start, half, True)
        block(start + half, half, start, half, False)
        block(start + half, half, start + half, half, True)
    block(seg, seg, 0, seg, False)
    block(seg, seg, 2 * seg, seg, False)
    block(pl.multiple_of(other * seg, seg), seg, pl.multiple_of(2 * seg + other * seg, seg), seg, False)
    dq[...] = (aq[...] * 0.125).T.astype(bf16)
    dkv[0] = (ak[0 : 2 * seg] * 0.125).astype(bf16)
    dkvo[0] = (ak[2 * seg :] * 0.125).astype(bf16)
    dkv[1] = av[0 : 2 * seg].astype(bf16)
    dkvo[1] = av[2 * seg :].astype(bf16)


def attend_back(meta, q, kv, kvo, kcol, qx, do, o):
    rows, width = q.shape
    seg = rows // 2
    pairs = width // 128
    block = pl.BlockSpec((rows, 128), lambda i, m: (0, i))
    mine = pl.BlockSpec((2, rows, 128), lambda i, m: (0, 0, i))
    theirs = pl.BlockSpec((2, rows, 128), lambda i, m: (0, 0, m[1 + i]))
    return pl.pallas_call(
        partial(attend_back_kernel, seg),
        grid_spec=pltpu.PrefetchScalarGridSpec(
            num_scalar_prefetch=1,
            grid=(pairs,),
            in_specs=[block, mine, theirs, pl.BlockSpec((2 * rows, 128), lambda i, m: (0, 0))] + [block] * 3,
            out_specs=[block, mine, theirs],
            scratch_shapes=[
                pltpu.VMEM((2, rows, 128), bf16),
                pltpu.VMEM((2, 2 * rows, 128), bf16),
                pltpu.VMEM((2, 2 * rows, 128), bf16),
                pltpu.VMEM((2, rows, 128), bf16),
                pltpu.VMEM((128, 2 * rows), bf16),
                pltpu.VMEM((2, rows, 128), bf16),
                pltpu.VMEM((2, rows, 128), bf16),
                pltpu.VMEM((128, rows), f32),
                pltpu.VMEM((2 * rows, 128), f32),
                pltpu.VMEM((2 * rows, 128), f32),
            ],
        ),
        out_shape=[
            jax.ShapeDtypeStruct((rows, width), bf16),
            jax.ShapeDtypeStruct((2, rows, width), bf16),
            jax.ShapeDtypeStruct((2, rows, width), bf16),
        ],
        compiler_params=pltpu.CompilerParams(vmem_limit_bytes=48 * MIB),
        cost_estimate=pl.CostEstimate(
            flops=100 * 256 * seg * seg * pairs, bytes_accessed=rows * width * 26, transcendentals=10 * seg * seg * pairs
        ),
        name="attend_back",
    )(meta, q, kv, kvo, kcol, qx, do, o)


def fixed(shape):
    return pl.BlockSpec(shape, lambda *_: (0,) * len(shape), pipeline_mode=pl.Buffered(1))


def joined(refs, *index):
    return jnp.concatenate([ref[index] if index else ref[...] for ref in refs], axis=0) if len(refs) > 1 else refs[0][index] if index else refs[0][...]


def project_kernel(count, a, *refs):
    pieces, bias, q, kv = refs[:count], refs[count], refs[count + 1], refs[count + 2]
    step = pl.program_id(0)
    result = (dot_nt(a[...], joined(pieces, 0)) + bias[0]).astype(bf16)

    @pl.when(step == 0)
    def _():
        q[...] = result

    @pl.when(step > 0)
    def _():
        kv[0] = result


def project_heads(a, pieces, bias):
    rows, width = a.shape
    columns = sum(piece.shape[1] for piece in pieces)
    return pl.pallas_call(
        partial(project_kernel, len(pieces)),
        grid=(3,),
        in_specs=[fixed(a.shape)]
        + [pl.BlockSpec((1,) + piece.shape[1:], lambda i: (i, 0, 0)) for piece in pieces]
        + [pl.BlockSpec((1, 1, columns), lambda i: (i, 0, 0))],
        out_specs=[
            pl.BlockSpec((rows, columns), lambda i: (0, 0)),
            pl.BlockSpec((1, rows, columns), lambda i: (jnp.maximum(i - 1, 0), 0, 0)),
        ],
        out_shape=[jax.ShapeDtypeStruct((rows, columns), bf16), jax.ShapeDtypeStruct((2, rows, columns), bf16)],
        cost_estimate=pl.CostEstimate(
            flops=6 * rows * width * columns, bytes_accessed=2 * rows * width + 6 * width * columns + 6 * rows * columns, transcendentals=0
        ),
        compiler_params=pltpu.CompilerParams(vmem_limit_bytes=40 * MIB),
        name="project",
    )(a, *pieces, bias)


def normalize(value):
    center = jnp.mean(value, axis=-1, keepdims=True)
    centred = value - center
    spread = jnp.mean(centred * centred, axis=-1, keepdims=True)
    factor = lax.rsqrt(spread + eps)
    return centred * factor, factor


def normed_rows(value, vectors):
    normal, _ = normalize(value)
    return (normal * vectors[1:2] + vectors[2:3]).astype(bf16)


def first_norm_kernel(x, vectors, out):
    out[...] = normed_rows(x[...].astype(f32), vectors)


def first_norm(x, vectors):
    rows, width = x.shape
    tile = rows // 4
    return pl.pallas_call(
        first_norm_kernel,
        grid=(rows // tile,),
        in_specs=[pl.BlockSpec((tile, width), lambda i: (i, 0)), fixed(vectors.shape)],
        out_specs=pl.BlockSpec((tile, width), lambda i: (i, 0)),
        out_shape=jax.ShapeDtypeStruct((rows, width), bf16),
        name="first_norm",
    )(x, vectors)


def eight_rows(*rows):
    return jnp.concatenate([jnp.stack(rows), jnp.zeros((8 - len(rows), rows[0].shape[-1]), f32)])


def mix_kernel(counts, *refs):
    heads, weights = refs[: counts[0]], refs[counts[0] : sum(counts)]
    x, vectors, out, normed = refs[sum(counts) :]
    left = jnp.concatenate([ref[...] for ref in heads], axis=1) if len(heads) > 1 else heads[0][...]
    total = x[...].astype(f32) + vectors[0:1] + dot_nn(left, joined(weights, 0))
    out[...] = total
    normed[...] = normed_rows(total, vectors)


def mix(x, heads, pieces, vectors):
    rows, width = x.shape
    tile = rows // 2
    return pl.pallas_call(
        partial(mix_kernel, (len(heads), len(pieces))),
        grid=(rows // tile,),
        in_specs=[pl.BlockSpec((tile, h.shape[1]), lambda i: (i, 0)) for h in heads]
        + [pl.BlockSpec((1,) + p.shape[1:], lambda i: (3, 0, 0), pipeline_mode=pl.Buffered(1)) for p in pieces]
        + [pl.BlockSpec((tile, width), lambda i: (i, 0)), fixed(vectors.shape)],
        out_specs=[pl.BlockSpec((tile, width), lambda i: (i, 0))] * 2,
        out_shape=[jax.ShapeDtypeStruct((rows, width), f32), jax.ShapeDtypeStruct((rows, width), bf16)],
        cost_estimate=pl.CostEstimate(flops=2 * rows * width * width, bytes_accessed=14 * rows * width, transcendentals=0),
        compiler_params=pltpu.CompilerParams(vmem_limit_bytes=40 * MIB),
        name="mix",
    )(*heads, *pieces, x, vectors)


STEPS = 8
GELU_A = 0.7978845608028654
GELU_B = 0.044715


def share_specs(pieces, steps):
    specs = [pl.BlockSpec((2, 2, pieces[0].shape[2] // steps, pieces[0].shape[3]), lambda i, m: (0, 0, i, 0))]
    for piece in pieces[1:]:
        specs.append(pl.BlockSpec((2, piece.shape[1] // steps, piece.shape[2]), lambda i, m: (0, i, 0)))
    return specs


def share(refs, matrix, core):
    own = refs[0]
    return jnp.concatenate([own[matrix, core], own[matrix, 1 - core]] + [ref[matrix] for ref in refs[1:]], axis=0)


def feed_kernel(meta, middle, after, vectors, bias, own, near, near_too, far, far_too, pre, hidden, out, normed, total):
    core = meta[0]
    step = pl.program_id(0)
    refs = (own, near, near_too, far, far_too)
    up, down = share(refs, 0, core), share(refs, 1, core)
    units = up.shape[0]
    parts = []
    count = max(units // 256, 1)
    size = units // count
    for n in range(count):
        at = slice(n * size, (n + 1) * size)
        u = dot_nt(middle[...], up[at]) + bias[0, 0:1, at]
        pre[0, :, at] = u.astype(bf16)
        h = (0.5 * u * (1.0 + jnp.tanh(GELU_A * (u + GELU_B * u * u * u)))).astype(bf16)
        hidden[0, :, at] = h
        parts.append(dot_nn(h, down[at]))
    term = parts[0]
    for part in parts[1:]:
        term = term + part

    @pl.when(step == 0)
    def _():
        total[...] = term

    @pl.when(step > 0)
    def _():
        total[...] += term

    @pl.when(step == pl.num_programs(0) - 1)
    def _():
        tile = total.shape[0] // 4
        for n in range(4):
            at = slice(n * tile, (n + 1) * tile)
            value = (total[at] + after[at] + vectors[0:1]).astype(bf16)
            out[at] = value
            normed[at] = normed_rows(value.astype(f32), vectors)


def feed(meta, middle, after, vectors, bias, pieces):
    rows, width = middle.shape
    units = 4 * pieces[1].shape[1]
    steps = STEPS
    wide = units // steps
    return pl.pallas_call(
        feed_kernel,
        grid_spec=pltpu.PrefetchScalarGridSpec(
            num_scalar_prefetch=1,
            grid=(steps,),
            in_specs=[fixed(middle.shape), fixed(after.shape), fixed(vectors.shape), pl.BlockSpec((1, 1, wide), lambda i, m: (i, 0, 0))]
            + share_specs(pieces, steps),
            out_specs=[pl.BlockSpec((1, rows, wide), lambda i, m: (i, 0, 0))] * 2 + [pl.BlockSpec((rows, width), lambda i, m: (0, 0))] * 2,
            scratch_shapes=[pltpu.VMEM((rows, width), f32)],
        ),
        out_shape=[jax.ShapeDtypeStruct((steps, rows, wide), bf16)] * 2 + [jax.ShapeDtypeStruct((rows, width), bf16)] * 2,
        cost_estimate=pl.CostEstimate(
            flops=4 * rows * width * units, bytes_accessed=4 * units * (rows + width) + 10 * rows * width, transcendentals=rows * units
        ),
        compiler_params=pltpu.CompilerParams(vmem_limit_bytes=52 * MIB),
        name="feed",
    )(meta, middle, after, vectors, bias, *pieces)


def norm_back_rows(total, value, above, gain):
    normal, factor = normalize(value)
    scaled = total * gain
    first = jnp.mean(scaled, axis=-1, keepdims=True)
    second = jnp.mean(scaled * normal, axis=-1, keepdims=True)
    return above + factor * (scaled - first - normal * second), normal


def norm_back_all(total, value, above, gain, out, low, sums):
    tile = total.shape[0] // 4
    rows = []
    for n in range(4):
        at = slice(n * tile, (n + 1) * tile)
        part = total[at]
        top = above[at].astype(f32)
        grad, normal = norm_back_rows(part, value[at].astype(f32), top, gain)
        if out is not None:
            out[at] = grad
        low[at] = grad.astype(bf16)
        rows.append([jnp.sum(v, axis=0, keepdims=True) for v in (part * normal, part, grad, top)])
    for n in range(4):
        sums[n : n + 1] = rows[0][n] + rows[1][n] + rows[2][n] + rows[3][n]


def feed_back_kernel(
    meta, above, middle, after, vectors, pre, hidden, own, near, near_too, far, far_too, keep, send, bias_sums, out, low, sums, total
):
    core = meta[0]
    step = pl.program_id(0)
    refs = (own, near, near_too, far, far_too)
    up, down = share(refs, 0, core), share(refs, 1, core)
    u = pre[0].astype(f32)
    inner = GELU_A * (u + GELU_B * u * u * u)
    t = jnp.tanh(inner)
    slope = 0.5 * (1.0 + t) + 0.5 * u * (1.0 - t * t) * (GELU_A * (1.0 + 3.0 * GELU_B * u * u))
    grad = dot_nt(above[...], down) * slope
    low_grad = grad.astype(bf16)
    bias_sums[0] = jnp.broadcast_to(jnp.sum(low_grad.astype(f32), axis=0, keepdims=True), bias_sums.shape[1:])
    term = dot_nn(low_grad, up)

    @pl.when(step == 0)
    def _():
        total[...] = term

    @pl.when(step > 0)
    def _():
        total[...] += term

    grads = (dot_tn(low_grad, middle[...]).astype(bf16), dot_tn(hidden[0], above[...]).astype(bf16))
    part = up.shape[0] // 8
    for n, value in enumerate(grads):
        keep[n, 0, 0 : 2 * part] = value[2 * part : 4 * part]
        keep[n, 0, 2 * part : 3 * part] = value[6 * part : 7 * part]
        keep[n, 0, 3 * part :] = value[0:part]
        send[n, 0, 0 : 2 * part] = value[4 * part : 6 * part]
        send[n, 0, 2 * part : 3 * part] = value[7 * part :]
        send[n, 0, 3 * part :] = value[part : 2 * part]

    @pl.when(step == pl.num_programs(0) - 1)
    def _():
        norm_back_all(total, after, above, vectors[0:1], out, low, sums)


def feed_back(meta, above, middle, after, gain, pre, hidden, pieces):
    rows, width = middle.shape
    units = 4 * pieces[1].shape[1]
    steps = STEPS
    wide = units // steps
    vectors = jnp.broadcast_to(gain[None], (8, width))
    per_step = pl.BlockSpec((1, rows, wide), lambda i, m: (i, 0, 0))
    grads = pl.BlockSpec((2, 1, wide // 2, width), lambda i, m: (0, i, 0, 0))
    whole = pl.BlockSpec((rows, width), lambda i, m: (0, 0))
    return pl.pallas_call(
        feed_back_kernel,
        grid_spec=pltpu.PrefetchScalarGridSpec(
            num_scalar_prefetch=1,
            grid=(steps,),
            in_specs=[fixed(above.shape), fixed(middle.shape), fixed(after.shape), fixed(vectors.shape), per_step, per_step]
            + share_specs(pieces, steps),
            out_specs=[grads, grads, pl.BlockSpec((1, 8, wide), lambda i, m: (i, 0, 0)), whole, whole, pl.BlockSpec((8, width), lambda i, m: (0, 0))],
            scratch_shapes=[pltpu.VMEM((rows, width), f32)],
        ),
        out_shape=[jax.ShapeDtypeStruct((2, steps, wide // 2, width), bf16)] * 2
        + [
            jax.ShapeDtypeStruct((steps, 8, wide), f32),
            jax.ShapeDtypeStruct((rows, width), f32),
            jax.ShapeDtypeStruct((rows, width), bf16),
            jax.ShapeDtypeStruct((8, width), f32),
        ],
        cost_estimate=pl.CostEstimate(
            flops=8 * rows * width * units, bytes_accessed=12 * units * (rows + width) + 14 * rows * width, transcendentals=rows * units
        ),
        compiler_params=pltpu.CompilerParams(vmem_limit_bytes=58 * MIB),
        name="feed_back",
    )(meta, above, middle, after, vectors, pre, hidden, *pieces)


def heads_back_kernel(count, low, *refs):
    pieces, out = refs[:count], refs[count]
    out[...] = dot_nt(low[...], joined(pieces, 0)).astype(bf16)


def heads_back(low, pieces):
    rows, width = low.shape
    columns = sum(piece.shape[1] for piece in pieces)
    tile = rows // 2
    return pl.pallas_call(
        partial(heads_back_kernel, len(pieces)),
        grid=(rows // tile,),
        in_specs=[pl.BlockSpec((tile, width), lambda i: (i, 0))]
        + [pl.BlockSpec((1,) + p.shape[1:], lambda i: (3, 0, 0), pipeline_mode=pl.Buffered(1)) for p in pieces],
        out_specs=pl.BlockSpec((tile, columns), lambda i: (i, 0)),
        out_shape=jax.ShapeDtypeStruct((rows, columns), bf16),
        cost_estimate=pl.CostEstimate(
            flops=2 * rows * width * columns, bytes_accessed=2 * (rows * width + width * columns + rows * columns), transcendentals=0
        ),
        compiler_params=pltpu.CompilerParams(vmem_limit_bytes=40 * MIB),
        name="heads_back",
    )(low, *pieces)


def project_back_kernel(groups, first, last, meta, *refs):
    refs = list(refs)
    take = lambda n: [refs.pop(0) for _ in range(n)]
    dq, dkv, dkv_got, o, a, low = take(6)
    pieces = take(len(groups))
    so_far = None if first else refs.pop(0)
    if last:
        value, above, vectors = take(3)
    keep, send, bias_sums = take(3)
    outs = take(2) if last else take(1)
    lefts, flipped = take(2)
    total = refs.pop(0) if last else None
    step = pl.program_id(0)
    core = meta[0]

    @pl.when(step == 0)
    def _():
        lefts[0] = dq[...]
        for n in range(2):
            lefts[1 + n] = (dkv[n].astype(f32) + dkv_got[n].astype(f32)).astype(bf16)
        for n in range(3):
            flipped[n] = lefts[n].T
        flipped[3] = o[...].T
        for n, c in enumerate((0, 2)):
            bias_sums[n : n + 1] = jnp.sum(lefts[c].astype(f32), axis=0, keepdims=True)

    for c in range(4):
        value_c = dot_nn(flipped[c], (low if c == 3 else a)[...]).astype(bf16)
        keep_at = send_at = at = 0
        for name, size in groups:
            if name == "own":
                half = size // 2
                keep[c, keep_at : keep_at + half] = jnp.where(core == 0, value_c[at : at + half], value_c[at + half : at + size])
                send[c, send_at : send_at + half] = jnp.where(core == 0, value_c[at + half : at + size], value_c[at : at + half])
                keep_at, send_at = keep_at + half, send_at + half
            elif name in ("near", "far"):
                keep[c, keep_at : keep_at + size] = value_c[at : at + size]
                keep_at += size
            else:
                send[c, send_at : send_at + size] = value_c[at : at + size]
                send_at += size
            at += size
    term = None
    for c in range(3):
        part = dot_nn(lefts[c], joined(pieces, c))
        term = part if term is None else term + part
    if not first:
        term = term + so_far[...]
    if not last:
        outs[0][...] = term
        return
    tile = total.shape[1] // pl.num_programs(0) if isinstance(pl.num_programs(0), int) else term.shape[1]
    total[:, pl.ds(pl.multiple_of(step * tile, tile), tile)] = term

    @pl.when(step == pl.num_programs(0) - 1)
    def _():
        norm_back_all(total, value, above, vectors[0:1], None, outs[0], outs[1])


def project_back(meta, names, dq, dkv, dkv_got, o, a, low, pieces, so_far, norm):
    rows, width = a.shape
    columns = dq.shape[1]
    groups = [(name, piece.shape[1]) for name, piece in zip(names, pieces)]
    tiles = 4
    tile = width // tiles
    slim = pl.BlockSpec((rows, tile), lambda i, m: (0, i))
    grads = pl.BlockSpec((4, columns // 2, tile), lambda i, m: (0, 0, i))
    args = [dq, dkv, dkv_got, o, a, low, *pieces]
    specs = [fixed(dq.shape), fixed(dkv.shape), fixed(dkv.shape), fixed(o.shape), slim, slim]
    specs += [pl.BlockSpec((3, p.shape[1], tile), lambda i, m: (0, 0, i)) for p in pieces]
    if so_far is not None:
        args.append(so_far)
        specs.append(slim)
    out_specs = [grads, grads, pl.BlockSpec((8, columns), lambda i, m: (0, 0))]
    out_shape = [jax.ShapeDtypeStruct((4, columns // 2, width), bf16)] * 2 + [jax.ShapeDtypeStruct((8, columns), f32)]
    scratch = [pltpu.VMEM((3, rows, columns), bf16), pltpu.VMEM((4, columns, rows), bf16)]
    if norm is None:
        out_specs.append(slim)
        out_shape.append(jax.ShapeDtypeStruct((rows, width), f32))
    else:
        value, above, gain = norm
        args += [value, above, jnp.broadcast_to(gain[None], (8, width))]
        specs += [fixed(value.shape), fixed(above.shape), fixed((8, width))]
        out_specs += [pl.BlockSpec((rows, width), lambda i, m: (0, 0)), pl.BlockSpec((8, width), lambda i, m: (0, 0))]
        out_shape += [jax.ShapeDtypeStruct((rows, width), bf16), jax.ShapeDtypeStruct((8, width), f32)]
        scratch.append(pltpu.VMEM((rows, width), f32))
    return pl.pallas_call(
        partial(project_back_kernel, groups, so_far is None, norm is not None),
        grid_spec=pltpu.PrefetchScalarGridSpec(
            num_scalar_prefetch=1, grid=(tiles,), in_specs=specs, out_specs=out_specs, scratch_shapes=scratch
        ),
        out_shape=out_shape,
        cost_estimate=pl.CostEstimate(
            flops=14 * rows * width * columns, bytes_accessed=2 * (6 * rows * columns + 7 * width * columns + 6 * rows * width), transcendentals=0
        ),
        compiler_params=pltpu.CompilerParams(vmem_limit_bytes=58 * MIB),
        name="project_back",
    )(meta, *args)


def gathered(own, core):
    near = hop(own, FIRST_HOP)
    near_too = swap(near)
    far = hop(half_of(near, 1, core), SECOND_HOP)
    far_too = swap(far)
    return {"own": own, "near": near, "near_too": near_too, "far": far, "far_too": far_too}


def plus(*values):
    total = values[0].astype(f32)
    for value in values[1:]:
        total = total + value.astype(f32)
    return total.astype(bf16)


def summed(near, far, own, core):
    relayed = hop(far, SECOND_HOP)
    matrices, units, width = near.shape
    place_of_half = jnp.arange(2)[None, :, None, None] == core
    near = near.reshape(matrices, 2, units // 2, width)
    near = plus(near, jnp.where(place_of_half, relayed[:, None], jnp.zeros((), bf16)))
    got = hop(near.reshape(matrices, units, width), FIRST_HOP)
    total = plus(own, half_of(got, 1, core), swap(half_of(got, 1, 1 - core)))
    return lax.psum(total, "dp")


def in_order(own, near, near_too, far, far_too, core, chip):
    first = core == 0
    last = jnp.concatenate([jnp.where(first, far, far_too), jnp.where(first, far_too, far)], axis=-1)
    by_distance = jnp.stack([own, jnp.where(first, near, near_too), jnp.where(first, near_too, near), last])
    rows = [lax.dynamic_index_in_dim(by_distance, quarter ^ chip, 0, keepdims=False) for quarter in CHIPS]
    return jnp.concatenate(rows, axis=-1)


PIECES = ("own", "near", "near_too", "far", "far_too")
GROUPS = ((("own",), ("near", "near_too"), ("far", "far_too")), (PIECES,))


def on_row(
    ends_in, lengths, ln_gains, ln_biases, w_qkv, qv_bias, w_out, w_up, up_bias, w_down, out_biases
):
    core = lax.axis_index("section")
    chip = lax.axis_index("tensor")
    first_core = core == 0
    micro, rows_here, seg = ends_in.shape[1:4]
    ends = ends_in.reshape(micro * rows_here, seg, D)
    lo_segment, hi_segment = core, 3 - core
    n_qv = qv_bias.shape[-1]
    n_up = up_bias.shape[-1]

    def row_from(section):
        got = [
            hop(
                lax.dynamic_index_in_dim(ends, chip ^ k, 0, keepdims=False),
                [(place(section, t), place(core_of(t), t ^ k)) for t in CHIPS],
            )
            for k in CHIPS
        ]

        def pick(k):
            return jnp.where(k == 0, got[0], jnp.where(k == 1, got[1], jnp.where(k == 2, got[2], got[3])))

        return jnp.concatenate([pick(chip ^ lo_segment), pick(chip ^ hi_segment)])

    def row_to(section, row):
        got = []
        for k in CHIPS:
            segment = chip ^ k
            sent = jnp.where(segment == lo_segment, row[:seg], row[seg:])
            got.append(hop(sent, [(place(core_of(t), t ^ k), place(section, t)) for t in CHIPS]))
        return got

    def both(mine):
        theirs = swap(mine)
        return (jnp.where(first_core, mine, theirs), jnp.where(first_core, theirs, mine))

    vectors = jnp.concatenate(
        [ln_gains[0].reshape(-1), ln_biases[0].reshape(-1), out_biases[0].reshape(-1), qv_bias[0].reshape(-1), up_bias[0]]
    )
    vectors = both(vectors[None])
    x = row_from(0)
    attention_own = both(jnp.concatenate([jnp.swapaxes(w_qkv[0], 1, 2), w_out]))
    feed_own = both(jnp.concatenate([w_up[0].T[None], w_down]))
    biases = jnp.concatenate([v[:, 6 * D :] for v in vectors])
    near = hop(biases, FIRST_HOP)
    far = hop(near, SECOND_HOP)
    bias_quarters = {"own": biases, "near": near, "near_too": swap(near), "far": far, "far_too": far}

    def bias_of(name, layer, start, size):
        part = bias_quarters[name][layer, start : start + size]
        if name == "far":
            part = half_of(part, 0, core)
        if name == "far_too":
            part = half_of(part, 0, 1 - core)
        return part

    weights = []
    for layer in range(2):
        own_bias = bias_quarters["own"][layer, 2 * n_qv :]
        shares = [half_of(own_bias, 0, core), half_of(own_bias, 0, 1 - core)]
        shares += [bias_of(name, layer, 2 * n_qv, n_up) for name in PIECES[1:]]
        six = vectors[layer][0, : 6 * D].reshape(6, D)
        attention, feeding = gathered(attention_own[layer], core), gathered(feed_own[layer], core)
        feeding["own"] = feeding["own"].reshape(2, 2, -1, D)
        weights.append(
            dict(
                gains=six[0:2],
                shifts=six[2:4],
                ends=six[4:6],
                attention=attention,
                feed=[feeding[name] for name in PIECES],
                feed_bias=jnp.concatenate([part.reshape(STEPS, -1) for part in shares], axis=1)[:, None],
            )
        )

    length = lax.dynamic_index_in_dim(lengths.reshape(-1), chip, 0, keepdims=False)
    segments = jnp.stack([lo_segment, hi_segment, 1 - core, 2 + core])
    positions = (segments[:, None] * seg + jnp.arange(seg)[None]).reshape(-1)
    kcol = key_columns(positions, length)
    heads_here = n_qv // HEAD
    quarters = {"own": chip, "near": chip ^ (1 + core), "near_too": chip ^ (2 - core), "far": chip ^ 3, "far_too": chip ^ 3}
    pairs_of = {name: n_qv // 128 // (2 if name.startswith("far") else 1) for name in PIECES}
    across = {"own": "own", "near": "near_too", "near_too": "near", "far": "far_too", "far_too": "far"}

    def head_slopes(name):
        head = quarters[name] * heads_here + jnp.arange(heads_here)
        if name == "far":
            head = half_of(head, 0, core)
        if name == "far_too":
            head = half_of(head, 0, 1 - core)
        return jnp.exp2(-8.0 * (head + 1).astype(f32) / HEADS)

    slopes = {name: head_slopes(name) for name in PIECES}

    def group_meta(names):
        starts, at = {}, 0
        for name in names:
            starts[name] = at
            at += pairs_of[name]
        table = [starts[across[name]] + n for name in names for n in range(pairs_of[name])]
        return jnp.concatenate([core[None].astype(jnp.int32), jnp.array(table, jnp.int32)])

    groups = [
        [
            dict(
                names=names,
                meta=group_meta(names),
                qcol=query_columns(jnp.concatenate([slopes[name] for name in names])),
                pieces=[weights[layer]["attention"][name] for name in names],
                bias=jnp.stack(
                    [
                        jnp.concatenate([bias_of(name, layer, 0, n_qv) for name in names]),
                        jnp.zeros((sum(pairs_of[name] for name in names) * 128,), f32),
                        jnp.concatenate([bias_of(name, layer, n_qv, n_qv) for name in names]),
                    ]
                )[:, None],
            )
            for names in GROUPS[layer]
        ]
        for layer in range(2)
    ]
    meta = core[None].astype(jnp.int32)

    kept = []
    normed = first_norm(x, eight_rows(jnp.zeros((D,), f32), weights[0]["gains"][0], weights[0]["shifts"][0]))
    for layer in range(2):
        w = weights[layer]
        saved = []
        for group in groups[layer]:
            q, kv = project_heads(normed, group["pieces"], group["bias"])
            kvo = swap(kv)
            o, qx = attend(group["meta"], q, kv, kvo, kcol, group["qcol"])
            saved.append((q, kv, kvo, o, qx))
        after, middle = mix(
            x,
            [s[3] for s in saved],
            [p for group in groups[layer] for p in group["pieces"]],
            eight_rows(w["ends"][0], w["gains"][1], w["shifts"][1]),
        )
        following = weights[min(layer + 1, 1)]
        pre, hidden, result, normed_next = feed(
            meta, middle, after, eight_rows(w["ends"][1], following["gains"][0], following["shifts"][0]), w["feed_bias"], w["feed"]
        )
        kept.append((x, normed, saved, after, middle, pre, hidden))
        x, normed = result, normed_next

    sent_back = row_to(1, x)
    grad = row_from(1)

    matrices, vector_sums = [None, None], [None, None]
    for layer in (1, 0):
        w = weights[layer]
        x_in, normed, saved, after, middle, pre, hidden = kept[layer]
        keep, send, unit_sums, grad_after, low, sums_two = feed_back(
            meta, grad, middle, after, w["gains"][1], pre, hidden, w["feed"]
        )
        total = plus(keep, swap(send))
        part = total.shape[2] // 4
        feed_grads = summed(
            total[:, :, : 2 * part].reshape(2, -1, D), total[:, :, 2 * part : 3 * part].reshape(2, -1, D), total[:, :, 3 * part :].reshape(2, -1, D), core
        )
        so_far = None
        sums_of, kept_rows = {}, {}
        order = list(reversed(range(len(groups[layer]))))
        for index in order:
            group = groups[layer][index]
            q, kv, kvo, o, qx = saved[index]
            grad_heads = heads_back(low, group["pieces"])
            dq, dkv, dkvo = attend_back(group["meta"], q, kv, kvo, kcol, qx, grad_heads, o)
            got = swap(dkvo)
            last = index == order[-1]
            norm = (x_in, grad_after, w["gains"][0]) if last else None
            results = project_back(meta, group["names"], dq, dkv, got, o, normed, low, group["pieces"], so_far, norm)
            keep, send, bias_sums = results[:3]
            if last:
                grad, sums_one = results[3:]
            else:
                so_far = results[3]
            total = plus(keep, swap(send))
            at = at_kept = 0
            for name in group["names"]:
                size = pairs_of[name] * 128
                sums_of[name] = bias_sums[0:2, at : at + size]
                at += size
                if not name.endswith("_too"):
                    size = size // 2 if name == "own" else size
                    kept_rows[name] = total[:, at_kept : at_kept + size]
                    at_kept += size
        attention_grads = summed(kept_rows["near"], kept_rows["far"], kept_rows["own"], core)
        matrices[layer] = (attention_grads, feed_grads)
        unit_sums = unit_sums[:, 0]
        part = unit_sums.shape[1] // 8

        def unit_part(start, count):
            return unit_sums[:, start * part : (start + count) * part].reshape(-1)

        own_keep, own_send = unit_part(0, 1), unit_part(1, 1)
        own = jnp.concatenate([jnp.where(first_core, own_keep, own_send), jnp.where(first_core, own_send, own_keep)])
        flat = jnp.concatenate(
            [
                jnp.stack([sums_one[0], sums_two[0], sums_one[1], sums_two[1], sums_two[2], sums_two[3]]),
                in_order(*[sums_of[name] for name in PIECES], core, chip),
                in_order(own, unit_part(2, 2), unit_part(4, 2), unit_part(6, 1), unit_part(7, 1), core, chip).reshape(-1, D),
            ]
        )
        vector_sums[layer] = lax.psum(flat, ("section", "dp", "tensor"))

    first_rows = row_to(0, grad)

    def rows_of(got):
        return [
            jnp.where(
                row == chip, got[0], jnp.where(row == chip ^ 1, got[1], jnp.where(row == chip ^ 2, got[2], got[3]))
            )
            for row in CHIPS
        ]

    ends_out = jnp.stack([jnp.where(first_core, a, b) for a, b in zip(rows_of(first_rows), rows_of(sent_back))])
    ends_out = ends_out.astype(f32).reshape(1, micro, rows_here, seg, D)

    def finished(lower, upper):
        to_upper = lax.ppermute(upper, "section", [(0, 1)])
        to_lower = lax.ppermute(lower, "section", [(1, 0)])
        return jnp.where(
            first_core,
            jnp.concatenate([lower, to_lower], axis=1),
            jnp.concatenate([to_upper, upper], axis=1),
        ).astype(f32)

    attention_grads, feed_grads = (finished(a, b) for a, b in zip(*matrices))
    sums = jnp.where(first_core, vector_sums[0], vector_sums[1])
    grad_qv = lax.dynamic_slice_in_dim(sums[6:8], chip * n_qv, n_qv, 1)[None]
    grad_up_bias = lax.dynamic_slice_in_dim(sums[8:].reshape(-1), chip * n_up, n_up, 0)[None]
    return (
        ends_out,
        sums[0:2][None],
        sums[2:4][None],
        jnp.swapaxes(attention_grads[:3], 1, 2)[None],
        grad_qv,
        attention_grads[3:],
        feed_grads[0].T[None],
        grad_up_bias,
        feed_grads[1:],
        sums[4:6][None],
    )


def solution(mesh):
    return jax.shard_map(
        on_row if one_row_a_chip(mesh) else on_device,
        mesh=mesh,
        in_specs=(
            P("section", None, "dp", "tensor", None),
            P(None, "dp"),
            P("section", None, None),
            P("section", None, None),
            P("section", None, None, "tensor"),
            P("section", None, "tensor"),
            P("section", "tensor", None),
            P("section", None, "tensor"),
            P("section", "tensor"),
            P("section", "tensor", None),
            P("section", None, None),
        ),
        out_specs=(
            P("section", None, "dp", "tensor", None),
            P("section", None, None),
            P("section", None, None),
            P("section", None, None, "tensor"),
            P("section", None, "tensor"),
            P("section", "tensor", None),
            P("section", None, "tensor"),
            P("section", "tensor"),
            P("section", "tensor", None),
            P("section", None, None),
        ),
        check_vma=False,
    )
```

```python
from functools import partial

import jax
import jax.numpy as jnp
from jax import lax
from jax.experimental import pallas as pl
from jax.experimental.pallas import tpu as pltpu
from jax.sharding import PartitionSpec as P

D = 1024
HEADS = 16


eps = 1e-05
widest = 512


def shifted(shard, axis, by):
    devices = lax.axis_size(axis)
    pairs = [(i, i + by) for i in range(devices) if 0 <= i + by < devices]
    return lax.ppermute(shard, axis, pairs)


def layer_norm(inputs, gain, bias):
    center = jnp.mean(inputs, axis=-1, keepdims=True)
    centred = inputs - center
    spread = jnp.mean(centred * centred, axis=-1, keepdims=True)
    factor = lax.rsqrt(spread + eps)
    normal = centred * factor
    return (normal * gain + bias, normal, factor)


def norm_back(grad_norm, normal, factor, gain):
    scaled = grad_norm * gain
    first_mean = jnp.mean(scaled, axis=-1, keepdims=True)
    second_mean = jnp.mean(scaled * normal, axis=-1, keepdims=True)
    return factor * (scaled - first_mean - normal * second_mean)


def gather_tokens(values):
    return lax.all_gather(values, "tensor", axis=1, tiled=True)


def scatter_tokens(values):
    return lax.psum_scatter(values, "tensor", scatter_dimension=1, tiled=True)


def gather_grads(values):
    return lax.all_gather(values, "tensor", axis=1, tiled=True)


def scatter_grads(values):
    return lax.psum_scatter(
        values.astype(jnp.bfloat16), "tensor", scatter_dimension=1, tiled=True
    ).astype(jnp.float32)


def project(whole_rows, w_proj, proj_bias):
    combined = jnp.einsum("rld,cde->crle", whole_rows, w_proj, preferred_element_type=jnp.float32)
    queries = (combined[0] + proj_bias[0]).astype(jnp.bfloat16)
    key_rows = combined[1].astype(jnp.bfloat16)
    value_rows = (combined[2] + proj_bias[1]).astype(jnp.bfloat16)
    return (queries, key_rows, value_rows)


def score_block(query_block, key_heads, row_start, row_lengths, slopes_here):
    block_rows = query_block.shape[1]
    seq_len = key_heads.shape[1]
    head_size = key_heads.shape[-1]
    scores = jnp.einsum(
        "rqhd,rkhd->rhqk", query_block, key_heads, preferred_element_type=jnp.float32
    ) * head_size ** (-0.5)
    rowpos = row_start + jnp.arange(block_rows)
    keypos = jnp.arange(seq_len)
    distance = (rowpos[:, None] - keypos[None, :]).astype(jnp.float32)
    scores = scores - slopes_here[None, :, None, None] * distance[None, None]
    causal = keypos[None, :] <= rowpos[:, None]
    inside = keypos[None, :] < row_lengths[:, None]
    allowed = causal[None, None] & inside[:, None, None, :]
    return jnp.where(allowed, scores, -1e30)


def attention(queries, key_rows, value_rows, row_lengths, slopes_here):
    row_count, seq_len, width = queries.shape
    head_count = slopes_here.shape[0]
    head_size = width // head_count
    block_rows = min(widest, seq_len)
    query_heads = queries.reshape(row_count, seq_len, head_count, head_size)
    key_heads = key_rows.reshape(row_count, seq_len, head_count, head_size)
    value_heads = value_rows.reshape(row_count, seq_len, head_count, head_size)

    def one_block(row_start):
        query_block = lax.dynamic_slice_in_dim(query_heads, row_start, block_rows, 1)
        scores = score_block(query_block, key_heads, row_start, row_lengths, slopes_here)
        row_max = jnp.max(scores, axis=-1, keepdims=True)
        powers = jnp.exp(scores - row_max)
        row_total = jnp.sum(powers, axis=-1, keepdims=True)
        probs = (powers / row_total).astype(jnp.bfloat16)
        block_out = jnp.einsum(
            "rhqk,rkhd->rqhd", probs, value_heads, preferred_element_type=jnp.float32
        )
        return (block_out.astype(jnp.bfloat16), (row_max + jnp.log(row_total))[..., 0])

    starts = jnp.arange(seq_len // block_rows) * block_rows
    blocks_out, log_totals = lax.map(one_block, starts)
    attended = jnp.moveaxis(blocks_out, 0, 1).reshape(row_count, seq_len, width)
    log_totals = jnp.moveaxis(log_totals, 0, 2).reshape(row_count, head_count, seq_len)
    return (attended, log_totals)


def attention_back(
    queries, key_rows, value_rows, grad_attended, log_totals, row_lengths, slopes_here
):
    row_count, seq_len, width = queries.shape
    head_count = slopes_here.shape[0]
    head_size = width // head_count
    scale = head_size ** (-0.5)
    block_rows = min(widest, seq_len)
    query_heads = queries.reshape(row_count, seq_len, head_count, head_size)
    key_heads = key_rows.reshape(row_count, seq_len, head_count, head_size)
    value_heads = value_rows.reshape(row_count, seq_len, head_count, head_size)
    grad_heads = grad_attended.reshape(row_count, seq_len, head_count, head_size)

    def one_block(carry, row_start):
        grad_keys, grad_values = carry
        query_block = lax.dynamic_slice_in_dim(query_heads, row_start, block_rows, 1)
        grad_block = lax.dynamic_slice_in_dim(grad_heads, row_start, block_rows, 1)
        scores = score_block(query_block, key_heads, row_start, row_lengths, slopes_here)
        block_logs = lax.dynamic_slice_in_dim(log_totals, row_start, block_rows, 2)
        probs = jnp.exp(scores - block_logs[..., None])
        grad_values = grad_values + jnp.einsum(
            "rhqk,rqhd->rkhd",
            probs.astype(jnp.bfloat16),
            grad_block,
            preferred_element_type=jnp.float32,
        )
        grad_probs = jnp.einsum(
            "rqhd,rkhd->rhqk", grad_block, value_heads, preferred_element_type=jnp.float32
        )
        inner = jnp.sum(probs * grad_probs, axis=-1, keepdims=True)
        grad_scores = (probs * (grad_probs - inner)).astype(jnp.bfloat16)
        grad_query = (
            jnp.einsum(
                "rhqk,rkhd->rqhd", grad_scores, key_heads, preferred_element_type=jnp.float32
            )
            * scale
        )
        grad_keys = (
            grad_keys
            + jnp.einsum(
                "rhqk,rqhd->rkhd", grad_scores, query_block, preferred_element_type=jnp.float32
            )
            * scale
        )
        return ((grad_keys, grad_values), grad_query.astype(jnp.bfloat16))

    zeros_heads = jnp.zeros((row_count, seq_len, head_count, head_size), jnp.float32)
    starts = jnp.arange(seq_len // block_rows) * block_rows
    (grad_keys, grad_values), grad_queries = lax.scan(one_block, (zeros_heads, zeros_heads), starts)
    grad_queries = jnp.moveaxis(grad_queries, 0, 1).reshape(row_count, seq_len, width)
    grad_keys = grad_keys.reshape(row_count, seq_len, width).astype(jnp.bfloat16)
    grad_values = grad_values.reshape(row_count, seq_len, width).astype(jnp.bfloat16)
    return (grad_queries, grad_keys, grad_values)


def layer_forward(inputs, row_lengths, weights, slopes_here):
    gains, biases, w_proj, proj_bias, w_attn, w_first, first_bias, w_second, end_biases = weights
    normed, _, _ = layer_norm(inputs, gains[0], biases[0])
    whole_rows = gather_tokens(normed.astype(jnp.bfloat16))
    queries, key_rows, value_rows = project(whole_rows, w_proj, proj_bias)
    attended, log_totals = attention(queries, key_rows, value_rows, row_lengths, slopes_here)
    attn_part = jnp.dot(attended, w_attn, preferred_element_type=jnp.float32)
    after_attn = inputs + scatter_tokens(attn_part) + end_biases[0]
    middle, _, _ = layer_norm(after_attn, gains[1], biases[1])
    middle_rows = gather_tokens(middle.astype(jnp.bfloat16))
    pre_act = jnp.dot(middle_rows, w_first, preferred_element_type=jnp.float32) + first_bias
    hidden = jax.nn.gelu(pre_act, approximate=True).astype(jnp.bfloat16)
    ffn_part = jnp.dot(hidden, w_second, preferred_element_type=jnp.float32)
    result = after_attn + scatter_tokens(ffn_part) + end_biases[1]
    return (result, after_attn, attended, log_totals, whole_rows, middle_rows)


def layer_backward(grad_result, stored, row_lengths, weights, slopes_here):
    gains, biases, w_proj, proj_bias, w_attn, w_first, first_bias, w_second, end_biases = weights
    inputs = stored[0].astype(jnp.float32)
    after_attn = stored[1]
    attended = stored[2]
    log_totals = stored[3]
    normed, normal_one, factor_one = layer_norm(inputs, gains[0], biases[0])
    middle, normal_two, factor_two = layer_norm(after_attn, gains[1], biases[1])
    whole_rows = gather_tokens(normed.astype(jnp.bfloat16))
    middle_rows = gather_tokens(middle.astype(jnp.bfloat16))
    pre_act = jnp.dot(middle_rows, w_first, preferred_element_type=jnp.float32) + first_bias
    hidden, gelu_pull = jax.vjp(partial(jax.nn.gelu, approximate=True), pre_act)
    hidden = hidden.astype(jnp.bfloat16)
    grad_end_two = jnp.sum(grad_result, axis=(0, 1))
    grad_branch = gather_grads(grad_result.astype(jnp.bfloat16))
    grad_second = jnp.einsum("rlf,rld->fd", hidden, grad_branch, preferred_element_type=jnp.float32)
    grad_hidden = jnp.einsum(
        "rld,fd->rlf", grad_branch, w_second, preferred_element_type=jnp.float32
    )
    grad_pre = gelu_pull(grad_hidden)[0].astype(jnp.bfloat16)
    grad_first_bias = jnp.sum(grad_pre, axis=(0, 1), dtype=jnp.float32)
    grad_first = jnp.einsum(
        "rld,rlf->df", middle_rows, grad_pre, preferred_element_type=jnp.float32
    )
    grad_middle = scatter_grads(
        jnp.einsum("rlf,df->rld", grad_pre, w_first, preferred_element_type=jnp.float32)
    )
    grad_gain_two = jnp.sum(grad_middle * normal_two, axis=(0, 1))
    grad_bias_two = jnp.sum(grad_middle, axis=(0, 1))
    grad_after = grad_result + norm_back(grad_middle, normal_two, factor_two, gains[1])
    grad_end_one = jnp.sum(grad_after, axis=(0, 1))
    grad_attn_rows = gather_grads(grad_after.astype(jnp.bfloat16))
    grad_attn = jnp.einsum(
        "rle,rld->ed", attended, grad_attn_rows, preferred_element_type=jnp.float32
    )
    grad_attended = jnp.einsum(
        "rld,ed->rle", grad_attn_rows, w_attn, preferred_element_type=jnp.float32
    ).astype(jnp.bfloat16)
    queries, key_rows, value_rows = project(whole_rows, w_proj, proj_bias)
    grad_queries, grad_keys, grad_values = attention_back(
        queries, key_rows, value_rows, grad_attended, log_totals, row_lengths, slopes_here
    )
    stacked = jnp.stack([grad_queries, grad_keys, grad_values])
    grad_proj = jnp.einsum("rld,crle->cde", whole_rows, stacked, preferred_element_type=jnp.float32)
    grad_proj_bias = jnp.stack(
        [
            jnp.sum(grad_queries, axis=(0, 1), dtype=jnp.float32),
            jnp.sum(grad_values, axis=(0, 1), dtype=jnp.float32),
        ]
    )
    grad_normed = scatter_grads(
        jnp.einsum("crle,cde->rld", stacked, w_proj, preferred_element_type=jnp.float32)
    )
    grad_gain_one = jnp.sum(grad_normed * normal_one, axis=(0, 1))
    grad_bias_one = jnp.sum(grad_normed, axis=(0, 1))
    grad_inputs = grad_after + norm_back(grad_normed, normal_one, factor_one, gains[0])
    sharded = (grad_proj, grad_proj_bias, grad_attn, grad_first, grad_first_bias, grad_second)
    shared = (
        jnp.stack([grad_gain_one, grad_gain_two]),
        jnp.stack([grad_bias_one, grad_bias_two]),
        jnp.stack([grad_end_one, grad_end_two]),
    )
    return (grad_inputs, sharded, shared)


def on_device(
    ends_in, lengths, ln_gains, ln_biases, w_qkv, qv_bias, w_out, w_up, up_bias, w_down, out_biases
):
    section_index = lax.axis_index("section")
    weights = tuple(
        (
            stored[0]
            for stored in (
                ln_gains,
                ln_biases,
                w_qkv,
                qv_bias,
                w_out,
                w_up,
                up_bias,
                w_down,
                out_biases,
            )
        )
    )
    local_ends = ends_in[0]
    micro_count = local_ends.shape[0]
    heads_here = w_qkv.shape[-1] // (D // HEADS)
    first_head = lax.axis_index("tensor") * heads_here
    slopes_here = jnp.exp2(
        -8.0 * (first_head + jnp.arange(heads_here) + 1).astype(jnp.float32) / HEADS
    )
    padded = jnp.concatenate([local_ends, jnp.zeros_like(local_ends[:1])], axis=0)
    tick_list = jnp.arange(micro_count + 1)

    def forward_tick(received, item):
        arriving, tick_index = item
        entering = jnp.where(section_index == 0, arriving, received)
        slot_index = jnp.clip(tick_index - section_index, 0, micro_count - 1)
        row_lengths = lax.dynamic_index_in_dim(lengths, slot_index, 0, keepdims=False)
        result, after_attn, attended, log_totals, whole_rows, middle_rows = layer_forward(
            entering.astype(jnp.float32), row_lengths, weights, slopes_here
        )
        outgoing = shifted(result.astype(jnp.bfloat16), "section", 1)
        stored = (entering, after_attn, attended, log_totals)
        return (outgoing, (result, stored))

    _, (results, kept_all) = lax.scan(
        forward_tick, jnp.zeros_like(local_ends[0]), (padded, tick_list)
    )
    sharded_zero = (
        jnp.zeros(w_qkv.shape[1:], jnp.float32),
        jnp.zeros(qv_bias.shape[1:], jnp.float32),
        jnp.zeros(w_out.shape[1:], jnp.float32),
        jnp.zeros(w_up.shape[1:], jnp.float32),
        jnp.zeros(up_bias.shape[1:], jnp.float32),
        jnp.zeros(w_down.shape[1:], jnp.float32),
    )
    shared_zero = (
        jnp.zeros(ln_gains.shape[1:], jnp.float32),
        jnp.zeros(ln_biases.shape[1:], jnp.float32),
        jnp.zeros(out_biases.shape[1:], jnp.float32),
    )

    def backward_tick(carry, item):
        received, sharded_total, shared_total = carry
        arriving, tick_index = item
        grad_result = jnp.where(section_index == 1, arriving, received).astype(jnp.float32)
        slot_index = tick_index - 1 + section_index
        is_valid = ((slot_index >= 0) & (slot_index < micro_count)).astype(jnp.float32)
        slot_index = jnp.clip(slot_index, 0, micro_count - 1)
        stored = tuple(
            (
                lax.dynamic_index_in_dim(kept, slot_index + section_index, 0, keepdims=False)
                for kept in kept_all
            )
        )
        row_lengths = lax.dynamic_index_in_dim(lengths, slot_index, 0, keepdims=False)
        grad_inputs, sharded, shared = layer_backward(
            grad_result, stored, row_lengths, weights, slopes_here
        )
        outgoing = shifted(grad_inputs.astype(jnp.bfloat16), "section", -1)
        sharded = tuple((value * is_valid for value in sharded))
        shared = tuple((value * is_valid for value in shared))
        sharded_total = tuple((left + right for left, right in zip(sharded_total, sharded)))
        shared_total = tuple((left + right for left, right in zip(shared_total, shared)))
        return ((outgoing, sharded_total, shared_total), grad_inputs)

    start_carry = (jnp.zeros_like(local_ends[0]), sharded_zero, shared_zero)
    (_, sharded_total, shared_total), grads_in = lax.scan(
        backward_tick, start_carry, (padded, tick_list)
    )
    sharded_total = (
        lax.psum(sharded_total[0].astype(jnp.bfloat16), "dp").astype(jnp.float32),
        lax.psum(sharded_total[1].astype(jnp.bfloat16), "dp").astype(jnp.float32),
        lax.psum(sharded_total[2].astype(jnp.bfloat16), "dp").astype(jnp.float32),
        lax.psum(sharded_total[3].astype(jnp.bfloat16), "dp").astype(jnp.float32),
        lax.psum(sharded_total[4].astype(jnp.bfloat16), "dp").astype(jnp.float32),
        lax.psum(sharded_total[5].astype(jnp.bfloat16), "dp").astype(jnp.float32),
    )
    shared_total = lax.psum((shared_total[0], shared_total[1], shared_total[2]), ("dp", "tensor"))
    ends_local = jnp.where(section_index == 0, grads_in[1:], results[1:])
    return (
        ends_local[None],
        shared_total[0][None],
        shared_total[1][None],
        sharded_total[0][None],
        sharded_total[1][None],
        sharded_total[2][None],
        sharded_total[3][None],
        sharded_total[4][None],
        sharded_total[5][None],
        shared_total[2][None],
    )


bf16, f32 = jnp.bfloat16, jnp.float32
HEAD = D // HEADS
LOG2E = 1.4426950408889634
GROUP = 4
ST = ("section", "tensor")
MIB = 2**20


def one_row_a_chip(mesh):
    return mesh.shape["section"] == 2 and mesh.shape["tensor"] == GROUP


def core_of(segment):
    return (segment & 1) ^ (segment >> 1)


def place(core, chip):
    return core * GROUP + chip


CHIPS = range(GROUP)
FIRST_HOP = [(place(0, t), place(0, t ^ 1)) for t in CHIPS] + [(place(1, t), place(1, t ^ 2)) for t in CHIPS]
LAST_HOP = [(place(c, t), place(c, t ^ 3)) for c in range(2) for t in CHIPS]
SECOND_HOP = [(place(0, t), place(0, t ^ 2)) for t in CHIPS] + [(place(1, t), place(1, t ^ 1)) for t in CHIPS]


def hop(value, pairs):
    return lax.ppermute(value, ST, pairs)


def swap(value):
    return lax.ppermute(value, "section", [(0, 1), (1, 0)])


def half_of(value, axis, index):
    size = value.shape[axis] // 2
    return lax.dynamic_slice_in_dim(value, index * size, size, axis)


def dot_nn(left, right):
    return lax.dot_general(left, right, (((1,), (0,)), ((), ())), preferred_element_type=f32)


def dot_nt(left, right):
    return lax.dot_general(left, right, (((1,), (1,)), ((), ())), preferred_element_type=f32)


def dot_tn(left, right):
    return lax.dot_general(left, right, (((0,), (0,)), ((), ())), preferred_element_type=f32)


def three_parts(value):
    first = value.astype(bf16)
    rest = value - first.astype(f32)
    second = rest.astype(bf16)
    third = (rest - second.astype(f32)).astype(bf16)
    return first, second, third


def key_columns(positions, length):
    high = (positions // 8 * 8).astype(f32)
    low = (positions % 8).astype(f32)
    mask = jnp.where(positions < length, 0.0, -1e30).astype(f32)
    one = jnp.ones_like(high)
    columns = jnp.stack([high, high, high, low, low, low, mask, one, one, one], axis=1)
    half = jnp.pad(columns, ((0, 0), (0, HEAD - 10)))
    return jnp.concatenate([half, half], axis=1).astype(bf16)


def query_columns(slopes):
    first, second, third = three_parts(slopes * 8.0)
    one = jnp.ones_like(first)
    columns = jnp.stack([first, second, third, first, second, third, one], axis=1)
    half = jnp.pad(columns, ((0, 0), (0, HEAD - 7))).reshape(-1, 2, HEAD)
    row = jnp.concatenate([half[:, 1], half[:, 0]], axis=1).astype(f32)
    return jnp.broadcast_to(row[:, None, :], (row.shape[0], 8, 2 * HEAD))


def attend_kernel(seg, meta, q, kv, kvo, kcol, qcol, o, qx, qp, kp, vp, st_m, st_a):
    other = 1 - meta[0]
    lane = lax.broadcasted_iota(jnp.int32, (1, 128), 1)
    low = lane < 64
    base = qcol[0, 0:1, :].astype(bf16)
    scale = LOG2E / 8
    one = jnp.ones((1, 128), bf16)
    for h in range(2):
        mine = low if h == 0 else ~low
        qp[h] = jnp.where(mine, q[...], base)
        kp[h, 0 : 2 * seg] = jnp.where(mine, kv[0], kcol[0 : 2 * seg])
        kp[h, 2 * seg :] = jnp.where(mine, kvo[0], kcol[2 * seg :])
        vp[h, 0 : 2 * seg] = jnp.where(mine, kv[1], one)
        vp[h, 2 * seg :] = jnp.where(mine, kvo[1], one)

    def scores_of(h, start, keys, masked):
        queries = qp[h, pl.ds(start, seg)]
        scores = []
        for n, (key_start, key_count) in enumerate(keys):
            part = dot_nt(queries, kp[h, pl.ds(key_start, key_count)])
            if masked and n == len(keys) - 1:
                row = lax.broadcasted_iota(jnp.int32, (seg, key_count), 0)
                column = lax.broadcasted_iota(jnp.int32, (seg, key_count), 1)
                part = jnp.where(column <= row, part, -1e30)
            scores.append(part)
        top = scores[0].max(axis=1, keepdims=True)
        for part in scores[1:]:
            top = jnp.maximum(top, part.max(axis=1, keepdims=True))
        return scores, top

    def weigh(h, scores, top, keys):
        total = None
        for part, (key_start, key_count) in zip(scores, keys):
            powers = jnp.exp2((part - top) * scale).astype(bf16)
            term = dot_nn(powers, vp[h, pl.ds(key_start, key_count)])
            total = term if total is None else total + term
        return total

    for h in range(2):
        start = pl.multiple_of(other * seg, seg)
        keys = [(pl.multiple_of(2 * seg + other * seg, seg), seg)]
        scores, top = scores_of(h, start, keys, False)
        st_a[h] = weigh(h, scores, top, keys)
        st_m[h] = jnp.broadcast_to(top, (seg, 128))
    for segment in range(2):
        use = other == segment
        rows = slice(segment * seg, (segment + 1) * seg)
        totals, tops = [], []
        for h in range(2):
            keys = [(segment * seg, seg)]
            if segment == 1:
                keys = [(0, seg), (2 * seg, seg)] + keys
            scores, top = scores_of(h, segment * seg, keys, True)
            fifth = jnp.where(use, st_m[h][:, 0:1], -1e30)
            top = jnp.maximum(top, fifth)
            weight = jnp.where(use, jnp.exp2((fifth - top) * scale), 0.0)
            totals.append(weigh(h, scores, top, keys) + weight * st_a[h])
            tops.append(top)
        number = jnp.where(low, totals[0], totals[1])
        sums = jnp.where(low, totals[1], totals[0])
        o[rows] = (number / pltpu.roll(sums, 64, 1)).astype(bf16)
        logs = jnp.where(low, tops[1], tops[0]) + jnp.log(sums) * 8.0
        first, second, third = three_parts(logs)
        at = lane & 63
        qx[rows] = jnp.where(at == 7, -first, jnp.where(at == 8, -second, jnp.where(at == 9, -third, base)))


def attend(meta, q, kv, kvo, kcol, qcol):
    rows, width = q.shape
    seg = rows // 2
    pairs = width // 128
    block = pl.BlockSpec((rows, 128), lambda i, m: (0, i))
    return pl.pallas_call(
        partial(attend_kernel, seg),
        grid_spec=pltpu.PrefetchScalarGridSpec(
            num_scalar_prefetch=1,
            grid=(pairs,),
            in_specs=[
                block,
                pl.BlockSpec((2, rows, 128), lambda i, m: (0, 0, i)),
                pl.BlockSpec((2, rows, 128), lambda i, m: (0, 0, m[1 + i])),
                pl.BlockSpec((2 * rows, 128), lambda i, m: (0, 0)),
                pl.BlockSpec((1, 8, 128), lambda i, m: (i, 0, 0)),
            ],
            out_specs=[block, block],
            scratch_shapes=[
                pltpu.VMEM((2, rows, 128), bf16),
                pltpu.VMEM((2, 2 * rows, 128), bf16),
                pltpu.VMEM((2, 2 * rows, 128), bf16),
                pltpu.VMEM((2, seg, 128), f32),
                pltpu.VMEM((2, seg, 128), f32),
            ],
        ),
        out_shape=[jax.ShapeDtypeStruct((rows, width), bf16)] * 2,
        compiler_params=pltpu.CompilerParams(vmem_limit_bytes=60 * MIB),
        cost_estimate=cost(
            flops=40 * 256 * seg * seg * pairs, bytes_accessed=rows * width * 14, transcendentals=10 * seg * seg * pairs
        ),
        name="attend",
    )(meta, q, kv, kvo, kcol, qcol)


def attend_back_kernel(
    seg, meta, q, kv, kvo, kcol, qx, do, o, dq, dkv, dkvo, qp, kp, vp, dp, kt, qm, dm, aq, ak, av
):
    other = 1 - meta[0]
    lane = lax.broadcasted_iota(jnp.int32, (1, 128), 1)
    low = lane < 64
    at = lane & 63
    scale = LOG2E / 8
    zero = jnp.zeros((1, 128), bf16)
    product = do[...].astype(f32) * o[...].astype(f32)
    for h in range(2):
        mine = low if h == 0 else ~low
        qp[h] = jnp.where(mine, q[...], qx[...])
        kp[h, 0 : 2 * seg] = jnp.where(mine, kv[0], kcol[0 : 2 * seg])
        kp[h, 2 * seg :] = jnp.where(mine, kvo[0], kcol[2 * seg :])
        vp[h, 0 : 2 * seg] = jnp.where(mine, kv[1], kcol[0 : 2 * seg])
        vp[h, 2 * seg :] = jnp.where(mine, kvo[1], kcol[2 * seg :])
        first, second, third = three_parts(jnp.sum(jnp.where(mine, product, 0.0), axis=1, keepdims=True))
        extra = jnp.where(at == 7, -first, jnp.where(at == 8, -second, jnp.where(at == 9, -third, zero)))
        dp[h] = jnp.where(mine, do[...], extra)
        qm[h] = jnp.where(mine, q[...], zero)
        dm[h] = jnp.where(mine, do[...], zero)
    kt[:, 0 : 2 * seg] = kv[0].T
    kt[:, 2 * seg :] = kvo[0].T
    aq[...] = jnp.zeros_like(aq)
    ak[...] = jnp.zeros_like(ak)
    av[...] = jnp.zeros_like(av)

    def block(query_start, query_count, key_start, key_count, masked):
        queries, keys = pl.ds(query_start, query_count), pl.ds(key_start, key_count)
        for h in range(2):
            probs = jnp.exp2(dot_nt(kp[h, keys], qp[h, queries]) * scale)
            if masked:
                row = lax.broadcasted_iota(jnp.int32, (key_count, query_count), 0)
                column = lax.broadcasted_iota(jnp.int32, (key_count, query_count), 1)
                probs = jnp.where(row <= column, probs, 0.0)
            grads = (probs * dot_nt(vp[h, keys], dp[h, queries])).astype(bf16)
            av[keys] += dot_nn(probs.astype(bf16), dm[h, queries])
            ak[keys] += dot_nn(grads, qm[h, queries])
            aq[h * 64 : (h + 1) * 64, queries] += dot_nn(kt[h * 64 : (h + 1) * 64, keys], grads)

    half = seg // 2
    for segment in range(2):
        start = segment * seg
        block(start, half, start, half, True)
        block(start + half, half, start, half, False)
        block(start + half, half, start + half, half, True)
    block(seg, seg, 0, seg, False)
    block(seg, seg, 2 * seg, seg, False)
    block(pl.multiple_of(other * seg, seg), seg, pl.multiple_of(2 * seg + other * seg, seg), seg, False)
    dq[...] = (aq[...] * 0.125).T.astype(bf16)
    dkv[0] = (ak[0 : 2 * seg] * 0.125).astype(bf16)
    dkvo[0] = (ak[2 * seg :] * 0.125).astype(bf16)
    dkv[1] = av[0 : 2 * seg].astype(bf16)
    dkvo[1] = av[2 * seg :].astype(bf16)


def attend_back(meta, q, kv, kvo, kcol, qx, do, o):
    rows, width = q.shape
    seg = rows // 2
    pairs = width // 128
    block = pl.BlockSpec((rows, 128), lambda i, m: (0, i))
    mine = pl.BlockSpec((2, rows, 128), lambda i, m: (0, 0, i))
    theirs = pl.BlockSpec((2, rows, 128), lambda i, m: (0, 0, m[1 + i]))
    return pl.pallas_call(
        partial(attend_back_kernel, seg),
        grid_spec=pltpu.PrefetchScalarGridSpec(
            num_scalar_prefetch=1,
            grid=(pairs,),
            in_specs=[block, mine, theirs, pl.BlockSpec((2 * rows, 128), lambda i, m: (0, 0))] + [block] * 3,
            out_specs=[block, mine, theirs],
            scratch_shapes=[
                pltpu.VMEM((2, rows, 128), bf16),
                pltpu.VMEM((2, 2 * rows, 128), bf16),
                pltpu.VMEM((2, 2 * rows, 128), bf16),
                pltpu.VMEM((2, rows, 128), bf16),
                pltpu.VMEM((128, 2 * rows), bf16),
                pltpu.VMEM((2, rows, 128), bf16),
                pltpu.VMEM((2, rows, 128), bf16),
                pltpu.VMEM((128, rows), f32),
                pltpu.VMEM((2 * rows, 128), f32),
                pltpu.VMEM((2 * rows, 128), f32),
            ],
        ),
        out_shape=[
            jax.ShapeDtypeStruct((rows, width), bf16),
            jax.ShapeDtypeStruct((2, rows, width), bf16),
            jax.ShapeDtypeStruct((2, rows, width), bf16),
        ],
        compiler_params=pltpu.CompilerParams(vmem_limit_bytes=60 * MIB),
        cost_estimate=cost(
            flops=100 * 256 * seg * seg * pairs, bytes_accessed=rows * width * 26, transcendentals=10 * seg * seg * pairs
        ),
        name="attend_back",
    )(meta, q, kv, kvo, kcol, qx, do, o)


PART = 8


def cost(flops, bytes_accessed, transcendentals):
    return pl.CostEstimate(flops=flops // PART, bytes_accessed=bytes_accessed // PART, transcendentals=transcendentals // PART)


def fixed(shape):
    return pl.BlockSpec(shape, lambda *_: (0,) * len(shape), pipeline_mode=pl.Buffered(1))


BIAS_ROWS = 16


def units_of(piece):
    return (piece.shape[0] - BIAS_ROWS) // 4


def joined(refs, size=0, matrix=0):
    parts = [ref[matrix * ref.shape[0] // size : (matrix + 1) * ref.shape[0] // size] if size else ref[...] for ref in refs]
    return jnp.concatenate(parts, axis=0) if len(parts) > 1 else parts[0]


def project_kernel(count, a, *refs):
    pieces, bias, q, kv = refs[:count], refs[count], refs[count + 1], refs[count + 2]
    step = pl.program_id(0)
    result = (dot_nt(a[...], joined(pieces)) + bias[0]).astype(bf16)

    @pl.when(step == 0)
    def _():
        q[...] = result

    @pl.when(step > 0)
    def _():
        kv[0] = result


def project_heads(a, pieces, bias):
    rows, width = a.shape
    columns = sum(units_of(piece) for piece in pieces)
    return pl.pallas_call(
        partial(project_kernel, len(pieces)),
        grid=(3,),
        in_specs=[fixed(a.shape)]
        + [pl.BlockSpec((units_of(piece), width), lambda i: (i, 0)) for piece in pieces]
        + [pl.BlockSpec((1, 1, columns), lambda i: (i, 0, 0))],
        out_specs=[
            pl.BlockSpec((rows, columns), lambda i: (0, 0)),
            pl.BlockSpec((1, rows, columns), lambda i: (jnp.maximum(i - 1, 0), 0, 0)),
        ],
        out_shape=[jax.ShapeDtypeStruct((rows, columns), bf16), jax.ShapeDtypeStruct((2, rows, columns), bf16)],
        cost_estimate=cost(
            flops=6 * rows * width * columns, bytes_accessed=2 * rows * width + 6 * width * columns + 6 * rows * columns, transcendentals=0
        ),
        compiler_params=pltpu.CompilerParams(vmem_limit_bytes=60 * MIB),
        name="project",
    )(a, *pieces, bias)


def normalize(value):
    center = jnp.mean(value, axis=-1, keepdims=True)
    centred = value - center
    spread = jnp.mean(centred * centred, axis=-1, keepdims=True)
    factor = lax.rsqrt(spread + eps)
    return centred * factor, factor


def normed_rows(value, vectors):
    normal, _ = normalize(value)
    return (normal * vectors[1:2] + vectors[2:3]).astype(bf16)


def first_norm_kernel(x, vectors, out):
    out[...] = normed_rows(x[...].astype(f32), vectors)


def first_norm(x, vectors):
    rows, width = x.shape
    tile = rows // 4
    return pl.pallas_call(
        first_norm_kernel,
        grid=(rows // tile,),
        in_specs=[pl.BlockSpec((tile, width), lambda i: (i, 0)), fixed(vectors.shape)],
        out_specs=pl.BlockSpec((tile, width), lambda i: (i, 0)),
        out_shape=jax.ShapeDtypeStruct((rows, width), bf16),
        name="first_norm",
    )(x, vectors)


def eight_rows(*rows):
    return jnp.concatenate([jnp.stack(rows), jnp.zeros((8 - len(rows), rows[0].shape[-1]), f32)])


STEPS = 4
GELU_A = 0.7978845608028654
GELU_B = 0.044715


def share_specs(pieces, steps):
    specs = [pl.BlockSpec((2, 2, pieces[0].shape[2] // steps, pieces[0].shape[3]), lambda i, m: (0, 0, i, 0))]
    for piece in pieces[1:]:
        specs.append(pl.BlockSpec((2, piece.shape[1] // steps, piece.shape[2]), lambda i, m: (0, i, 0)))
    return specs


def share(refs, matrix, core):
    own = refs[0]
    return jnp.concatenate([own[matrix, core], own[matrix, 1 - core]] + [ref[matrix] for ref in refs[1:]], axis=0)


def feed_rows(middle, up, down, bias):
    u = dot_nt(middle, up) + bias
    square = u * u
    t = jnp.tanh(u * (GELU_A + (GELU_A * GELU_B) * square))
    half = 0.5 * u
    value = (half + half * t).astype(bf16)
    slope = 0.5 + 0.5 * t + (half - half * t * t) * (GELU_A + (3 * GELU_A * GELU_B) * square)
    return slope.astype(bf16), value, dot_nn(value, down)


def feed_kernel(counts, meta, *refs):
    heads, weights = refs[: counts[0]], refs[counts[0] : sum(counts)]
    x, vectors, bias, own, near, near_too, slope, hidden, after, middle, total = refs[sum(counts) :]
    core = meta[0]
    tile = total.shape[0] // 4

    @pl.when(pl.program_id(0) == 0)
    def _():
        for n in range(4):
            at = slice(n * tile, (n + 1) * tile)
            left = jnp.concatenate([ref[at] for ref in heads], axis=1)
            value = x[at].astype(f32) + vectors[0:1] + dot_nn(left, joined(weights))
            after[at] = value
            middle[at] = normed_rows(value, vectors)
            total[at] = value + vectors[3:4]

    refs = (own, near, near_too)
    up, down = share(refs, 0, core), share(refs, 1, core)
    for n in range(4):
        at = slice(n * tile, (n + 1) * tile)
        slope[0, at], hidden[0, at], term = feed_rows(middle[at], up, down, bias[0])
        total[at] += term


def feed(meta, x, heads, heads_pieces, vectors, bias, pieces):
    rows, width = x.shape
    units = 3 * pieces[1].shape[1]
    steps = STEPS
    wide = units // steps
    per_step = pl.BlockSpec((1, rows, wide), lambda i, m: (i, 0, 0))
    whole = pl.BlockSpec((rows, width), lambda i, m: (0, 0))
    return pl.pallas_call(
        partial(feed_kernel, (len(heads), len(heads_pieces))),
        grid_spec=pltpu.PrefetchScalarGridSpec(
            num_scalar_prefetch=1,
            grid=(steps,),
            in_specs=[fixed(h.shape) for h in heads]
            + [pl.BlockSpec((units_of(p), width), lambda i, m: (3, 0), pipeline_mode=pl.Buffered(1)) for p in heads_pieces]
            + [fixed(x.shape), fixed(vectors.shape), pl.BlockSpec((1, 1, wide), lambda i, m: (i, 0, 0))]
            + share_specs(pieces[:3], steps),
            out_specs=[per_step, per_step, whole, whole, whole],
        ),
        out_shape=[jax.ShapeDtypeStruct((steps, rows, wide), bf16)] * 2
        + [jax.ShapeDtypeStruct((rows, width), kind) for kind in (f32, bf16, f32)],
        cost_estimate=cost(
            flops=2 * rows * width * (2 * units + width), bytes_accessed=4 * units * (rows + width) + 16 * rows * width, transcendentals=rows * units
        ),
        compiler_params=pltpu.CompilerParams(vmem_limit_bytes=60 * MIB),
        name="feed",
    )(meta, *heads, *heads_pieces, x, vectors, bias, *pieces[:3])


def feed_last_kernel(middle, so_far, vectors, bias, far, far_too, slope, hidden, out, normed, weights):
    steps = slope.shape[0]

    @pl.when(pl.program_id(0) == 0)
    def _():
        size = far.shape[1] // steps
        for n in range(2):
            for i in range(steps):
                weights[n, 2 * i * size : (2 * i + 1) * size] = far[n, i * size : (i + 1) * size]
                weights[n, (2 * i + 1) * size : (2 * i + 2) * size] = far_too[n, i * size : (i + 1) * size]

    slopes, values, term = feed_rows(middle[...], weights[0], weights[1], bias[...])
    wide = slope.shape[2]
    for i in range(steps):
        slope[i] = slopes[:, i * wide : (i + 1) * wide]
        hidden[i] = values[:, i * wide : (i + 1) * wide]
    value = (so_far[...] + term).astype(bf16)
    out[...] = value
    normed[...] = normed_rows(value.astype(f32), vectors)


def feed_last(middle, so_far, vectors, bias, pieces):
    rows, width = middle.shape
    units = pieces[1].shape[1]
    steps = STEPS
    wide = units // steps
    tile = rows // 4
    slim = pl.BlockSpec((tile, width), lambda i: (i, 0))
    per_step = pl.BlockSpec((steps, tile, wide), lambda i: (0, i, 0))
    return pl.pallas_call(
        feed_last_kernel,
        grid=(rows // tile,),
        in_specs=[slim, slim, fixed(vectors.shape), fixed(bias.shape), fixed(pieces[3].shape), fixed(pieces[4].shape)],
        out_specs=[per_step, per_step, slim, slim],
        out_shape=[jax.ShapeDtypeStruct((steps, rows, wide), bf16)] * 2 + [jax.ShapeDtypeStruct((rows, width), bf16)] * 2,
        scratch_shapes=[pltpu.VMEM((2, units, width), bf16)],
        cost_estimate=cost(
            flops=4 * rows * width * units, bytes_accessed=4 * units * (rows + width) + 10 * rows * width, transcendentals=rows * units
        ),
        compiler_params=pltpu.CompilerParams(vmem_limit_bytes=60 * MIB),
        name="feed_last",
    )(middle, so_far, vectors, bias, pieces[3], pieces[4])


def norm_back_rows(total, value, above, gain):
    normal, factor = normalize(value)
    scaled = total * gain
    first = jnp.mean(scaled, axis=-1, keepdims=True)
    second = jnp.mean(scaled * normal, axis=-1, keepdims=True)
    return above + factor * (scaled - first - normal * second), normal


def norm_back_all(total, value, above, gain, low, sums):
    tile = total.shape[0] // 4
    rows = []
    for n in range(4):
        at = slice(n * tile, (n + 1) * tile)
        part = total[at]
        top = above[at].astype(f32)
        grad, normal = norm_back_rows(part, value[at].astype(f32), top, gain)
        low[at] = grad.astype(bf16)
        rows.append([jnp.sum(v, axis=0, keepdims=True) for v in (part * normal, part, grad, top)])
    for n in range(4):
        sums[n : n + 1] = rows[0][n] + rows[1][n] + rows[2][n] + rows[3][n]


def feed_back_kernel(
    meta, above, middle, after, vectors, slope, slope_last, hidden, hidden_last, own, near, near_too, far, far_too,
    keep, send, bias_sums, low, sums, total
):
    core = meta[0]
    step = pl.program_id(0)
    refs = (own, near, near_too, far, far_too)
    up, down = share(refs, 0, core), share(refs, 1, core)
    part = up.shape[0] // 8

    def spread(n, value):
        value = value.astype(bf16)
        keep[n, 0, 0 : 2 * part] = value[2 * part : 4 * part]
        keep[n, 0, 2 * part : 3 * part] = value[6 * part : 7 * part]
        keep[n, 0, 3 * part :] = value[0:part]
        send[n, 0, 0 : 2 * part] = value[4 * part : 6 * part]
        send[n, 0, 2 * part : 3 * part] = value[7 * part :]
        send[n, 0, 3 * part :] = value[part : 2 * part]

    @pl.when(step == 0)
    def _():
        total[...] = jnp.zeros_like(total)

    slopes = jnp.concatenate([slope[0], slope_last[0]], axis=1)
    values = jnp.concatenate([hidden[0], hidden_last[0]], axis=1)
    grad = dot_nt(above[...], down) * slopes.astype(f32)
    bias_sums[0] = jnp.broadcast_to(jnp.sum(grad, axis=0, keepdims=True), bias_sums.shape[1:])
    low_grad = grad.astype(bf16)
    spread(1, dot_tn(values, above[...]))
    total[...] += dot_nn(low_grad, up)
    spread(0, dot_tn(low_grad, middle[...]))

    @pl.when(step == pl.num_programs(0) - 1)
    def _():
        norm_back_all(total, after, above, vectors[0:1], low, sums)


def feed_back(meta, above, middle, after, gain, slopes, values, pieces):
    rows, width = middle.shape
    units = 4 * pieces[1].shape[1]
    steps = STEPS
    wide = units // steps
    vectors = jnp.broadcast_to(gain[None], (8, width))
    per_step = [pl.BlockSpec((1, rows, v.shape[2]), lambda i, m: (i, 0, 0)) for v in slopes]
    grads = pl.BlockSpec((2, 1, wide // 2, width), lambda i, m: (0, i, 0, 0))
    return pl.pallas_call(
        feed_back_kernel,
        grid_spec=pltpu.PrefetchScalarGridSpec(
            num_scalar_prefetch=1,
            grid=(steps,),
            in_specs=[fixed(above.shape), fixed(middle.shape), fixed(after.shape), fixed(vectors.shape)] + per_step * 2
            + share_specs(pieces, steps),
            out_specs=[grads, grads, pl.BlockSpec((1, 8, wide), lambda i, m: (i, 0, 0)), pl.BlockSpec((rows, width), lambda i, m: (0, 0)), pl.BlockSpec((8, width), lambda i, m: (0, 0))],
            scratch_shapes=[pltpu.VMEM((rows, width), f32)],
        ),
        out_shape=[jax.ShapeDtypeStruct((2, steps, wide // 2, width), bf16)] * 2
        + [
            jax.ShapeDtypeStruct((steps, 8, wide), f32),
            jax.ShapeDtypeStruct((rows, width), bf16),
            jax.ShapeDtypeStruct((8, width), f32),
        ],
        cost_estimate=cost(
            flops=8 * rows * width * units, bytes_accessed=12 * units * (rows + width) + 14 * rows * width, transcendentals=0
        ),
        compiler_params=pltpu.CompilerParams(vmem_limit_bytes=60 * MIB),
        name="feed_back",
    )(meta, above, middle, after, vectors, *slopes, *values, *pieces)


def heads_back_kernel(count, low, *refs):
    pieces, out = refs[:count], refs[count]
    out[...] = dot_nt(low[...], joined(pieces)).astype(bf16)


def heads_back(low, pieces):
    rows, width = low.shape
    columns = sum(units_of(piece) for piece in pieces)
    tile = rows // 2
    return pl.pallas_call(
        partial(heads_back_kernel, len(pieces)),
        grid=(rows // tile,),
        in_specs=[pl.BlockSpec((tile, width), lambda i: (i, 0))]
        + [pl.BlockSpec((units_of(p), width), lambda i: (3, 0), pipeline_mode=pl.Buffered(1)) for p in pieces],
        out_specs=pl.BlockSpec((tile, columns), lambda i: (i, 0)),
        out_shape=jax.ShapeDtypeStruct((rows, columns), bf16),
        cost_estimate=cost(
            flops=2 * rows * width * columns, bytes_accessed=2 * (rows * width + width * columns + rows * columns), transcendentals=0
        ),
        compiler_params=pltpu.CompilerParams(vmem_limit_bytes=60 * MIB),
        name="heads_back",
    )(low, *pieces)


def project_back_kernel(groups, first, last, meta, *refs):
    refs = list(refs)
    take = lambda n: [refs.pop(0) for _ in range(n)]
    dq, dkv, dkv_got, o, a, low = take(6)
    pieces = take(len(groups))
    so_far = None if first else refs.pop(0)
    if last:
        value, above, vectors = take(3)
    keep, send, bias_sums = take(3)
    outs = take(2) if last else take(1)
    lefts = refs.pop(0)
    total = refs.pop(0) if last else None
    step = pl.program_id(0)
    core = meta[0]

    @pl.when(step == 0)
    def _():
        bias_sums[0:1] = jnp.sum(dq[...].astype(f32), axis=0, keepdims=True)
        for n in range(2):
            value_n = dkv[n].astype(f32) + dkv_got[n].astype(f32)
            lefts[n] = value_n.astype(bf16)
            if n == 1:
                bias_sums[1:2] = jnp.sum(value_n, axis=0, keepdims=True)

    sides = (dq, lefts.at[0], lefts.at[1], o)
    term = None
    for c in range(4):
        value_c = dot_tn(sides[c][...], (low if c == 3 else a)[...]).astype(bf16)
        keep_at = send_at = at = 0
        for name, size in groups:
            if name == "own":
                half = size // 2
                one, two = value_c[at : at + half], value_c[at + half : at + size]
                keep[c, keep_at : keep_at + half] = jnp.where(core == 0, one, two)
                send[c, send_at : send_at + half] = jnp.where(core == 0, two, one)
                keep_at, send_at = keep_at + half, send_at + half
            elif name in ("near", "far"):
                keep[c, keep_at : keep_at + size] = value_c[at : at + size]
                keep_at += size
            else:
                send[c, send_at : send_at + size] = value_c[at : at + size]
                send_at += size
            at += size
        if c < 3:
            part = dot_nn(sides[c][...], joined(pieces, 3, c))
            term = part if term is None else term + part
    if not first:
        term = term + so_far[...]
    if not last:
        outs[0][...] = term
        return
    tile = term.shape[1]
    total[:, pl.ds(pl.multiple_of(step * tile, tile), tile)] = term

    @pl.when(step == pl.num_programs(0) - 1)
    def _():
        norm_back_all(total, value, above, vectors[0:1], outs[0], outs[1])


def project_back(meta, names, dq, dkv, dkv_got, o, a, low, pieces, so_far, norm):
    rows, width = a.shape
    columns = dq.shape[1]
    groups = [(name, units_of(piece)) for name, piece in zip(names, pieces)]
    tiles = 2
    tile = width // tiles
    slim = pl.BlockSpec((rows, tile), lambda i, m: (0, i))
    grads = pl.BlockSpec((4, columns // 2, tile), lambda i, m: (0, 0, i))
    args = [dq, dkv, dkv_got, o, a, low, *pieces]
    specs = [fixed(dq.shape), fixed(dkv.shape), fixed(dkv.shape), fixed(o.shape), slim, slim]
    specs += [pl.BlockSpec((3 * units_of(p), tile), lambda i, m: (0, i)) for p in pieces]
    if so_far is not None:
        args.append(so_far)
        specs.append(slim)
    out_specs = [grads, grads, pl.BlockSpec((8, columns), lambda i, m: (0, 0))]
    out_shape = [jax.ShapeDtypeStruct((4, columns // 2, width), bf16)] * 2 + [jax.ShapeDtypeStruct((8, columns), f32)]
    scratch = [pltpu.VMEM((2, rows, columns), bf16)]
    if norm is None:
        out_specs.append(slim)
        out_shape.append(jax.ShapeDtypeStruct((rows, width), f32))
    else:
        value, above, gain = norm
        args += [value, above, jnp.broadcast_to(gain[None], (8, width))]
        specs += [fixed(value.shape), fixed(above.shape), fixed((8, width))]
        out_specs += [pl.BlockSpec((rows, width), lambda i, m: (0, 0)), pl.BlockSpec((8, width), lambda i, m: (0, 0))]
        out_shape += [jax.ShapeDtypeStruct((rows, width), bf16), jax.ShapeDtypeStruct((8, width), f32)]
        scratch.append(pltpu.VMEM((rows, width), f32))
    return pl.pallas_call(
        partial(project_back_kernel, groups, so_far is None, norm is not None),
        grid_spec=pltpu.PrefetchScalarGridSpec(
            num_scalar_prefetch=1, grid=(tiles,), in_specs=specs, out_specs=out_specs, scratch_shapes=scratch
        ),
        out_shape=out_shape,
        cost_estimate=cost(
            flops=14 * rows * width * columns, bytes_accessed=2 * (6 * rows * columns + 7 * width * columns + 6 * rows * width), transcendentals=0
        ),
        compiler_params=pltpu.CompilerParams(vmem_limit_bytes=60 * MIB),
        name="project_back",
    )(meta, *args)


def tie(values, *others):
    return lax.optimization_barrier((values, others))[0]


def plus(*values):
    total = values[0].astype(f32)
    for value in values[1:]:
        total = total + value.astype(f32)
    return total.astype(bf16)


def meet_kernel(meta, keep_early, keep_late, got_early, got_late, far, own, early, late):
    core = meta[0]
    size = early.shape[1]
    for half, out, kept, got in ((1 - core, early, keep_early, got_early), (core, late, keep_late, got_late)):
        total = (kept[0, 0].astype(f32) + got[0, 0].astype(f32)).astype(bf16)
        out[0] = total[:size]
        far[0, half, 0] = total[size : size + size // 2]
        own[0, half, 0] = total[size + size // 2 :]


def meet(meta, keep, got):
    matrices, steps, units, width = keep.shape
    each = steps // 2
    view = lambda late: pl.BlockSpec(
        (1, 1, units, width), lambda n, j, m: (n, (m[0] if late else 1 - m[0]) * each + j, 0, 0)
    )
    halves = pl.BlockSpec((1, 2, 1, units // 4, width), lambda n, j, m: (n, 0, j, 0, 0))
    rows = pl.BlockSpec((1, units // 2, width), lambda n, j, m: (n, j, 0))
    both_shape = jax.ShapeDtypeStruct((matrices, 2, each, units // 4, width), bf16)
    rows_shape = jax.ShapeDtypeStruct((matrices, each * units // 2, width), bf16)
    far, own, early, late = pl.pallas_call(
        meet_kernel,
        grid_spec=pltpu.PrefetchScalarGridSpec(
            num_scalar_prefetch=1,
            grid=(matrices, each),
            in_specs=[view(False), view(True)] * 2,
            out_specs=[halves, halves, rows, rows],
        ),
        out_shape=[both_shape, both_shape, rows_shape, rows_shape],
        cost_estimate=cost(flops=keep.size, bytes_accessed=6 * keep.size, transcendentals=0),
        compiler_params=pltpu.CompilerParams(vmem_limit_bytes=60 * MIB),
        name="meet",
    )(meta, keep, keep, got, got)
    flat = lambda value: value.reshape(matrices, -1, width)
    return flat(far), flat(own), early, late


def exchanged(value, axis, distance):
    count = lax.axis_size(axis)
    return lax.ppermute(value, axis, [(n, n ^ distance) for n in range(count)])


def ordered(first, mine, other):
    return jnp.where(first, jnp.concatenate([mine, other], axis=1), jnp.concatenate([other, mine], axis=1))


class Send:
    def __init__(self, transfer, value):
        self.transfer, self.value = transfer, value


def hopping(value, pairs):
    return Send(lambda v: hop(v, pairs), value)


def swapping(value):
    return Send(swap, value)


def exchanging(value, axis, distance):
    return Send(lambda v: exchanged(v, axis, distance), value)


class Chain:
    def __init__(self, steps):
        self.steps, self.result, self.done = steps, None, False
        self.advance(None)

    def advance(self, value):
        self.pending, self.under_way = None, None
        try:
            self.pending, self.wait = self.steps.send(value)
        except StopIteration as stop:
            self.result, self.done = stop.value, True


def once(sends, wait):
    value = yield sends, wait
    return value


class Chains:
    def __init__(self):
        self.running = []

    def start(self, steps):
        chain = Chain(steps)
        self.running.append(chain)
        return chain

    def turn(self, values):
        self.running = [chain for chain in self.running if not chain.done]
        due = []
        for chain in self.running:
            chain.wait -= 1
            if chain.wait <= 0:
                due.append(chain)
        values, there = lax.optimization_barrier((values, [chain.under_way for chain in due]))
        for chain, value in zip(due, there):
            chain.advance(value)
        return values

    def launch(self, values):
        chains = [chain for chain in self.running if chain.pending is not None]
        sends = [chain.pending if isinstance(chain.pending, list) else [chain.pending] for chain in chains]
        values, sent = lax.optimization_barrier((values, [[send.value for send in each] for each in sends]))
        for chain, each, operands in zip(chains, sends, sent):
            under_way = [send.transfer(value) for send, value in zip(each, operands)]
            chain.under_way = under_way if isinstance(chain.pending, list) else under_way[0]
            chain.pending = None
        return values

    def step(self, values, *new):
        values = self.turn(values)
        started = [self.start(make()) for make in new]
        values = self.launch(values)
        return (values, *started) if new else values


def summed_feed(meta, keep, send, waits):
    waits = iter(waits)
    got = yield swapping(send), next(waits)
    far, own, early, late = meet(meta, keep, got)
    relayed, early = yield [hopping(far, SECOND_HOP), hopping(early, FIRST_HOP)], next(waits)
    late, back = yield [hopping(plus(late, relayed), FIRST_HOP), swapping(early)], next(waits)
    return (yield from summed_over_line(plus(own, late, back), waits))


def summed_far(keep, send, waits):
    waits = iter(waits)
    got = yield swapping(send), next(waits)
    return (yield hopping(plus(keep, got), LAST_HOP), next(waits))


def summed_near(keep, send, core, waits):
    waits = iter(waits)
    got = yield swapping(send), next(waits)
    near = yield hopping(plus(keep, got), FIRST_HOP), next(waits)
    back = yield swapping(half_of(near, 1, 1 - core)), next(waits)
    return half_of(near, 1, core), back


def summed_over_line(total, waits):
    if lax.axis_size("dp") != 4:
        return lax.psum(total, "dp")
    line = lax.axis_index("dp")
    low, high = line & 1, line >> 1
    got = yield exchanging(half_of(total, 1, 1 - low), "dp", 1), next(waits)
    total = plus(half_of(total, 1, low), got)
    got = yield exchanging(half_of(total, 1, 1 - high), "dp", 2), next(waits)
    total = plus(half_of(total, 1, high), got)
    got = yield exchanging(total, "dp", 2), next(waits)
    total = ordered(high == 0, total, got)
    got = yield exchanging(total, "dp", 1), next(waits)
    return ordered(low == 0, total, got)


def summed_everywhere(value):
    for axis in ("section", "tensor", "dp"):
        count = lax.axis_size(axis)
        if count & (count - 1):
            value = lax.psum(value, axis)
            continue
        distance = 1
        while distance < count:
            got = yield exchanging(value, axis, distance), 1
            value = value + got
            distance *= 2
    return value


def in_order(own, near, near_too, far, far_too, core, chip):
    first = core == 0
    last = jnp.concatenate([jnp.where(first, far, far_too), jnp.where(first, far_too, far)], axis=-1)
    by_distance = jnp.stack([own, jnp.where(first, near, near_too), jnp.where(first, near_too, near), last])
    rows = [lax.dynamic_index_in_dim(by_distance, quarter ^ chip, 0, keepdims=False) for quarter in CHIPS]
    return jnp.concatenate(rows, axis=-1)


PIECES = ("own", "near", "near_too", "far", "far_too")
GROUPS = (("own",), ("near", "near_too"), ("far", "far_too"))
OWN, NEAR, FAR = range(3)


def on_row(
    ends_in, lengths, ln_gains, ln_biases, w_qkv, qv_bias, w_out, w_up, up_bias, w_down, out_biases
):
    core = lax.axis_index("section")
    chip = lax.axis_index("tensor")
    first_core = core == 0
    micro, rows_here, seg = ends_in.shape[1:4]
    ends = ends_in.reshape(micro * rows_here, seg, D)
    lo_segment, hi_segment = core, 3 - core
    n_qv = qv_bias.shape[-1]
    n_up = up_bias.shape[-1]

    def row_from(section):
        return [
            hopping(
                lax.dynamic_index_in_dim(ends, chip ^ k, 0, keepdims=False),
                [(place(section, t), place(core_of(t), t ^ k)) for t in CHIPS],
            )
            for k in CHIPS
        ]

    def chosen_rows(got):
        def pick(k):
            return jnp.where(k == 0, got[0], jnp.where(k == 1, got[1], jnp.where(k == 2, got[2], got[3])))

        return jnp.concatenate([pick(chip ^ lo_segment), pick(chip ^ hi_segment)])

    def row_to(section, row, distances):
        got = []
        for k in distances:
            segment = chip ^ k
            sent = jnp.where(segment == lo_segment, row[:seg], row[seg:])
            got.append(hopping(sent, [(place(core_of(t), t ^ k), place(section, t)) for t in CHIPS]))
        return got

    def both(mine):
        theirs = swap(mine)
        return (jnp.where(first_core, mine, theirs), jnp.where(first_core, theirs, mine))

    chains = Chains()
    six = both(jnp.concatenate([ln_gains[0], ln_biases[0], out_biases[0]]))
    bias = jnp.concatenate([qv_bias[0].reshape(-1), up_bias[0]])
    bias = jnp.stack(three_parts(bias))
    bias = jnp.pad(bias, ((0, 0), (0, -bias.shape[1] % D))).reshape(-1, D)
    bias = jnp.pad(bias, ((0, BIAS_ROWS - bias.shape[0]), (0, 0)))
    pack = jnp.concatenate([jnp.swapaxes(w_qkv[0], 1, 2).reshape(-1, D), w_out[0], bias])
    x = chosen_rows([send.transfer(send.value) for send in row_from(0)])
    attention_own = both(pack)
    feed_own = both(jnp.concatenate([w_up[0].T[None], w_down]))

    def gathered_heads(own, pieces, waits):
        pieces["own"] = own
        near = yield hopping(own, FIRST_HOP), waits[0]
        pieces["near"], pieces["near_too"] = near, swap(near)
        heads = half_of(near[: 4 * n_qv].reshape(4, n_qv, D), 1, core).reshape(-1, D)
        far = yield hopping(jnp.concatenate([heads, near[4 * n_qv :]]), SECOND_HOP), waits[1]
        pieces["far"], pieces["far_too"] = far, swap(far)

    def gathered_feed(own, pieces, waits):
        near = yield hopping(own, FIRST_HOP), waits[0]
        pieces += [own.reshape(2, 2, -1, D), near, swap(near)]
        far = yield hopping(half_of(near, 1, core), SECOND_HOP), waits[1]
        pieces += [far, swap(far)]

    attention, feeding = ({}, {}), ([], [])
    x, attention_own = tie((x, attention_own))

    def bias_of(name, layer, start, size):
        rows = attention[layer][name][-BIAS_ROWS:].astype(f32)
        count = -(-(2 * n_qv + n_up) // D)
        parts = rows[: 3 * count].reshape(3, -1)
        part = ((parts[0] + parts[1]) + parts[2])[start : start + size]
        if name == "far":
            part = half_of(part, 0, core)
        if name == "far_too":
            part = half_of(part, 0, 1 - core)
        return part

    gains, shifts, end_biases = ([layer_six[n : n + 2] for layer_six in six] for n in (0, 2, 4))

    length = lax.dynamic_index_in_dim(lengths.reshape(-1), chip, 0, keepdims=False)
    segments = jnp.stack([lo_segment, hi_segment, 1 - core, 2 + core])
    positions = (segments[:, None] * seg + jnp.arange(seg)[None]).reshape(-1)
    kcol = key_columns(positions, length)
    heads_here = n_qv // HEAD
    quarters = {"own": chip, "near": chip ^ (1 + core), "near_too": chip ^ (2 - core), "far": chip ^ 3, "far_too": chip ^ 3}
    pairs_of = {name: n_qv // 128 // (2 if name.startswith("far") else 1) for name in PIECES}
    across = {"own": "own", "near": "near_too", "near_too": "near", "far": "far_too", "far_too": "far"}

    def head_slopes(name):
        head = quarters[name] * heads_here + jnp.arange(heads_here)
        if name == "far":
            head = half_of(head, 0, core)
        if name == "far_too":
            head = half_of(head, 0, 1 - core)
        return jnp.exp2(-8.0 * (head + 1).astype(f32) / HEADS)

    slopes = {name: head_slopes(name) for name in PIECES}

    def group_meta(names):
        starts, at = {}, 0
        for name in names:
            starts[name] = at
            at += pairs_of[name]
        table = [starts[across[name]] + n for name in names for n in range(pairs_of[name])]
        return jnp.concatenate([core[None].astype(jnp.int32), jnp.array(table, jnp.int32)])

    groups = [
        [
            dict(names=names, meta=group_meta(names), qcol=query_columns(jnp.concatenate([slopes[name] for name in names])))
            for names in GROUPS
        ]
        for layer in range(2)
    ]

    def pieces_of(layer, index):
        return [attention[layer][name] for name in groups[layer][index]["names"]]

    def heads_bias(layer, index):
        names = groups[layer][index]["names"]
        return jnp.stack(
            [
                jnp.concatenate([bias_of(name, layer, 0, n_qv) for name in names]),
                jnp.zeros((sum(pairs_of[name] for name in names) * 128,), f32),
                jnp.concatenate([bias_of(name, layer, n_qv, n_qv) for name in names]),
            ]
        )[:, None]

    meta = core[None].astype(jnp.int32)

    def into_heads(layer, index, normed):
        q, kv = project_heads(normed, pieces_of(layer, index), heads_bias(layer, index))
        return q, kv, swap(kv)

    def attended(layer, index, projected):
        group = groups[layer][index]
        return tuple(projected) + tuple(attend(group["meta"], *projected, kcol, group["qcol"]))

    def fed(layer, x, saved):
        vectors = eight_rows(end_biases[layer][0], gains[layer][1], shifts[layer][1], end_biases[layer][1])
        pieces = [p for index in range(len(saved)) for p in pieces_of(layer, index)]
        bias = [bias_of("own", layer, 2 * n_qv, n_up)]
        bias = [half_of(bias[0], 0, core), half_of(bias[0], 0, 1 - core)]
        bias += [bias_of(name, layer, 2 * n_qv, n_up) for name in ("near", "near_too")]
        bias = jnp.concatenate([part.reshape(STEPS, -1) for part in bias], axis=1)[:, None]
        return feed(meta, x, [v[3] for v in saved], pieces, vectors, bias, feeding[layer])

    def fed_last(layer, middle, total):
        following = min(layer + 1, 1)
        vectors = eight_rows(jnp.zeros((D,), f32), gains[following][0], shifts[following][0])
        bias = [bias_of(name, layer, 2 * n_qv, n_up).reshape(STEPS, -1) for name in ("far", "far_too")]
        return feed_last(middle, total, vectors, jnp.concatenate(bias, axis=1).reshape(1, -1), feeding[layer])

    kept = [None, None]
    chains.start(gathered_heads(attention_own[0], attention[0], (1, 1)))
    x = chains.launch(x)
    normed = first_norm(x, eight_rows(jnp.zeros((D,), f32), gains[0][0], shifts[0][0]))
    for layer in range(2):
        saved = [None] * 3
        saved[OWN] = attended(layer, OWN, into_heads(layer, OWN, normed))
        (normed, saved[OWN], feed_own), _ = chains.step(
            (normed, saved[OWN], feed_own), lambda: gathered_feed(feed_own[layer], feeding[layer], (2, 1))
        )
        saved[NEAR] = attended(layer, NEAR, into_heads(layer, NEAR, normed))
        normed, saved[NEAR] = chains.step((normed, saved[NEAR]))
        saved[FAR] = attended(layer, FAR, into_heads(layer, FAR, normed))
        saved = chains.step(saved)
        slope, hidden, after, middle, total = fed(layer, x, saved)
        (total, attention_own, ends), following = chains.step(
            (total, attention_own, ends),
            lambda: once(row_from(1), 1) if layer else gathered_heads(attention_own[1], attention[1], (2, 1)),
        )
        slope_last, hidden_last, result, normed_next = fed_last(layer, middle, total)
        kept[layer] = (x, normed, saved, after, middle, (slope, slope_last), (hidden, hidden_last))
        if layer == 0:
            x, normed = chains.step((result, normed_next))
    x, *sent_back = chains.step(result, lambda: once(row_to(1, result, (0, 1)), 1))
    grad = chosen_rows(following.result)

    def heads_gradients(layer, index, low):
        group = groups[layer][index]
        q, kv, kvo, o, qx = kept[layer][2][index]
        return attend_back(group["meta"], q, kv, kvo, kcol, qx, heads_back(low, pieces_of(layer, index)), o)

    def weight_gradients(layer, index, grads, low, so_far, last):
        group = groups[layer][index]
        norm = (kept[layer][0], low, gains[layer][0]) if last else None
        return project_back(
            meta, group["names"], *grads, kept[layer][2][index][3], kept[layer][1], low, pieces_of(layer, index), so_far, norm
        )

    def sums_of(layer, results, unit_sums, sums_one, sums_two):
        parts = {}
        for index, group in enumerate(groups[layer]):
            at = 0
            for name in group["names"]:
                size = pairs_of[name] * 128
                parts[name] = results[index][2][0:2, at : at + size]
                at += size
        unit_sums = unit_sums[:, 0]
        part = unit_sums.shape[1] // 8

        def unit_part(start, count):
            return unit_sums[:, start * part : (start + count) * part].reshape(-1)

        own_keep, own_send = unit_part(0, 1), unit_part(1, 1)
        own = jnp.concatenate([jnp.where(first_core, own_keep, own_send), jnp.where(first_core, own_send, own_keep)])
        return jnp.concatenate(
            [
                jnp.stack([sums_one[0], sums_two[0], sums_one[1], sums_two[1], sums_two[2], sums_two[3]]),
                in_order(*[parts[name] for name in PIECES], core, chip),
                in_order(own, unit_part(2, 2), unit_part(4, 2), unit_part(6, 1), unit_part(7, 1), core, chip).reshape(-1, D),
            ]
        )

    def feed_gradients(layer, grad):
        _, _, _, after, middle, slope, hidden = kept[layer]
        return feed_back(meta, grad, middle, after, gains[layer][1], slope, hidden, feeding[layer])

    def backward(layer, grad, others, *new):
        keep, send, unit_sums, low, sums_two = feed_gradients(layer, grad)
        (low, keep, send, others), feed_sums, *started = chains.step(
            (low, keep, send, others),
            lambda: summed_feed(meta, keep, send, (1, 2, 2, 2, 1, 1, 1)),
            *(lambda make=make: make(others) for make in new),
        )
        results = [None] * 3
        dq_far, dkv_far, sent_far = heads_gradients(layer, FAR, low)
        (low, sent_far), got_far = chains.step((low, sent_far), lambda: once(swapping(sent_far), 1))
        dq_near, dkv_near, sent_near = heads_gradients(layer, NEAR, low)
        (low, sent_near), got_near = chains.step((low, sent_near), lambda: once(swapping(sent_near), 1))
        results[FAR] = weight_gradients(layer, FAR, (dq_far, dkv_far, got_far.result), low, None, False)
        (low, results[FAR]), far_sum = chains.step((low, results[FAR]), lambda: summed_far(*results[FAR][:2], (1, 1)))
        results[NEAR] = weight_gradients(layer, NEAR, (dq_near, dkv_near, got_near.result), low, results[FAR][3], False)
        (low, results[NEAR]), near_sum = chains.step(
            (low, results[NEAR]), lambda: summed_near(*results[NEAR][:2], core, (1, 2, 1))
        )
        dq_own, dkv_own, sent_own = heads_gradients(layer, OWN, low)
        (low, sent_own), got_own = chains.step((low, sent_own), lambda: once(swapping(sent_own), 1))
        low, dq_own, dkv_own = chains.step((low, dq_own, dkv_own))
        results[OWN] = weight_gradients(layer, OWN, (dq_own, dkv_own, got_own.result), low, results[NEAR][3], True)
        grad, sums_one = results[OWN][3:]
        sums = sums_of(layer, results, unit_sums, sums_one, sums_two)
        return grad, results[OWN], sums, feed_sums, near_sum, far_sum, started

    grad, own, sums_upper, upper_feed, near_sum, far_sum, again = backward(
        1, grad, x, lambda row: once(row_to(1, row, (2, 3)), 1)
    )
    sent_back += again
    (grad, own), own_sum = chains.step((grad, own), lambda: once(swapping(own[1]), 1))

    def summed_heads(_, keep=own[0], own_sum=own_sum, near_sum=near_sum, far_sum=far_sum):
        return summed_over_line(plus(keep, own_sum.result, *near_sum.result, far_sum.result), iter((1, 1, 1, 1)))

    grad, own, sums_lower, lower_feed, near_sum, far_sum, (upper_heads,) = backward(0, grad, (), summed_heads)
    (grad, sums_lower, own), first_one, own_sum, both_sums = chains.step(
        (grad, sums_lower, own),
        lambda: once(row_to(0, grad, (0, 1)), 1),
        lambda: once(swapping(own[1]), 1),
        lambda: summed_everywhere(jnp.stack([sums_lower, sums_upper])),
    )
    grad, first_two, lower_heads = chains.step(
        grad,
        lambda: once(row_to(0, grad, (2, 3)), 2),
        lambda: summed_over_line(plus(own[0], own_sum.result, *near_sum.result, far_sum.result), iter((1, 1, 1, 1))),
    )
    first_rows = [first_one, first_two]

    def rows_of(got):
        return [
            jnp.where(
                row == chip, got[0], jnp.where(row == chip ^ 1, got[1], jnp.where(row == chip ^ 2, got[2], got[3]))
            )
            for row in CHIPS
        ]

    def finished(lower, upper):
        to_upper = lax.ppermute(upper, "section", [(0, 1)])
        to_lower = lax.ppermute(lower, "section", [(1, 0)])
        return jnp.where(
            first_core,
            jnp.concatenate([lower, to_lower], axis=1),
            jnp.concatenate([to_upper, upper], axis=1),
        ).astype(f32)

    def feed_outputs():
        grads = finished(lower_feed.result, upper_feed.result)
        return grads[0].T[None], grads[1:]

    def ends_outputs():
        first, second = ([*chains_of[0].result, *chains_of[1].result] for chains_of in (first_rows, sent_back))
        ends = jnp.stack([jnp.where(first_core, a, b) for a, b in zip(rows_of(first), rows_of(second))])
        return ends.astype(f32).reshape(1, micro, rows_here, seg, D)

    ready, waiting = {}, {"ends": (ends_outputs, first_rows), "feed": (feed_outputs, [lower_feed, upper_feed])}
    while any(not chain.done for chain in chains.running):
        ready = chains.step(ready)
        for name in list(waiting):
            make, needed = waiting[name]
            if all(chain.done for chain in needed):
                ready[name] = make()
                del waiting[name]
    for name, (make, _) in waiting.items():
        ready[name] = make()
    ends_out, (grad_up, grad_down) = ready["ends"], ready["feed"]
    attention_grads = finished(lower_heads.result, upper_heads.result)
    both_sums = both_sums.result
    sums = jnp.where(first_core, both_sums[0], both_sums[1])
    grad_qv = lax.dynamic_slice_in_dim(sums[6:8], chip * n_qv, n_qv, 1)[None]
    grad_up_bias = lax.dynamic_slice_in_dim(sums[8:].reshape(-1), chip * n_up, n_up, 0)[None]
    return (
        ends_out,
        sums[0:2][None],
        sums[2:4][None],
        jnp.swapaxes(attention_grads[:3], 1, 2)[None],
        grad_qv,
        attention_grads[3:],
        grad_up,
        grad_up_bias,
        grad_down,
        sums[4:6][None],
    )


def solution(mesh):
    return jax.shard_map(
        on_row if one_row_a_chip(mesh) else on_device,
        mesh=mesh,
        in_specs=(
            P("section", None, "dp", "tensor", None),
            P(None, "dp"),
            P("section", None, None),
            P("section", None, None),
            P("section", None, None, "tensor"),
            P("section", None, "tensor"),
            P("section", "tensor", None),
            P("section", None, "tensor"),
            P("section", "tensor"),
            P("section", "tensor", None),
            P("section", None, None),
        ),
        out_specs=(
            P("section", None, "dp", "tensor", None),
            P("section", None, None),
            P("section", None, None),
            P("section", None, None, "tensor"),
            P("section", None, "tensor"),
            P("section", "tensor", None),
            P("section", None, "tensor"),
            P("section", "tensor"),
            P("section", "tensor", None),
            P("section", None, None),
        ),
        check_vma=False,
    )
```

```python
from functools import partial

import jax
import jax.numpy as jnp
from jax import lax
from jax.experimental import pallas as pl
from jax.experimental.pallas import tpu as pltpu
from jax.sharding import PartitionSpec as P

D = 1024
HEADS = 16


eps = 1e-05
widest = 512


def shifted(shard, axis, by):
    devices = lax.axis_size(axis)
    pairs = [(i, i + by) for i in range(devices) if 0 <= i + by < devices]
    return lax.ppermute(shard, axis, pairs)


def layer_norm(inputs, gain, bias):
    center = jnp.mean(inputs, axis=-1, keepdims=True)
    centred = inputs - center
    spread = jnp.mean(centred * centred, axis=-1, keepdims=True)
    factor = lax.rsqrt(spread + eps)
    normal = centred * factor
    return (normal * gain + bias, normal, factor)


def norm_back(grad_norm, normal, factor, gain):
    scaled = grad_norm * gain
    first_mean = jnp.mean(scaled, axis=-1, keepdims=True)
    second_mean = jnp.mean(scaled * normal, axis=-1, keepdims=True)
    return factor * (scaled - first_mean - normal * second_mean)


def gather_tokens(values):
    return lax.all_gather(values, "tensor", axis=1, tiled=True)


def scatter_tokens(values):
    return lax.psum_scatter(values, "tensor", scatter_dimension=1, tiled=True)


def gather_grads(values):
    return lax.all_gather(values, "tensor", axis=1, tiled=True)


def scatter_grads(values):
    return lax.psum_scatter(
        values.astype(jnp.bfloat16), "tensor", scatter_dimension=1, tiled=True
    ).astype(jnp.float32)


def project(whole_rows, w_proj, proj_bias):
    combined = jnp.einsum("rld,cde->crle", whole_rows, w_proj, preferred_element_type=jnp.float32)
    queries = (combined[0] + proj_bias[0]).astype(jnp.bfloat16)
    key_rows = combined[1].astype(jnp.bfloat16)
    value_rows = (combined[2] + proj_bias[1]).astype(jnp.bfloat16)
    return (queries, key_rows, value_rows)


def score_block(query_block, key_heads, row_start, row_lengths, slopes_here):
    block_rows = query_block.shape[1]
    seq_len = key_heads.shape[1]
    head_size = key_heads.shape[-1]
    scores = jnp.einsum(
        "rqhd,rkhd->rhqk", query_block, key_heads, preferred_element_type=jnp.float32
    ) * head_size ** (-0.5)
    rowpos = row_start + jnp.arange(block_rows)
    keypos = jnp.arange(seq_len)
    distance = (rowpos[:, None] - keypos[None, :]).astype(jnp.float32)
    scores = scores - slopes_here[None, :, None, None] * distance[None, None]
    causal = keypos[None, :] <= rowpos[:, None]
    inside = keypos[None, :] < row_lengths[:, None]
    allowed = causal[None, None] & inside[:, None, None, :]
    return jnp.where(allowed, scores, -1e30)


def attention(queries, key_rows, value_rows, row_lengths, slopes_here):
    row_count, seq_len, width = queries.shape
    head_count = slopes_here.shape[0]
    head_size = width // head_count
    block_rows = min(widest, seq_len)
    query_heads = queries.reshape(row_count, seq_len, head_count, head_size)
    key_heads = key_rows.reshape(row_count, seq_len, head_count, head_size)
    value_heads = value_rows.reshape(row_count, seq_len, head_count, head_size)

    def one_block(row_start):
        query_block = lax.dynamic_slice_in_dim(query_heads, row_start, block_rows, 1)
        scores = score_block(query_block, key_heads, row_start, row_lengths, slopes_here)
        row_max = jnp.max(scores, axis=-1, keepdims=True)
        powers = jnp.exp(scores - row_max)
        row_total = jnp.sum(powers, axis=-1, keepdims=True)
        probs = (powers / row_total).astype(jnp.bfloat16)
        block_out = jnp.einsum(
            "rhqk,rkhd->rqhd", probs, value_heads, preferred_element_type=jnp.float32
        )
        return (block_out.astype(jnp.bfloat16), (row_max + jnp.log(row_total))[..., 0])

    starts = jnp.arange(seq_len // block_rows) * block_rows
    blocks_out, log_totals = lax.map(one_block, starts)
    attended = jnp.moveaxis(blocks_out, 0, 1).reshape(row_count, seq_len, width)
    log_totals = jnp.moveaxis(log_totals, 0, 2).reshape(row_count, head_count, seq_len)
    return (attended, log_totals)


def attention_back(
    queries, key_rows, value_rows, grad_attended, log_totals, row_lengths, slopes_here
):
    row_count, seq_len, width = queries.shape
    head_count = slopes_here.shape[0]
    head_size = width // head_count
    scale = head_size ** (-0.5)
    block_rows = min(widest, seq_len)
    query_heads = queries.reshape(row_count, seq_len, head_count, head_size)
    key_heads = key_rows.reshape(row_count, seq_len, head_count, head_size)
    value_heads = value_rows.reshape(row_count, seq_len, head_count, head_size)
    grad_heads = grad_attended.reshape(row_count, seq_len, head_count, head_size)

    def one_block(carry, row_start):
        grad_keys, grad_values = carry
        query_block = lax.dynamic_slice_in_dim(query_heads, row_start, block_rows, 1)
        grad_block = lax.dynamic_slice_in_dim(grad_heads, row_start, block_rows, 1)
        scores = score_block(query_block, key_heads, row_start, row_lengths, slopes_here)
        block_logs = lax.dynamic_slice_in_dim(log_totals, row_start, block_rows, 2)
        probs = jnp.exp(scores - block_logs[..., None])
        grad_values = grad_values + jnp.einsum(
            "rhqk,rqhd->rkhd",
            probs.astype(jnp.bfloat16),
            grad_block,
            preferred_element_type=jnp.float32,
        )
        grad_probs = jnp.einsum(
            "rqhd,rkhd->rhqk", grad_block, value_heads, preferred_element_type=jnp.float32
        )
        inner = jnp.sum(probs * grad_probs, axis=-1, keepdims=True)
        grad_scores = (probs * (grad_probs - inner)).astype(jnp.bfloat16)
        grad_query = (
            jnp.einsum(
                "rhqk,rkhd->rqhd", grad_scores, key_heads, preferred_element_type=jnp.float32
            )
            * scale
        )
        grad_keys = (
            grad_keys
            + jnp.einsum(
                "rhqk,rqhd->rkhd", grad_scores, query_block, preferred_element_type=jnp.float32
            )
            * scale
        )
        return ((grad_keys, grad_values), grad_query.astype(jnp.bfloat16))

    zeros_heads = jnp.zeros((row_count, seq_len, head_count, head_size), jnp.float32)
    starts = jnp.arange(seq_len // block_rows) * block_rows
    (grad_keys, grad_values), grad_queries = lax.scan(one_block, (zeros_heads, zeros_heads), starts)
    grad_queries = jnp.moveaxis(grad_queries, 0, 1).reshape(row_count, seq_len, width)
    grad_keys = grad_keys.reshape(row_count, seq_len, width).astype(jnp.bfloat16)
    grad_values = grad_values.reshape(row_count, seq_len, width).astype(jnp.bfloat16)
    return (grad_queries, grad_keys, grad_values)


def layer_forward(inputs, row_lengths, weights, slopes_here):
    gains, biases, w_proj, proj_bias, w_attn, w_first, first_bias, w_second, end_biases = weights
    normed, _, _ = layer_norm(inputs, gains[0], biases[0])
    whole_rows = gather_tokens(normed.astype(jnp.bfloat16))
    queries, key_rows, value_rows = project(whole_rows, w_proj, proj_bias)
    attended, log_totals = attention(queries, key_rows, value_rows, row_lengths, slopes_here)
    attn_part = jnp.dot(attended, w_attn, preferred_element_type=jnp.float32)
    after_attn = inputs + scatter_tokens(attn_part) + end_biases[0]
    middle, _, _ = layer_norm(after_attn, gains[1], biases[1])
    middle_rows = gather_tokens(middle.astype(jnp.bfloat16))
    pre_act = jnp.dot(middle_rows, w_first, preferred_element_type=jnp.float32) + first_bias
    hidden = jax.nn.gelu(pre_act, approximate=True).astype(jnp.bfloat16)
    ffn_part = jnp.dot(hidden, w_second, preferred_element_type=jnp.float32)
    result = after_attn + scatter_tokens(ffn_part) + end_biases[1]
    return (result, after_attn, attended, log_totals, whole_rows, middle_rows)


def layer_backward(grad_result, stored, row_lengths, weights, slopes_here):
    gains, biases, w_proj, proj_bias, w_attn, w_first, first_bias, w_second, end_biases = weights
    inputs = stored[0].astype(jnp.float32)
    after_attn = stored[1]
    attended = stored[2]
    log_totals = stored[3]
    normed, normal_one, factor_one = layer_norm(inputs, gains[0], biases[0])
    middle, normal_two, factor_two = layer_norm(after_attn, gains[1], biases[1])
    whole_rows = gather_tokens(normed.astype(jnp.bfloat16))
    middle_rows = gather_tokens(middle.astype(jnp.bfloat16))
    pre_act = jnp.dot(middle_rows, w_first, preferred_element_type=jnp.float32) + first_bias
    hidden, gelu_pull = jax.vjp(partial(jax.nn.gelu, approximate=True), pre_act)
    hidden = hidden.astype(jnp.bfloat16)
    grad_end_two = jnp.sum(grad_result, axis=(0, 1))
    grad_branch = gather_grads(grad_result.astype(jnp.bfloat16))
    grad_second = jnp.einsum("rlf,rld->fd", hidden, grad_branch, preferred_element_type=jnp.float32)
    grad_hidden = jnp.einsum(
        "rld,fd->rlf", grad_branch, w_second, preferred_element_type=jnp.float32
    )
    grad_pre = gelu_pull(grad_hidden)[0].astype(jnp.bfloat16)
    grad_first_bias = jnp.sum(grad_pre, axis=(0, 1), dtype=jnp.float32)
    grad_first = jnp.einsum(
        "rld,rlf->df", middle_rows, grad_pre, preferred_element_type=jnp.float32
    )
    grad_middle = scatter_grads(
        jnp.einsum("rlf,df->rld", grad_pre, w_first, preferred_element_type=jnp.float32)
    )
    grad_gain_two = jnp.sum(grad_middle * normal_two, axis=(0, 1))
    grad_bias_two = jnp.sum(grad_middle, axis=(0, 1))
    grad_after = grad_result + norm_back(grad_middle, normal_two, factor_two, gains[1])
    grad_end_one = jnp.sum(grad_after, axis=(0, 1))
    grad_attn_rows = gather_grads(grad_after.astype(jnp.bfloat16))
    grad_attn = jnp.einsum(
        "rle,rld->ed", attended, grad_attn_rows, preferred_element_type=jnp.float32
    )
    grad_attended = jnp.einsum(
        "rld,ed->rle", grad_attn_rows, w_attn, preferred_element_type=jnp.float32
    ).astype(jnp.bfloat16)
    queries, key_rows, value_rows = project(whole_rows, w_proj, proj_bias)
    grad_queries, grad_keys, grad_values = attention_back(
        queries, key_rows, value_rows, grad_attended, log_totals, row_lengths, slopes_here
    )
    stacked = jnp.stack([grad_queries, grad_keys, grad_values])
    grad_proj = jnp.einsum("rld,crle->cde", whole_rows, stacked, preferred_element_type=jnp.float32)
    grad_proj_bias = jnp.stack(
        [
            jnp.sum(grad_queries, axis=(0, 1), dtype=jnp.float32),
            jnp.sum(grad_values, axis=(0, 1), dtype=jnp.float32),
        ]
    )
    grad_normed = scatter_grads(
        jnp.einsum("crle,cde->rld", stacked, w_proj, preferred_element_type=jnp.float32)
    )
    grad_gain_one = jnp.sum(grad_normed * normal_one, axis=(0, 1))
    grad_bias_one = jnp.sum(grad_normed, axis=(0, 1))
    grad_inputs = grad_after + norm_back(grad_normed, normal_one, factor_one, gains[0])
    sharded = (grad_proj, grad_proj_bias, grad_attn, grad_first, grad_first_bias, grad_second)
    shared = (
        jnp.stack([grad_gain_one, grad_gain_two]),
        jnp.stack([grad_bias_one, grad_bias_two]),
        jnp.stack([grad_end_one, grad_end_two]),
    )
    return (grad_inputs, sharded, shared)


def on_device(
    ends_in, lengths, ln_gains, ln_biases, w_qkv, qv_bias, w_out, w_up, up_bias, w_down, out_biases
):
    section_index = lax.axis_index("section")
    weights = tuple(
        (
            stored[0]
            for stored in (
                ln_gains,
                ln_biases,
                w_qkv,
                qv_bias,
                w_out,
                w_up,
                up_bias,
                w_down,
                out_biases,
            )
        )
    )
    local_ends = ends_in[0]
    micro_count = local_ends.shape[0]
    heads_here = w_qkv.shape[-1] // (D // HEADS)
    first_head = lax.axis_index("tensor") * heads_here
    slopes_here = jnp.exp2(
        -8.0 * (first_head + jnp.arange(heads_here) + 1).astype(jnp.float32) / HEADS
    )
    padded = jnp.concatenate([local_ends, jnp.zeros_like(local_ends[:1])], axis=0)
    tick_list = jnp.arange(micro_count + 1)

    def forward_tick(received, item):
        arriving, tick_index = item
        entering = jnp.where(section_index == 0, arriving, received)
        slot_index = jnp.clip(tick_index - section_index, 0, micro_count - 1)
        row_lengths = lax.dynamic_index_in_dim(lengths, slot_index, 0, keepdims=False)
        result, after_attn, attended, log_totals, whole_rows, middle_rows = layer_forward(
            entering.astype(jnp.float32), row_lengths, weights, slopes_here
        )
        outgoing = shifted(result.astype(jnp.bfloat16), "section", 1)
        stored = (entering, after_attn, attended, log_totals)
        return (outgoing, (result, stored))

    _, (results, kept_all) = lax.scan(
        forward_tick, jnp.zeros_like(local_ends[0]), (padded, tick_list)
    )
    sharded_zero = (
        jnp.zeros(w_qkv.shape[1:], jnp.float32),
        jnp.zeros(qv_bias.shape[1:], jnp.float32),
        jnp.zeros(w_out.shape[1:], jnp.float32),
        jnp.zeros(w_up.shape[1:], jnp.float32),
        jnp.zeros(up_bias.shape[1:], jnp.float32),
        jnp.zeros(w_down.shape[1:], jnp.float32),
    )
    shared_zero = (
        jnp.zeros(ln_gains.shape[1:], jnp.float32),
        jnp.zeros(ln_biases.shape[1:], jnp.float32),
        jnp.zeros(out_biases.shape[1:], jnp.float32),
    )

    def backward_tick(carry, item):
        received, sharded_total, shared_total = carry
        arriving, tick_index = item
        grad_result = jnp.where(section_index == 1, arriving, received).astype(jnp.float32)
        slot_index = tick_index - 1 + section_index
        is_valid = ((slot_index >= 0) & (slot_index < micro_count)).astype(jnp.float32)
        slot_index = jnp.clip(slot_index, 0, micro_count - 1)
        stored = tuple(
            (
                lax.dynamic_index_in_dim(kept, slot_index + section_index, 0, keepdims=False)
                for kept in kept_all
            )
        )
        row_lengths = lax.dynamic_index_in_dim(lengths, slot_index, 0, keepdims=False)
        grad_inputs, sharded, shared = layer_backward(
            grad_result, stored, row_lengths, weights, slopes_here
        )
        outgoing = shifted(grad_inputs.astype(jnp.bfloat16), "section", -1)
        sharded = tuple((value * is_valid for value in sharded))
        shared = tuple((value * is_valid for value in shared))
        sharded_total = tuple((left + right for left, right in zip(sharded_total, sharded)))
        shared_total = tuple((left + right for left, right in zip(shared_total, shared)))
        return ((outgoing, sharded_total, shared_total), grad_inputs)

    start_carry = (jnp.zeros_like(local_ends[0]), sharded_zero, shared_zero)
    (_, sharded_total, shared_total), grads_in = lax.scan(
        backward_tick, start_carry, (padded, tick_list)
    )
    sharded_total = (
        lax.psum(sharded_total[0].astype(jnp.bfloat16), "dp").astype(jnp.float32),
        lax.psum(sharded_total[1].astype(jnp.bfloat16), "dp").astype(jnp.float32),
        lax.psum(sharded_total[2].astype(jnp.bfloat16), "dp").astype(jnp.float32),
        lax.psum(sharded_total[3].astype(jnp.bfloat16), "dp").astype(jnp.float32),
        lax.psum(sharded_total[4].astype(jnp.bfloat16), "dp").astype(jnp.float32),
        lax.psum(sharded_total[5].astype(jnp.bfloat16), "dp").astype(jnp.float32),
    )
    shared_total = lax.psum((shared_total[0], shared_total[1], shared_total[2]), ("dp", "tensor"))
    ends_local = jnp.where(section_index == 0, grads_in[1:], results[1:])
    return (
        ends_local[None],
        shared_total[0][None],
        shared_total[1][None],
        sharded_total[0][None],
        sharded_total[1][None],
        sharded_total[2][None],
        sharded_total[3][None],
        sharded_total[4][None],
        sharded_total[5][None],
        shared_total[2][None],
    )


bf16, f32 = jnp.bfloat16, jnp.float32
HEAD = D // HEADS
LOG2E = 1.4426950408889634
GROUP = 4
ST = ("section", "tensor")
MIB = 2**20


def one_row_a_chip(mesh):
    return mesh.shape["section"] == 2 and mesh.shape["tensor"] == GROUP


def core_of(segment):
    return (segment & 1) ^ (segment >> 1)


def place(core, chip):
    return core * GROUP + chip


CHIPS = range(GROUP)
FIRST_HOP = [(place(0, t), place(0, t ^ 1)) for t in CHIPS] + [(place(1, t), place(1, t ^ 2)) for t in CHIPS]
LAST_HOP = [(place(c, t), place(c, t ^ 3)) for c in range(2) for t in CHIPS]
SECOND_HOP = [(place(0, t), place(0, t ^ 2)) for t in CHIPS] + [(place(1, t), place(1, t ^ 1)) for t in CHIPS]


def hop(value, pairs):
    return lax.ppermute(value, ST, pairs)


def swap(value):
    return lax.ppermute(value, "section", [(0, 1), (1, 0)])


def half_of(value, axis, index):
    size = value.shape[axis] // 2
    return lax.dynamic_slice_in_dim(value, index * size, size, axis)


def dot_nn(left, right):
    return lax.dot_general(left, right, (((1,), (0,)), ((), ())), preferred_element_type=f32)


def dot_nt(left, right):
    return lax.dot_general(left, right, (((1,), (1,)), ((), ())), preferred_element_type=f32)


def dot_tn(left, right):
    return lax.dot_general(left, right, (((0,), (0,)), ((), ())), preferred_element_type=f32)


def three_parts(value):
    first = value.astype(bf16)
    rest = value - first.astype(f32)
    second = rest.astype(bf16)
    third = (rest - second.astype(f32)).astype(bf16)
    return first, second, third


def three_rounded(value):
    parts = []
    for _ in range(3):
        part = lax.reduce_precision(value, 8, 7)
        parts.append(part.astype(bf16))
        value = value - part
    return tuple(parts)


def key_columns(positions, length):
    high = (positions // 8 * 8).astype(f32)
    low = (positions % 8).astype(f32)
    mask = jnp.where(positions < length, 0.0, -1e30).astype(f32)
    one = jnp.ones_like(high)
    columns = jnp.stack([high, high, high, low, low, low, mask, one, one, one], axis=1)
    half = jnp.pad(columns, ((0, 0), (0, HEAD - 10)))
    return jnp.concatenate([half, half], axis=1).astype(bf16)


def query_columns(slopes):
    first, second, third = three_rounded(slopes * 8.0)
    one = jnp.ones_like(first)
    columns = jnp.stack([first, second, third, first, second, third, one], axis=1)
    half = jnp.pad(columns, ((0, 0), (0, HEAD - 7))).reshape(-1, 2, HEAD)
    row = jnp.concatenate([half[:, 1], half[:, 0]], axis=1).astype(f32)
    return jnp.broadcast_to(row[:, None, :], (row.shape[0], 8, 2 * HEAD))


def attend_kernel(seg, meta, q, kv, kvo, kcol, qcol, o, qx, qp, kp, vp):
    other = 1 - meta[0]
    lane = lax.broadcasted_iota(jnp.int32, (1, 128), 1)
    low = lane < 64
    base = qcol[0, 0:1, :].astype(bf16)
    scale = LOG2E / 8
    one = jnp.ones((1, 128), bf16)
    for h in range(2):
        mine = low if h == 0 else ~low
        qp[h] = jnp.where(mine, q[...], base)
        kp[h, 0 : 2 * seg] = jnp.where(mine, kv[0], kcol[0 : 2 * seg])
        kp[h, 2 * seg :] = jnp.where(mine, kvo[0], kcol[2 * seg :])
        vp[h, 0 : 2 * seg] = jnp.where(mine, kv[1], one)
        vp[h, 2 * seg :] = jnp.where(mine, kvo[1], one)

    apart, first, second = range(3)
    far = pl.multiple_of(2 * seg + other * seg, seg)
    keys_of = ([far], [0], [0, 2 * seg, seg])
    units = [(part, h) for part in (apart, first, second) for h in range(2)]

    def scores_of(part, h):
        start = pl.multiple_of(other * seg, seg) if part == apart else (part - first) * seg
        scores = [dot_nt(qp[h, pl.ds(start, seg)], kp[h, pl.ds(key, seg)]) for key in keys_of[part]]
        if part != apart:
            row = lax.broadcasted_iota(jnp.int32, (seg, seg), 0)
            column = lax.broadcasted_iota(jnp.int32, (seg, seg), 1)
            scores[-1] = jnp.where(column <= row, scores[-1], -1e30)
        return scores

    done = {}

    def weigh(part, h, scores):
        top = scores[0].max(axis=1, keepdims=True)
        for score in scores[1:]:
            top = jnp.maximum(top, score.max(axis=1, keepdims=True))
        if part != apart:
            use = other == part - first
            apart_top, apart_total = done[apart, h]
            apart_top = jnp.where(use, apart_top, -1e30)
            top = jnp.maximum(top, apart_top)
            weight = jnp.where(use, jnp.exp2((apart_top - top) * scale), 0.0)
        total = None
        for score, key in zip(scores, keys_of[part]):
            powers = jnp.exp2((score - top) * scale).astype(bf16)
            term = dot_nn(powers, vp[h, pl.ds(key, seg)])
            total = term if total is None else total + term
        done[part, h] = top, total if part == apart else total + weight * apart_total

    scores = scores_of(*units[0])
    for n, unit in enumerate(units):
        following = scores_of(*units[n + 1]) if n + 1 < len(units) else None
        weigh(*unit, scores)
        scores = following
    at = lane & 63
    for segment in range(2):
        rows = slice(segment * seg, (segment + 1) * seg)
        (top_low, total_low), (top_high, total_high) = done[first + segment, 0], done[first + segment, 1]
        number = jnp.where(low, total_low, total_high)
        sums = jnp.where(low, total_high, total_low)
        o[rows] = (number / pltpu.roll(sums, 64, 1)).astype(bf16)
        logs = jnp.where(low, top_high, top_low) + jnp.log(sums) * 8.0
        parts = three_parts(logs)
        qx[rows] = jnp.where(at == 7, -parts[0], jnp.where(at == 8, -parts[1], jnp.where(at == 9, -parts[2], base)))


def attend(meta, q, kv, kvo, kcol, qcol):
    rows, width = q.shape
    seg = rows // 2
    pairs = width // 128
    block = pl.BlockSpec((rows, 128), lambda i, m: (0, i))
    return pl.pallas_call(
        partial(attend_kernel, seg),
        grid_spec=pltpu.PrefetchScalarGridSpec(
            num_scalar_prefetch=1,
            grid=(pairs,),
            in_specs=[
                block,
                pl.BlockSpec((2, rows, 128), lambda i, m: (0, 0, i)),
                pl.BlockSpec((2, rows, 128), lambda i, m: (0, 0, m[1 + i])),
                pl.BlockSpec((2 * rows, 128), lambda i, m: (0, 0)),
                pl.BlockSpec((1, 8, 128), lambda i, m: (i, 0, 0)),
            ],
            out_specs=[block, block],
            scratch_shapes=[
                pltpu.VMEM((2, rows, 128), bf16),
                pltpu.VMEM((2, 2 * rows, 128), bf16),
                pltpu.VMEM((2, 2 * rows, 128), bf16),
            ],
        ),
        out_shape=[jax.ShapeDtypeStruct((rows, width), bf16)] * 2,
        compiler_params=pltpu.CompilerParams(vmem_limit_bytes=60 * MIB),
        cost_estimate=cost(
            flops=40 * 256 * seg * seg * pairs, bytes_accessed=rows * width * 14, transcendentals=10 * seg * seg * pairs
        ),
        name="attend",
    )(meta, q, kv, kvo, kcol, qcol)


def attend_back_kernel(
    seg, starts, meta, q, kv, kvo, kcol, qx, low_grad, o, *refs
):
    weights, (dq, dkv, dkvo, qp, kp, vp, dp, kt, qm, dm, aq, ak, av, both) = refs[: 2 * len(starts)], refs[2 * len(starts) :]
    pair = pl.program_id(0)

    @pl.when(pair % 2 == 0)
    def _():
        two = []
        for n in range(2):
            weight = weights[n][...]
            for ref, start in zip(weights[2 + n :: 2], starts[1:]):
                weight = jnp.where(pair + n < start, weight, ref[...])
            two.append(weight)
        grads = dot_nt(low_grad[...], jnp.concatenate(two, axis=0)).astype(bf16)
        both[0], both[1] = grads[:, :128], grads[:, 128:]

    do = both[pair % 2]
    other = 1 - meta[0]
    lane = lax.broadcasted_iota(jnp.int32, (1, 128), 1)
    low = lane < 64
    at = lane & 63
    scale = LOG2E / 8
    zero = jnp.zeros((1, 128), bf16)
    product = do.astype(f32) * o[...].astype(f32)
    for h in range(2):
        mine = low if h == 0 else ~low
        qp[h] = jnp.where(mine, q[...], qx[...])
        kp[h, 0 : 2 * seg] = jnp.where(mine, kv[0], kcol[0 : 2 * seg])
        kp[h, 2 * seg :] = jnp.where(mine, kvo[0], kcol[2 * seg :])
        vp[h, 0 : 2 * seg] = jnp.where(mine, kv[1], kcol[0 : 2 * seg])
        vp[h, 2 * seg :] = jnp.where(mine, kvo[1], kcol[2 * seg :])
        first, second, third = three_parts(jnp.sum(jnp.where(mine, product, 0.0), axis=1, keepdims=True))
        extra = jnp.where(at == 7, -first, jnp.where(at == 8, -second, jnp.where(at == 9, -third, zero)))
        dp[h] = jnp.where(mine, do, extra)
        qm[h] = jnp.where(mine, q[...], zero)
        dm[h] = jnp.where(mine, do, zero)
    kt[:, 0 : 2 * seg] = kv[0].T
    kt[:, 2 * seg :] = kvo[0].T
    aq[...] = jnp.zeros_like(aq)
    ak[...] = jnp.zeros_like(ak)
    av[...] = jnp.zeros_like(av)

    def block(query_start, query_count, key_start, key_count, masked):
        queries, keys = pl.ds(query_start, query_count), pl.ds(key_start, key_count)
        for h in range(2):
            probs = jnp.exp2(dot_nt(kp[h, keys], qp[h, queries]) * scale)
            if masked:
                row = lax.broadcasted_iota(jnp.int32, (key_count, query_count), 0)
                column = lax.broadcasted_iota(jnp.int32, (key_count, query_count), 1)
                probs = jnp.where(row <= column, probs, 0.0)
            grads = (probs * dot_nt(vp[h, keys], dp[h, queries])).astype(bf16)
            av[keys] += dot_nn(probs.astype(bf16), dm[h, queries])
            ak[keys] += dot_nn(grads, qm[h, queries])
            aq[h * 64 : (h + 1) * 64, queries] += dot_nn(kt[h * 64 : (h + 1) * 64, keys], grads)

    half = seg // 2
    for segment in range(2):
        start = segment * seg
        block(start, half, start, half, True)
        block(start + half, half, start, half, False)
        block(start + half, half, start + half, half, True)
    block(seg, seg, 0, seg, False)
    block(seg, seg, 2 * seg, seg, False)
    block(pl.multiple_of(other * seg, seg), seg, pl.multiple_of(2 * seg + other * seg, seg), seg, False)
    dq[...] = (aq[...] * 0.125).T.astype(bf16)
    dkv[0] = (ak[0 : 2 * seg] * 0.125).astype(bf16)
    dkvo[0] = (ak[2 * seg :] * 0.125).astype(bf16)
    dkv[1] = av[0 : 2 * seg].astype(bf16)
    dkvo[1] = av[2 * seg :].astype(bf16)


def attend_back(meta, q, kv, kvo, kcol, qx, low_grad, o, pieces):
    rows, width = q.shape
    seg = rows // 2
    pairs = width // 128
    block = pl.BlockSpec((rows, 128), lambda i, m: (0, i))
    mine = pl.BlockSpec((2, rows, 128), lambda i, m: (0, 0, i))
    theirs = pl.BlockSpec((2, rows, 128), lambda i, m: (0, 0, m[1 + i]))
    starts, at, weights = [], 0, []
    for piece in pieces:
        count = units_of(piece) // 128
        for n in range(2):
            place_of = lambda i, m, at=at, count=count, n=n: (3 * count + jnp.clip(i // 2 * 2 + n - at, 0, count - 1), 0)
            weights.append(pl.BlockSpec((128, piece.shape[1]), place_of))
        starts.append(at)
        at += count
    return pl.pallas_call(
        partial(attend_back_kernel, seg, starts),
        grid_spec=pltpu.PrefetchScalarGridSpec(
            num_scalar_prefetch=1,
            grid=(pairs,),
            in_specs=[block, mine, theirs, pl.BlockSpec((2 * rows, 128), lambda i, m: (0, 0))] + [block, fixed(low_grad.shape), block]
            + weights,
            out_specs=[block, mine, theirs],
            scratch_shapes=[
                pltpu.VMEM((2, rows, 128), bf16),
                pltpu.VMEM((2, 2 * rows, 128), bf16),
                pltpu.VMEM((2, 2 * rows, 128), bf16),
                pltpu.VMEM((2, rows, 128), bf16),
                pltpu.VMEM((128, 2 * rows), bf16),
                pltpu.VMEM((2, rows, 128), bf16),
                pltpu.VMEM((2, rows, 128), bf16),
                pltpu.VMEM((128, rows), f32),
                pltpu.VMEM((2 * rows, 128), f32),
                pltpu.VMEM((2 * rows, 128), f32),
                pltpu.VMEM((2, rows, 128), bf16),
            ],
        ),
        out_shape=[
            jax.ShapeDtypeStruct((rows, width), bf16),
            jax.ShapeDtypeStruct((2, rows, width), bf16),
            jax.ShapeDtypeStruct((2, rows, width), bf16),
        ],
        compiler_params=pltpu.CompilerParams(vmem_limit_bytes=60 * MIB),
        cost_estimate=cost(
            flops=100 * 256 * seg * seg * pairs + 512 * rows * low_grad.shape[1] * pairs, bytes_accessed=rows * width * 26, transcendentals=10 * seg * seg * pairs
        ),
        name="attend_back",
    )(meta, q, kv, kvo, kcol, qx, low_grad, o, *(piece for piece in pieces for _ in range(2)))


PART = 64


def cost(flops, bytes_accessed, transcendentals):
    return pl.CostEstimate(flops=flops // PART, bytes_accessed=bytes_accessed // PART, transcendentals=transcendentals // PART)


def fixed(shape):
    return pl.BlockSpec(shape, lambda *_: (0,) * len(shape), pipeline_mode=pl.Buffered(1))


BIAS_ROWS = 32


def units_of(piece):
    return (piece.shape[0] - BIAS_ROWS) // 4


def joined(refs, size=0, matrix=0):
    parts = [ref[matrix * ref.shape[0] // size : (matrix + 1) * ref.shape[0] // size] if size else ref[...] for ref in refs]
    return jnp.concatenate(parts, axis=0) if len(parts) > 1 else parts[0]


def project_kernel(a, bias, *refs):
    pieces, (q, kv) = refs[:-2], refs[-2:]
    at = 0
    for piece in pieces:
        units = piece.shape[0] // 3
        result = dot_nt(a[...], piece[...])
        for n in range(3):
            part = (result[:, n * units : (n + 1) * units] + bias[n, :, at : at + units]).astype(bf16)
            if n == 0:
                q[:, at : at + units] = part
            else:
                kv[n - 1, :, at : at + units] = part
        at += units


def project_heads(a, pieces, bias):
    rows, width = a.shape
    columns = sum(units_of(piece) for piece in pieces)
    tile = rows // 4
    return pl.pallas_call(
        project_kernel,
        grid=(rows // tile,),
        in_specs=[pl.BlockSpec((tile, width), lambda i: (i, 0)), fixed(bias.shape)]
        + [pl.BlockSpec((3 * units_of(piece), width), lambda i: (0, 0), pipeline_mode=pl.Buffered(1)) for piece in pieces],
        out_specs=[pl.BlockSpec((tile, columns), lambda i: (i, 0)), pl.BlockSpec((2, tile, columns), lambda i: (0, i, 0))],
        out_shape=[jax.ShapeDtypeStruct((rows, columns), bf16), jax.ShapeDtypeStruct((2, rows, columns), bf16)],
        cost_estimate=cost(
            flops=6 * rows * width * columns, bytes_accessed=2 * rows * width + 6 * width * columns + 6 * rows * columns, transcendentals=0
        ),
        compiler_params=pltpu.CompilerParams(vmem_limit_bytes=60 * MIB),
        name="project",
    )(a, bias, *pieces)


def normalize(value):
    center = jnp.mean(value, axis=-1, keepdims=True)
    centred = value - center
    spread = jnp.mean(centred * centred, axis=-1, keepdims=True)
    factor = lax.rsqrt(spread + eps)
    return centred * factor, factor


def normed_rows(value, vectors):
    normal, _ = normalize(value)
    return (normal * vectors[1:2] + vectors[2:3]).astype(bf16)


def first_norm_kernel(x, vectors, out):
    out[...] = normed_rows(x[...].astype(f32), vectors)


def first_norm(x, vectors):
    rows, width = x.shape
    tile = rows // 4
    return pl.pallas_call(
        first_norm_kernel,
        grid=(rows // tile,),
        in_specs=[pl.BlockSpec((tile, width), lambda i: (i, 0)), fixed(vectors.shape)],
        out_specs=pl.BlockSpec((tile, width), lambda i: (i, 0)),
        out_shape=jax.ShapeDtypeStruct((rows, width), bf16),
        name="first_norm",
    )(x, vectors)


def eight_rows(*rows):
    return jnp.concatenate([jnp.stack(rows), jnp.zeros((8 - len(rows), rows[0].shape[-1]), f32)])


STEPS = 4
GELU_A = 0.7978845608028654
GELU_B = 0.044715


def share_specs(pieces, steps):
    specs = [pl.BlockSpec((2, 2, pieces[0].shape[2] // steps, pieces[0].shape[3]), lambda i, m: (0, 0, i, 0))]
    for piece in pieces[1:]:
        specs.append(pl.BlockSpec((2, piece.shape[1] // steps, piece.shape[2]), lambda i, m: (0, i, 0)))
    return specs


def share(refs, matrix, core):
    own = refs[0]
    return jnp.concatenate([own[matrix, core], own[matrix, 1 - core]] + [ref[matrix] for ref in refs[1:]], axis=0)


def gelu_parts(u):
    square = u * u
    t = jnp.tanh(u * (GELU_A + (GELU_A * GELU_B) * square))
    half = 0.5 * u
    slope = 0.5 + 0.5 * t + (half - half * t * t) * (GELU_A + (3 * GELU_A * GELU_B) * square)
    return slope.astype(bf16), (half + half * t).astype(bf16)


def in_turn(count, first, second):
    value = first(0)
    for n in range(count):
        following = first(n + 1) if n + 1 < count else None
        second(n, value)
        value = following


def feed_kernel(counts, meta, *refs):
    heads, weights = refs[: counts[0]], refs[counts[0] : sum(counts)]
    x, vectors, bias, own, near, near_too, slope, hidden, after, middle, total = refs[sum(counts) :]
    core = meta[0]
    tile = total.shape[0] // 4

    @pl.when(pl.program_id(0) == 0)
    def _():
        for n in range(4):
            at = slice(n * tile, (n + 1) * tile)
            left = jnp.concatenate([ref[at] for ref in heads], axis=1)
            value = x[at].astype(f32) + vectors[0:1] + dot_nn(left, joined(weights))
            after[at] = value
            middle[at] = normed_rows(value, vectors)
            total[at] = value + vectors[3:4]

    refs = (own, near, near_too)
    up, down = share(refs, 0, core), share(refs, 1, core)
    rows_of = lambda n: slice(n * tile, (n + 1) * tile)

    def rest(n, u):
        slope[0, rows_of(n)], value = gelu_parts(u)
        hidden[0, rows_of(n)] = value
        total[rows_of(n)] += dot_nn(value, down)

    in_turn(4, lambda n: dot_nt(middle[rows_of(n)], up) + bias[0], rest)


def feed(meta, x, heads, heads_pieces, vectors, bias, pieces):
    rows, width = x.shape
    units = 3 * pieces[1].shape[1]
    steps = STEPS
    wide = units // steps
    per_step = pl.BlockSpec((1, rows, wide), lambda i, m: (i, 0, 0))
    whole = pl.BlockSpec((rows, width), lambda i, m: (0, 0))
    return pl.pallas_call(
        partial(feed_kernel, (len(heads), len(heads_pieces))),
        grid_spec=pltpu.PrefetchScalarGridSpec(
            num_scalar_prefetch=1,
            grid=(steps,),
            in_specs=[fixed(h.shape) for h in heads]
            + [pl.BlockSpec((units_of(p), width), lambda i, m: (3, 0), pipeline_mode=pl.Buffered(1)) for p in heads_pieces]
            + [fixed(x.shape), fixed(vectors.shape), pl.BlockSpec((1, 1, wide), lambda i, m: (i, 0, 0))]
            + share_specs(pieces[:3], steps),
            out_specs=[per_step, per_step, whole, whole, whole],
        ),
        out_shape=[jax.ShapeDtypeStruct((steps, rows, wide), bf16)] * 2
        + [jax.ShapeDtypeStruct((rows, width), kind) for kind in (f32, bf16, f32)],
        cost_estimate=cost(
            flops=2 * rows * width * (2 * units + width), bytes_accessed=4 * units * (rows + width) + 16 * rows * width, transcendentals=rows * units
        ),
        compiler_params=pltpu.CompilerParams(vmem_limit_bytes=60 * MIB),
        name="feed",
    )(meta, *heads, *heads_pieces, x, vectors, bias, *pieces[:3])


def feed_last_kernel(middle, so_far, vectors, bias, far, far_too, slope, hidden, out, normed, weights):
    steps = slope.shape[0]

    @pl.when(pl.program_id(0) == 0)
    def _():
        size = far.shape[1] // steps
        for n in range(2):
            for i in range(steps):
                weights[n, 2 * i * size : (2 * i + 1) * size] = far[n, i * size : (i + 1) * size]
                weights[n, (2 * i + 1) * size : (2 * i + 2) * size] = far_too[n, i * size : (i + 1) * size]

    wide = slope.shape[2]
    count = 2
    tile = middle.shape[0] // count
    rows_of = lambda n: slice(n * tile, (n + 1) * tile)

    def rest(n, u):
        slopes, values = gelu_parts(u)
        for i in range(steps):
            slope[i, rows_of(n)] = slopes[:, i * wide : (i + 1) * wide]
            hidden[i, rows_of(n)] = values[:, i * wide : (i + 1) * wide]
        value = (so_far[rows_of(n)] + dot_nn(values, weights[1])).astype(bf16)
        out[rows_of(n)] = value
        normed[rows_of(n)] = normed_rows(value.astype(f32), vectors)

    in_turn(count, lambda n: dot_nt(middle[rows_of(n)], weights[0]) + bias[...], rest)


def feed_last(middle, so_far, vectors, bias, pieces):
    rows, width = middle.shape
    units = pieces[1].shape[1]
    steps = STEPS
    wide = units // steps
    tile = rows // 2
    slim = pl.BlockSpec((tile, width), lambda i: (i, 0))
    per_step = pl.BlockSpec((steps, tile, wide), lambda i: (0, i, 0))
    return pl.pallas_call(
        feed_last_kernel,
        grid=(rows // tile,),
        in_specs=[slim, slim, fixed(vectors.shape), fixed(bias.shape), fixed(pieces[3].shape), fixed(pieces[4].shape)],
        out_specs=[per_step, per_step, slim, slim],
        out_shape=[jax.ShapeDtypeStruct((steps, rows, wide), bf16)] * 2 + [jax.ShapeDtypeStruct((rows, width), bf16)] * 2,
        scratch_shapes=[pltpu.VMEM((2, units, width), bf16)],
        cost_estimate=cost(
            flops=4 * rows * width * units, bytes_accessed=4 * units * (rows + width) + 10 * rows * width, transcendentals=rows * units
        ),
        compiler_params=pltpu.CompilerParams(vmem_limit_bytes=60 * MIB),
        name="feed_last",
    )(middle, so_far, vectors, bias, pieces[3], pieces[4])


def norm_back_rows(total, value, above, gain):
    normal, factor = normalize(value)
    scaled = total * gain
    first = jnp.mean(scaled, axis=-1, keepdims=True)
    second = jnp.mean(scaled * normal, axis=-1, keepdims=True)
    return above + factor * (scaled - first - normal * second), normal


def norm_back_all(total, value, above, gain, low, sums):
    tile = total.shape[0] // 4
    rows = []
    for n in range(4):
        at = slice(n * tile, (n + 1) * tile)
        part = total[at]
        top = above[at].astype(f32)
        grad, normal = norm_back_rows(part, value[at].astype(f32), top, gain)
        low[at] = grad.astype(bf16)
        rows.append([jnp.sum(v, axis=0, keepdims=True) for v in (part * normal, part, grad, top)])
    for n in range(4):
        sums[n : n + 1] = rows[0][n] + rows[1][n] + rows[2][n] + rows[3][n]


def feed_back_kernel(
    meta, above, middle, after, vectors, slope, slope_last, hidden, hidden_last, own, near, near_too, far, far_too,
    keep, send, bias_sums, low, sums, total
):
    core = meta[0]
    step = pl.program_id(0)
    refs = (own, near, near_too, far, far_too)
    up, down = share(refs, 0, core), share(refs, 1, core)
    part = up.shape[0] // 8

    def spread(n, value):
        value = value.astype(bf16)
        keep[n, 0, 0 : 2 * part] = value[2 * part : 4 * part]
        keep[n, 0, 2 * part : 3 * part] = value[6 * part : 7 * part]
        keep[n, 0, 3 * part :] = value[0:part]
        send[n, 0, 0 : 2 * part] = value[4 * part : 6 * part]
        send[n, 0, 2 * part : 3 * part] = value[7 * part :]
        send[n, 0, 3 * part :] = value[part : 2 * part]

    @pl.when(step == 0)
    def _():
        total[...] = jnp.zeros_like(total)

    slopes = jnp.concatenate([slope[0], slope_last[0]], axis=1)
    values = jnp.concatenate([hidden[0], hidden_last[0]], axis=1)
    grad = dot_nt(above[...], down) * slopes.astype(f32)
    bias_sums[0] = jnp.broadcast_to(jnp.sum(grad, axis=0, keepdims=True), bias_sums.shape[1:])
    low_grad = grad.astype(bf16)
    spread(1, dot_tn(values, above[...]))
    total[...] += dot_nn(low_grad, up)
    spread(0, dot_tn(low_grad, middle[...]))

    @pl.when(step == pl.num_programs(0) - 1)
    def _():
        norm_back_all(total, after, above, vectors[0:1], low, sums)


def feed_back(meta, above, middle, after, gain, slopes, values, pieces):
    rows, width = middle.shape
    units = 4 * pieces[1].shape[1]
    steps = STEPS
    wide = units // steps
    vectors = jnp.broadcast_to(gain[None], (8, width))
    per_step = [pl.BlockSpec((1, rows, v.shape[2]), lambda i, m: (i, 0, 0)) for v in slopes]
    grads = pl.BlockSpec((2, 1, wide // 2, width), lambda i, m: (0, i, 0, 0))
    return pl.pallas_call(
        feed_back_kernel,
        grid_spec=pltpu.PrefetchScalarGridSpec(
            num_scalar_prefetch=1,
            grid=(steps,),
            in_specs=[fixed(above.shape), fixed(middle.shape), fixed(after.shape), fixed(vectors.shape)] + per_step * 2
            + share_specs(pieces, steps),
            out_specs=[grads, grads, pl.BlockSpec((1, 8, wide), lambda i, m: (i, 0, 0)), pl.BlockSpec((rows, width), lambda i, m: (0, 0)), pl.BlockSpec((8, width), lambda i, m: (0, 0))],
            scratch_shapes=[pltpu.VMEM((rows, width), f32)],
        ),
        out_shape=[jax.ShapeDtypeStruct((2, steps, wide // 2, width), bf16)] * 2
        + [
            jax.ShapeDtypeStruct((steps, 8, wide), f32),
            jax.ShapeDtypeStruct((rows, width), bf16),
            jax.ShapeDtypeStruct((8, width), f32),
        ],
        cost_estimate=cost(
            flops=8 * rows * width * units, bytes_accessed=12 * units * (rows + width) + 14 * rows * width, transcendentals=0
        ),
        compiler_params=pltpu.CompilerParams(vmem_limit_bytes=60 * MIB),
        name="feed_back",
    )(meta, above, middle, after, vectors, *slopes, *values, *pieces)


def project_back_kernel(groups, first, last, meta, *refs):
    refs = list(refs)
    take = lambda n: [refs.pop(0) for _ in range(n)]
    dq, dkv, dkv_got, o, a, low = take(6)
    pieces = take(len(groups))
    so_far = None if first else refs.pop(0)
    if last:
        value, above, vectors = take(3)
    keep, send, bias_sums = take(3)
    outs = take(2) if last else take(1)
    lefts = refs.pop(0)
    total = refs.pop(0) if last else None
    step = pl.program_id(0)
    core = meta[0]

    @pl.when(step == 0)
    def _():
        bias_sums[0:1] = jnp.sum(dq[...].astype(f32), axis=0, keepdims=True)
        for n in range(2):
            value_n = dkv[n].astype(f32) + dkv_got[n].astype(f32)
            lefts[n] = value_n.astype(bf16)
            if n == 1:
                bias_sums[1:2] = jnp.sum(value_n, axis=0, keepdims=True)

    sides = (dq, lefts.at[0], lefts.at[1], o)
    term = None
    for c in range(4):
        value_c = dot_tn(sides[c][...], (low if c == 3 else a)[...]).astype(bf16)
        keep_at = send_at = at = 0
        for name, size in groups:
            if name == "own":
                half = size // 2
                one, two = value_c[at : at + half], value_c[at + half : at + size]
                keep[c, keep_at : keep_at + half] = jnp.where(core == 0, one, two)
                send[c, send_at : send_at + half] = jnp.where(core == 0, two, one)
                keep_at, send_at = keep_at + half, send_at + half
            elif name in ("near", "far"):
                keep[c, keep_at : keep_at + size] = value_c[at : at + size]
                keep_at += size
            else:
                send[c, send_at : send_at + size] = value_c[at : at + size]
                send_at += size
            at += size
        if c < 3:
            part = dot_nn(sides[c][...], joined(pieces, 3, c))
            term = part if term is None else term + part
    if not first:
        term = term + so_far[...]
    if not last:
        outs[0][...] = term
        return
    tile = term.shape[1]
    total[:, pl.ds(pl.multiple_of(step * tile, tile), tile)] = term

    @pl.when(step == pl.num_programs(0) - 1)
    def _():
        norm_back_all(total, value, above, vectors[0:1], outs[0], outs[1])


def project_back(meta, names, dq, dkv, dkv_got, o, a, low, pieces, so_far, norm):
    rows, width = a.shape
    columns = dq.shape[1]
    groups = [(name, units_of(piece)) for name, piece in zip(names, pieces)]
    tiles = 4
    tile = width // tiles
    slim = pl.BlockSpec((rows, tile), lambda i, m: (0, i))
    grads = pl.BlockSpec((4, columns // 2, tile), lambda i, m: (0, 0, i))
    args = [dq, dkv, dkv_got, o, a, low, *pieces]
    specs = [fixed(dq.shape), fixed(dkv.shape), fixed(dkv.shape), fixed(o.shape), slim, slim]
    specs += [pl.BlockSpec((3 * units_of(p), tile), lambda i, m: (0, i)) for p in pieces]
    if so_far is not None:
        args.append(so_far)
        specs.append(slim)
    out_specs = [grads, grads, pl.BlockSpec((8, columns), lambda i, m: (0, 0))]
    out_shape = [jax.ShapeDtypeStruct((4, columns // 2, width), bf16)] * 2 + [jax.ShapeDtypeStruct((8, columns), f32)]
    scratch = [pltpu.VMEM((2, rows, columns), bf16)]
    if norm is None:
        out_specs.append(slim)
        out_shape.append(jax.ShapeDtypeStruct((rows, width), f32))
    else:
        value, above, gain = norm
        args += [value, above, jnp.broadcast_to(gain[None], (8, width))]
        specs += [fixed(value.shape), fixed(above.shape), fixed((8, width))]
        out_specs += [pl.BlockSpec((rows, width), lambda i, m: (0, 0)), pl.BlockSpec((8, width), lambda i, m: (0, 0))]
        out_shape += [jax.ShapeDtypeStruct((rows, width), bf16), jax.ShapeDtypeStruct((8, width), f32)]
        scratch.append(pltpu.VMEM((rows, width), f32))
    return pl.pallas_call(
        partial(project_back_kernel, groups, so_far is None, norm is not None),
        grid_spec=pltpu.PrefetchScalarGridSpec(
            num_scalar_prefetch=1, grid=(tiles,), in_specs=specs, out_specs=out_specs, scratch_shapes=scratch
        ),
        out_shape=out_shape,
        cost_estimate=cost(
            flops=14 * rows * width * columns, bytes_accessed=2 * (6 * rows * columns + 7 * width * columns + 6 * rows * width), transcendentals=0
        ),
        compiler_params=pltpu.CompilerParams(vmem_limit_bytes=60 * MIB),
        name="project_back",
    )(meta, *args)


def tie(values, *others):
    return lax.optimization_barrier((values, others))[0]


def plus(*values):
    if len(values) == 2:
        return values[0] + values[1]
    total = values[0].astype(f32)
    for value in values[1:]:
        total = total + value.astype(f32)
    return total.astype(bf16)


def meet_kernel(meta, keep_early, keep_late, got_early, got_late, far, own, early, late):
    core = meta[0]
    size = early.shape[1]
    for half, out, kept, got in ((1 - core, early, keep_early, got_early), (core, late, keep_late, got_late)):
        total = (kept[0, 0].astype(f32) + got[0, 0].astype(f32)).astype(bf16)
        out[0] = total[:size]
        far[0, half, 0] = total[size : size + size // 2]
        own[0, half, 0] = total[size + size // 2 :]


def meet(meta, keep, got):
    matrices, steps, units, width = keep.shape
    each = steps // 2
    view = lambda late: pl.BlockSpec(
        (1, 1, units, width), lambda n, j, m: (n, (m[0] if late else 1 - m[0]) * each + j, 0, 0)
    )
    halves = pl.BlockSpec((1, 2, 1, units // 4, width), lambda n, j, m: (n, 0, j, 0, 0))
    rows = pl.BlockSpec((1, units // 2, width), lambda n, j, m: (n, j, 0))
    both_shape = jax.ShapeDtypeStruct((matrices, 2, each, units // 4, width), bf16)
    rows_shape = jax.ShapeDtypeStruct((matrices, each * units // 2, width), bf16)
    far, own, early, late = pl.pallas_call(
        meet_kernel,
        grid_spec=pltpu.PrefetchScalarGridSpec(
            num_scalar_prefetch=1,
            grid=(matrices, each),
            in_specs=[view(False), view(True)] * 2,
            out_specs=[halves, halves, rows, rows],
        ),
        out_shape=[both_shape, both_shape, rows_shape, rows_shape],
        cost_estimate=cost(flops=keep.size, bytes_accessed=6 * keep.size, transcendentals=0),
        compiler_params=pltpu.CompilerParams(vmem_limit_bytes=60 * MIB),
        name="meet",
    )(meta, keep, keep, got, got)
    flat = lambda value: value.reshape(matrices, -1, width)
    return flat(far), flat(own), early, late


def exchanged(value, axis, distance):
    count = lax.axis_size(axis)
    return lax.ppermute(value, axis, [(n, n ^ distance) for n in range(count)])


def ordered(first, mine, other):
    return jnp.where(first, jnp.concatenate([mine, other], axis=1), jnp.concatenate([other, mine], axis=1))


class Send:
    def __init__(self, transfer, value):
        self.transfer, self.value = transfer, value


def hopping(value, pairs):
    return Send(lambda v: hop(v, pairs), value)


def swapping(value):
    return Send(swap, value)


def exchanging(value, axis, distance):
    return Send(lambda v: exchanged(v, axis, distance), value)


class Chain:
    def __init__(self, steps):
        self.steps, self.result, self.done = steps, None, False
        self.advance(None)

    def advance(self, value):
        self.pending, self.under_way = None, None
        try:
            self.pending, self.wait = self.steps.send(value)
        except StopIteration as stop:
            self.result, self.done = stop.value, True


def once(sends, wait):
    value = yield sends, wait
    return value


class Chains:
    def __init__(self):
        self.running = []

    def start(self, steps):
        chain = Chain(steps)
        self.running.append(chain)
        return chain

    def turn(self, values):
        self.running = [chain for chain in self.running if not chain.done]
        due = []
        for chain in self.running:
            chain.wait -= 1
            if chain.wait <= 0:
                due.append(chain)
        there = [lax.optimization_barrier((chain.under_way, values))[0] for chain in due]
        values = lax.optimization_barrier((values, [chain.under_way for chain in due]))[0]
        for chain, value in zip(due, there):
            chain.advance(value)
        return values

    def launch(self, values):
        chains = [chain for chain in self.running if chain.pending is not None]
        for chain in chains:
            sends = chain.pending if isinstance(chain.pending, list) else [chain.pending]
            values, sent = lax.optimization_barrier((values, [send.value for send in sends]))
            under_way = [send.transfer(value) for send, value in zip(sends, sent)]
            chain.under_way = under_way if isinstance(chain.pending, list) else under_way[0]
            chain.pending = None
        return values

    def stepped(self, values, new):
        values = self.turn(values)
        started = [self.start(make()) for make in new]
        return [self.launch(values), *started]

    def step(self, values, *new):
        values, *started = self.stepped(values, new)
        return (values, *started) if new else values


def summed_feed(meta, keep, send, waits):
    waits = iter(waits)
    got = yield swapping(send), next(waits)
    far, own, early, late = meet(meta, keep, got)
    relayed, early = yield [hopping(far, SECOND_HOP), hopping(early, FIRST_HOP)], next(waits)
    late, back = yield [hopping(plus(late, relayed), FIRST_HOP), swapping(early)], next(waits)
    return (yield from summed_over_line(plus(own, late, back), waits))


def summed_far(keep, send, waits):
    waits = iter(waits)
    got = yield swapping(send), next(waits)
    return (yield hopping(plus(keep, got), LAST_HOP), next(waits))


def summed_near(keep, send, core, waits):
    waits = iter(waits)
    got = yield swapping(send), next(waits)
    near = yield hopping(plus(keep, got), FIRST_HOP), next(waits)
    back = yield swapping(half_of(near, 1, 1 - core)), next(waits)
    return half_of(near, 1, core), back


def summed_over_line(total, waits):
    if lax.axis_size("dp") != 4:
        return lax.psum(total, "dp")
    line = lax.axis_index("dp")
    low, high = line & 1, line >> 1
    got = yield exchanging(half_of(total, 1, 1 - low), "dp", 1), next(waits)
    total = plus(half_of(total, 1, low), got)
    got = yield exchanging(half_of(total, 1, 1 - high), "dp", 2), next(waits)
    total = plus(half_of(total, 1, high), got)
    got = yield exchanging(total, "dp", 2), next(waits)
    total = ordered(high == 0, total, got)
    got = yield exchanging(total, "dp", 1), next(waits)
    return ordered(low == 0, total, got)


def ends_kernel(meta, *refs):
    out = refs[-1]
    for core in range(2):
        for distance in range(GROUP):

            @pl.when((meta[0] == core) & ((pl.program_id(1) ^ meta[1]) == distance))
            def _(ref=refs[core * GROUP + distance]):
                out[0] = ref[...].astype(f32)


def ends_rows(meta, first, second):
    rows, width = first[0].shape
    tile = rows // 2
    return pl.pallas_call(
        ends_kernel,
        grid_spec=pltpu.PrefetchScalarGridSpec(
            num_scalar_prefetch=1,
            grid=(rows // tile, GROUP),
            in_specs=[pl.BlockSpec((tile, width), lambda j, n, m: (j, 0))] * (2 * GROUP),
            out_specs=pl.BlockSpec((1, tile, width), lambda j, n, m: (n, j, 0)),
        ),
        out_shape=jax.ShapeDtypeStruct((GROUP, rows, width), f32),
        cost_estimate=cost(flops=GROUP * rows * width, bytes_accessed=16 * GROUP * rows * width, transcendentals=0),
        compiler_params=pltpu.CompilerParams(vmem_limit_bytes=60 * MIB),
        name="ends_rows",
    )(meta, *first, *second)


def feed_out_kernel(meta, lower, upper, to_lower, to_upper, up, down):
    for core, mine, other in ((0, lower, to_lower), (1, upper, to_upper)):
        for same, ref in ((True, mine), (False, other)):

            @pl.when((meta[0] == core) & ((pl.program_id(1) == core) == same))
            def _(ref=ref):
                up[...] = ref[0].astype(f32).T
                down[...] = ref[1].astype(f32)


def feed_out(meta, lower, upper, to_lower, to_upper):
    _, units, width = lower.shape
    tile = units // 2
    return pl.pallas_call(
        feed_out_kernel,
        grid_spec=pltpu.PrefetchScalarGridSpec(
            num_scalar_prefetch=1,
            grid=(units // tile, 2),
            in_specs=[pl.BlockSpec((2, tile, width), lambda j, h, m: (0, j, 0))] * 4,
            out_specs=[
                pl.BlockSpec((width, tile), lambda j, h, m: (0, h * 2 + j)),
                pl.BlockSpec((tile, width), lambda j, h, m: (h * 2 + j, 0)),
            ],
        ),
        out_shape=[jax.ShapeDtypeStruct((width, 2 * units), f32), jax.ShapeDtypeStruct((2 * units, width), f32)],
        cost_estimate=cost(flops=4 * units * width, bytes_accessed=32 * units * width, transcendentals=0),
        compiler_params=pltpu.CompilerParams(vmem_limit_bytes=60 * MIB),
        name="feed_out",
    )(meta, lower, upper, to_lower, to_upper)


def handed_over(steps, pairs, pause=0):
    total = yield from steps
    if pause:
        yield [], pause
    got = yield Send(lambda v: lax.ppermute(v, "section", pairs), total), 1
    return total, got


UP, DOWN = [(0, 1)], [(1, 0)]


def summed_everywhere(value):
    for axis in ("section", "tensor", "dp"):
        count = lax.axis_size(axis)
        if count & (count - 1):
            value = lax.psum(value, axis)
            continue
        distance = 1
        while distance < count:
            got = yield exchanging(value, axis, distance), 1
            value = value + got
            distance *= 2
    return value


def in_order(own, near, near_too, far, far_too, core, chip):
    first = core == 0
    last = jnp.concatenate([jnp.where(first, far, far_too), jnp.where(first, far_too, far)], axis=-1)
    by_distance = jnp.stack([own, jnp.where(first, near, near_too), jnp.where(first, near_too, near), last])
    rows = [lax.dynamic_index_in_dim(by_distance, quarter ^ chip, 0, keepdims=False) for quarter in CHIPS]
    return jnp.concatenate(rows, axis=-1)


PIECES = ("own", "near", "near_too", "far", "far_too")
GROUPS = (("own",), ("near", "near_too"), ("far", "far_too"))
OWN, NEAR, FAR = range(3)


def on_row(
    ends_in, lengths, ln_gains, ln_biases, w_qkv, qv_bias, w_out, w_up, up_bias, w_down, out_biases
):
    core = lax.axis_index("section")
    chip = lax.axis_index("tensor")
    first_core = core == 0
    micro, rows_here, seg = ends_in.shape[1:4]
    ends = ends_in.reshape(micro * rows_here, seg, D)
    lo_segment, hi_segment = core, 3 - core
    n_qv = qv_bias.shape[-1]
    n_up = up_bias.shape[-1]

    def row_from(section):
        return [
            hopping(
                lax.dynamic_index_in_dim(ends, chip ^ k, 0, keepdims=False),
                [(place(section, t), place(core_of(t), t ^ k)) for t in CHIPS if k or core_of(t) != section],
            )
            for k in CHIPS
        ]

    def chosen_rows(section, got):
        here = lax.dynamic_index_in_dim(ends, chip, 0, keepdims=False)
        got = [jnp.where(core == section, here, got[0]), *got[1:]]

        def pick(k):
            return jnp.where(k == 0, got[0], jnp.where(k == 1, got[1], jnp.where(k == 2, got[2], got[3])))

        return jnp.concatenate([pick(chip ^ lo_segment), pick(chip ^ hi_segment)])

    def segment_of(row, distance):
        return jnp.where(chip ^ distance == lo_segment, row[:seg], row[seg:])

    def row_to(section, row, distances):
        got = []
        for k in distances:
            pairs = [(place(core_of(t), t ^ k), place(section, t)) for t in CHIPS if k or core_of(t) != section]
            got.append(hopping(segment_of(row, k), pairs))
        return got

    def both(mine):
        theirs = swap(mine)
        return (jnp.where(first_core, mine, theirs), jnp.where(first_core, theirs, mine))

    chains = Chains()
    bias = jnp.concatenate([qv_bias[0].reshape(-1), up_bias[0]])
    bias_rows = -(-bias.shape[0] // D)
    bias = jnp.pad(bias, (0, bias_rows * D - bias.shape[0])).reshape(-1, D)
    extra = jnp.concatenate([bias, ln_gains[0], ln_biases[0], out_biases[0]])
    extra_rows = extra.shape[0]
    extra = jnp.concatenate(three_rounded(extra))
    extra = jnp.pad(extra, ((0, BIAS_ROWS - extra.shape[0]), (0, 0)))

    def extra_of(pack):
        rows = pack[-BIAS_ROWS:].astype(f32)
        return (rows[:extra_rows] + rows[extra_rows : 2 * extra_rows]) + rows[2 * extra_rows : 3 * extra_rows]

    pack = jnp.concatenate([jnp.swapaxes(w_qkv[0], 1, 2).reshape(-1, D), w_out[0], extra])
    sends = row_from(0)
    attention_own = both(pack)
    x = chosen_rows(0, [send.transfer(send.value) for send in sends])
    feed_mine = tie(jnp.concatenate([w_up[0].T[None], w_down]), x)
    feed_own = both(feed_mine)

    def gathered_heads(own, pieces, waits):
        pieces["own"] = own
        near = yield hopping(own, FIRST_HOP), waits[0]
        pieces["near"], pieces["near_too"] = near, swap(near)
        heads = half_of(near[: 4 * n_qv].reshape(4, n_qv, D), 1, core).reshape(-1, D)
        far = yield hopping(jnp.concatenate([heads, near[4 * n_qv :]]), SECOND_HOP), waits[1]
        pieces["far"], pieces["far_too"] = far, swap(far)

    def gathered_feed(own, pieces, waits):
        near = yield hopping(own, FIRST_HOP), waits[0]
        pieces += [own.reshape(2, 2, -1, D), near, swap(near)]
        far = yield hopping(half_of(near, 1, core), SECOND_HOP), waits[1]
        pieces += [far, swap(far)]

    attention, feeding = ({}, {}), ([], [])
    x, attention_own = tie((x, attention_own))

    def bias_of(name, layer, start, size):
        part = extra_of(attention[layer][name])[:bias_rows].reshape(-1)[start : start + size]
        if name == "far":
            part = half_of(part, 0, core)
        if name == "far_too":
            part = half_of(part, 0, 1 - core)
        return part

    six = [extra_of(own)[bias_rows:] for own in attention_own]
    gains, shifts, end_biases = ([layer_six[n : n + 2] for layer_six in six] for n in (0, 2, 4))

    length = lax.dynamic_index_in_dim(lengths.reshape(-1), chip, 0, keepdims=False)
    segments = jnp.stack([lo_segment, hi_segment, 1 - core, 2 + core])
    positions = (segments[:, None] * seg + jnp.arange(seg)[None]).reshape(-1)
    kcol = key_columns(positions, length)
    heads_here = n_qv // HEAD
    quarters = {"own": chip, "near": chip ^ (1 + core), "near_too": chip ^ (2 - core), "far": chip ^ 3, "far_too": chip ^ 3}
    pairs_of = {name: n_qv // 128 // (2 if name.startswith("far") else 1) for name in PIECES}
    across = {"own": "own", "near": "near_too", "near_too": "near", "far": "far_too", "far_too": "far"}

    def head_slopes(name):
        head = quarters[name] * heads_here + jnp.arange(heads_here)
        if name == "far":
            head = half_of(head, 0, core)
        if name == "far_too":
            head = half_of(head, 0, 1 - core)
        return jnp.exp2(-8.0 * (head + 1).astype(f32) / HEADS)

    slopes = {name: head_slopes(name) for name in PIECES}

    def group_meta(names):
        starts, at = {}, 0
        for name in names:
            starts[name] = at
            at += pairs_of[name]
        table = [starts[across[name]] + n for name in names for n in range(pairs_of[name])]
        return jnp.concatenate([core[None].astype(jnp.int32), jnp.array(table, jnp.int32)])

    groups = [
        [
            dict(names=names, meta=group_meta(names), qcol=query_columns(jnp.concatenate([slopes[name] for name in names])))
            for names in GROUPS
        ]
        for layer in range(2)
    ]

    def pieces_of(layer, index):
        return [attention[layer][name] for name in groups[layer][index]["names"]]

    def heads_bias(layer, index):
        names = groups[layer][index]["names"]
        return jnp.stack(
            [
                jnp.concatenate([bias_of(name, layer, 0, n_qv) for name in names]),
                jnp.zeros((sum(pairs_of[name] for name in names) * 128,), f32),
                jnp.concatenate([bias_of(name, layer, n_qv, n_qv) for name in names]),
            ]
        )[:, None]

    meta = core[None].astype(jnp.int32)

    def into_heads(layer, index, normed):
        q, kv = project_heads(normed, pieces_of(layer, index), heads_bias(layer, index))
        return q, kv, swap(kv)

    def attended(layer, index, projected):
        group = groups[layer][index]
        return tuple(projected) + tuple(attend(group["meta"], *projected, kcol, group["qcol"]))

    def fed(layer, x, saved):
        vectors = eight_rows(end_biases[layer][0], gains[layer][1], shifts[layer][1], end_biases[layer][1])
        pieces = [p for index in range(len(saved)) for p in pieces_of(layer, index)]
        bias = [bias_of("own", layer, 2 * n_qv, n_up)]
        bias = [half_of(bias[0], 0, core), half_of(bias[0], 0, 1 - core)]
        bias += [bias_of(name, layer, 2 * n_qv, n_up) for name in ("near", "near_too")]
        bias = jnp.concatenate([part.reshape(STEPS, -1) for part in bias], axis=1)[:, None]
        return feed(meta, x, [v[3] for v in saved], pieces, vectors, bias, feeding[layer])

    def fed_last(layer, middle, total):
        following = min(layer + 1, 1)
        vectors = eight_rows(jnp.zeros((D,), f32), gains[following][0], shifts[following][0])
        bias = [bias_of(name, layer, 2 * n_qv, n_up).reshape(STEPS, -1) for name in ("far", "far_too")]
        return feed_last(middle, total, vectors, jnp.concatenate(bias, axis=1).reshape(1, -1), feeding[layer])

    kept = [None, None]
    chains.start(gathered_heads(attention_own[0], attention[0], (1, 1)))
    x = chains.launch(x)
    normed = first_norm(x, eight_rows(jnp.zeros((D,), f32), gains[0][0], shifts[0][0]))
    for layer in range(2):
        saved = [None] * 3
        saved[OWN] = attended(layer, OWN, into_heads(layer, OWN, normed))
        (normed, saved[OWN], feed_own), *_ = chains.stepped(
            (normed, saved[OWN], feed_own),
            [] if layer else [lambda: gathered_feed(feed_own[0], feeding[0], (2, 1))],
        )
        saved[NEAR] = attended(layer, NEAR, into_heads(layer, NEAR, normed))
        normed, saved[NEAR] = chains.step((normed, saved[NEAR]))
        saved[FAR] = attended(layer, FAR, into_heads(layer, FAR, normed))
        saved = chains.step(saved)
        slope, hidden, after, middle, total = fed(layer, x, saved)
        (total, attention_own, ends), following = chains.step(
            (total, attention_own, ends),
            lambda: once(row_from(1), 1) if layer else gathered_heads(attention_own[1], attention[1], (2, 1)),
        )
        slope_last, hidden_last, result, normed_next = fed_last(layer, middle, total)
        kept[layer] = (x, normed, saved, after, middle, (slope, slope_last), (hidden, hidden_last))
        if layer == 0:
            (x, normed, feed_own), _ = chains.step(
                (result, normed_next, feed_own), lambda: gathered_feed(feed_own[1], feeding[1], (3, 1))
            )
    x, *sent_back = chains.step(result, lambda: once(row_to(1, result, (0, 1)), 1))
    grad = chosen_rows(1, following.result)

    def heads_gradients(layer, index, low):
        group = groups[layer][index]
        q, kv, kvo, o, qx = kept[layer][2][index]
        return attend_back(group["meta"], q, kv, kvo, kcol, qx, low, o, pieces_of(layer, index))

    def weight_gradients(layer, index, grads, low, so_far, last):
        group = groups[layer][index]
        norm = (kept[layer][0], low, gains[layer][0]) if last else None
        return project_back(
            meta, group["names"], *grads, kept[layer][2][index][3], kept[layer][1], low, pieces_of(layer, index), so_far, norm
        )

    def sums_of(layer, results, unit_sums, sums_one, sums_two):
        parts = {}
        for index, group in enumerate(groups[layer]):
            at = 0
            for name in group["names"]:
                size = pairs_of[name] * 128
                parts[name] = results[index][2][0:2, at : at + size]
                at += size
        unit_sums = unit_sums[:, 0]
        part = unit_sums.shape[1] // 8

        def unit_part(start, count):
            return unit_sums[:, start * part : (start + count) * part].reshape(-1)

        own_keep, own_send = unit_part(0, 1), unit_part(1, 1)
        own = jnp.concatenate([jnp.where(first_core, own_keep, own_send), jnp.where(first_core, own_send, own_keep)])
        return jnp.concatenate(
            [
                jnp.stack([sums_one[0], sums_two[0], sums_one[1], sums_two[1], sums_two[2], sums_two[3]]),
                in_order(*[parts[name] for name in PIECES], core, chip),
                in_order(own, unit_part(2, 2), unit_part(4, 2), unit_part(6, 1), unit_part(7, 1), core, chip).reshape(-1, D),
            ]
        )

    def feed_gradients(layer, grad):
        _, _, _, after, middle, slope, hidden = kept[layer]
        return feed_back(meta, grad, middle, after, gains[layer][1], slope, hidden, feeding[layer])

    def backward(layer, grad, others, new, late):
        keep, send, unit_sums, low, sums_two = feed_gradients(layer, grad)
        (low, keep, send, others), feed_sums, *started = chains.step(
            (low, keep, send, others),
            lambda: handed_over(
                summed_feed(meta, keep, send, (1, 2, 1, 1, 2, 1, 1) if layer else (1, 2, 1, 1, 2, 2, 1)), UP if layer else DOWN, 4 if layer else 0
            ),
            *(lambda make=make: make(others) for make in new),
        )

        results = [None] * 3
        dq_far, dkv_far, sent_far = heads_gradients(layer, FAR, low)
        (low, sent_far), got_far = chains.step((low, sent_far), lambda: once(swapping(sent_far), 1))
        dq_near, dkv_near, sent_near = heads_gradients(layer, NEAR, low)
        (low, sent_near), got_near = chains.step((low, sent_near), lambda: once(swapping(sent_near), 1))
        results[FAR] = weight_gradients(layer, FAR, (dq_far, dkv_far, got_far.result), low, None, False)
        (low, results[FAR]), far_sum, *started_late = chains.stepped(
            (low, results[FAR]), [lambda: summed_far(*results[FAR][:2], (1, 1)), *late]
        )
        results[NEAR] = weight_gradients(layer, NEAR, (dq_near, dkv_near, got_near.result), low, results[FAR][3], False)
        (low, results[NEAR]), near_sum = chains.step(
            (low, results[NEAR]), lambda: summed_near(*results[NEAR][:2], core, (1, 2, 1))
        )
        dq_own, dkv_own, sent_own = heads_gradients(layer, OWN, low)
        (low, sent_own), got_own = chains.step((low, sent_own), lambda: once(swapping(sent_own), 1))
        low, dq_own, dkv_own = chains.step((low, dq_own, dkv_own))
        results[OWN] = weight_gradients(layer, OWN, (dq_own, dkv_own, got_own.result), low, results[NEAR][3], True)
        grad, sums_one = results[OWN][3:]
        sums = sums_of(layer, results, unit_sums, sums_one, sums_two)
        return grad, results[OWN], sums, feed_sums, near_sum, far_sum, started + started_late

    grad, own, sums_upper, upper_feed, near_sum, far_sum, again = backward(
        1, grad, x, [lambda row: once(row_to(1, row, (2, 3)), 1)], []
    )
    sent_back += again
    (grad, own), own_sum = chains.step((grad, own), lambda: once(swapping(own[1]), 1))

    def summed_heads(pairs, keep, own_sum, near_sum, far_sum):
        total = plus(keep, own_sum.result, *near_sum.result, far_sum.result)
        return handed_over(summed_over_line(total, iter((1, 1, 1, 1))), pairs)

    upper_parts = own[0], own_sum, near_sum, far_sum
    grad, own, sums_lower, lower_feed, near_sum, far_sum, (upper_heads,) = backward(
        0, grad, (), [lambda _: summed_heads(UP, *upper_parts)], []
    )
    (grad, sums_lower, own), own_sum, zero, both_sums = chains.step(
        (grad, sums_lower, own),
        lambda: once(swapping(own[1]), 1),
        lambda: once(row_to(0, grad, (0,)), 1),
        lambda: summed_everywhere(jnp.stack([sums_lower, sums_upper])),
    )
    grad, lower_heads = chains.step(
        grad, lambda: summed_heads(DOWN, own[0], own_sum, near_sum, far_sum)
    )
    grad, three = chains.step(grad, lambda: once(row_to(0, grad, (3,)), 2))
    grad, one, two = chains.step(grad, lambda: once(row_to(0, grad, (1,)), 1), lambda: once(row_to(0, grad, (2,)), 1))
    first_rows = [zero, one, two, three]

    def feed_outputs():
        (lower, to_lower), (upper, to_upper) = lower_feed.result, upper_feed.result
        return feed_out(meta, lower, upper, to_lower, to_upper)

    def ends_outputs():
        place_here = jnp.stack([core, chip]).astype(jnp.int32)
        first, second = [chain.result[0] for chain in first_rows], [*sent_back[0].result, *sent_back[1].result]
        own_core = core_of(chip)
        first[0] = jnp.where(own_core == 0, segment_of(grad, 0), first[0])
        second[0] = jnp.where(own_core == 1, segment_of(result, 0), second[0])
        rows = ends_rows(place_here, first, second)
        return rows.reshape(1, micro, rows_here, seg, D)

    ready, waiting = {}, {"feed": (feed_outputs, [lower_feed, upper_feed]), "ends": (ends_outputs, first_rows)}
    while any(not chain.done for chain in chains.running):
        for name in list(waiting):
            make, needed = waiting[name]
            if all(chain.done for chain in needed):
                ready[name] = make()
                del waiting[name]
        ready, grad = chains.step((ready, grad))
    for name, (make, _) in waiting.items():
        ready[name] = make()
    ends_out, (grad_up, grad_down) = ready["ends"], ready["feed"]
    (lower, to_lower), (upper, to_upper) = lower_heads.result, upper_heads.result
    attention_grads = jnp.where(
        first_core, jnp.concatenate([lower, to_lower], axis=1), jnp.concatenate([to_upper, upper], axis=1)
    ).astype(f32)
    both_sums = both_sums.result
    sums = jnp.where(first_core, both_sums[0], both_sums[1])
    grad_qv = lax.dynamic_slice_in_dim(sums[6:8], chip * n_qv, n_qv, 1)[None]
    grad_up_bias = lax.dynamic_slice_in_dim(sums[8:].reshape(-1), chip * n_up, n_up, 0)[None]
    return (
        ends_out,
        sums[0:2][None],
        sums[2:4][None],
        jnp.swapaxes(attention_grads[:3], 1, 2)[None],
        grad_qv,
        attention_grads[3:],
        grad_up[None],
        grad_up_bias,
        grad_down[None],
        sums[4:6][None],
    )


def solution(mesh):
    return jax.shard_map(
        on_row if one_row_a_chip(mesh) else on_device,
        mesh=mesh,
        in_specs=(
            P("section", None, "dp", "tensor", None),
            P(None, "dp"),
            P("section", None, None),
            P("section", None, None),
            P("section", None, None, "tensor"),
            P("section", None, "tensor"),
            P("section", "tensor", None),
            P("section", None, "tensor"),
            P("section", "tensor"),
            P("section", "tensor", None),
            P("section", None, None),
        ),
        out_specs=(
            P("section", None, "dp", "tensor", None),
            P("section", None, None),
            P("section", None, None),
            P("section", None, None, "tensor"),
            P("section", None, "tensor"),
            P("section", "tensor", None),
            P("section", None, "tensor"),
            P("section", "tensor"),
            P("section", "tensor", None),
            P("section", None, None),
        ),
        check_vma=False,
    )
```

```python
from functools import partial

import jax
import jax.numpy as jnp
from jax import lax
from jax.experimental import pallas as pl
from jax.experimental.pallas import tpu as pltpu
from jax.sharding import PartitionSpec as P

D = 1024
HEADS = 16


eps = 1e-05
widest = 512


def shifted(shard, axis, by):
    devices = lax.axis_size(axis)
    pairs = [(i, i + by) for i in range(devices) if 0 <= i + by < devices]
    return lax.ppermute(shard, axis, pairs)


def layer_norm(inputs, gain, bias):
    center = jnp.mean(inputs, axis=-1, keepdims=True)
    centred = inputs - center
    spread = jnp.mean(centred * centred, axis=-1, keepdims=True)
    factor = lax.rsqrt(spread + eps)
    normal = centred * factor
    return (normal * gain + bias, normal, factor)


def norm_back(grad_norm, normal, factor, gain):
    scaled = grad_norm * gain
    first_mean = jnp.mean(scaled, axis=-1, keepdims=True)
    second_mean = jnp.mean(scaled * normal, axis=-1, keepdims=True)
    return factor * (scaled - first_mean - normal * second_mean)


def gather_tokens(values):
    return lax.all_gather(values, "tensor", axis=1, tiled=True)


def scatter_tokens(values):
    return lax.psum_scatter(values, "tensor", scatter_dimension=1, tiled=True)


def gather_grads(values):
    return lax.all_gather(values, "tensor", axis=1, tiled=True)


def scatter_grads(values):
    return lax.psum_scatter(
        values.astype(jnp.bfloat16), "tensor", scatter_dimension=1, tiled=True
    ).astype(jnp.float32)


def project(whole_rows, w_proj, proj_bias):
    combined = jnp.einsum("rld,cde->crle", whole_rows, w_proj, preferred_element_type=jnp.float32)
    queries = (combined[0] + proj_bias[0]).astype(jnp.bfloat16)
    key_rows = combined[1].astype(jnp.bfloat16)
    value_rows = (combined[2] + proj_bias[1]).astype(jnp.bfloat16)
    return (queries, key_rows, value_rows)


def score_block(query_block, key_heads, row_start, row_lengths, slopes_here):
    block_rows = query_block.shape[1]
    seq_len = key_heads.shape[1]
    head_size = key_heads.shape[-1]
    scores = jnp.einsum(
        "rqhd,rkhd->rhqk", query_block, key_heads, preferred_element_type=jnp.float32
    ) * head_size ** (-0.5)
    rowpos = row_start + jnp.arange(block_rows)
    keypos = jnp.arange(seq_len)
    distance = (rowpos[:, None] - keypos[None, :]).astype(jnp.float32)
    scores = scores - slopes_here[None, :, None, None] * distance[None, None]
    causal = keypos[None, :] <= rowpos[:, None]
    inside = keypos[None, :] < row_lengths[:, None]
    allowed = causal[None, None] & inside[:, None, None, :]
    return jnp.where(allowed, scores, -1e30)


def attention(queries, key_rows, value_rows, row_lengths, slopes_here):
    row_count, seq_len, width = queries.shape
    head_count = slopes_here.shape[0]
    head_size = width // head_count
    block_rows = min(widest, seq_len)
    query_heads = queries.reshape(row_count, seq_len, head_count, head_size)
    key_heads = key_rows.reshape(row_count, seq_len, head_count, head_size)
    value_heads = value_rows.reshape(row_count, seq_len, head_count, head_size)

    def one_block(row_start):
        query_block = lax.dynamic_slice_in_dim(query_heads, row_start, block_rows, 1)
        scores = score_block(query_block, key_heads, row_start, row_lengths, slopes_here)
        row_max = jnp.max(scores, axis=-1, keepdims=True)
        powers = jnp.exp(scores - row_max)
        row_total = jnp.sum(powers, axis=-1, keepdims=True)
        probs = (powers / row_total).astype(jnp.bfloat16)
        block_out = jnp.einsum(
            "rhqk,rkhd->rqhd", probs, value_heads, preferred_element_type=jnp.float32
        )
        return (block_out.astype(jnp.bfloat16), (row_max + jnp.log(row_total))[..., 0])

    starts = jnp.arange(seq_len // block_rows) * block_rows
    blocks_out, log_totals = lax.map(one_block, starts)
    attended = jnp.moveaxis(blocks_out, 0, 1).reshape(row_count, seq_len, width)
    log_totals = jnp.moveaxis(log_totals, 0, 2).reshape(row_count, head_count, seq_len)
    return (attended, log_totals)


def attention_back(
    queries, key_rows, value_rows, grad_attended, log_totals, row_lengths, slopes_here
):
    row_count, seq_len, width = queries.shape
    head_count = slopes_here.shape[0]
    head_size = width // head_count
    scale = head_size ** (-0.5)
    block_rows = min(widest, seq_len)
    query_heads = queries.reshape(row_count, seq_len, head_count, head_size)
    key_heads = key_rows.reshape(row_count, seq_len, head_count, head_size)
    value_heads = value_rows.reshape(row_count, seq_len, head_count, head_size)
    grad_heads = grad_attended.reshape(row_count, seq_len, head_count, head_size)

    def one_block(carry, row_start):
        grad_keys, grad_values = carry
        query_block = lax.dynamic_slice_in_dim(query_heads, row_start, block_rows, 1)
        grad_block = lax.dynamic_slice_in_dim(grad_heads, row_start, block_rows, 1)
        scores = score_block(query_block, key_heads, row_start, row_lengths, slopes_here)
        block_logs = lax.dynamic_slice_in_dim(log_totals, row_start, block_rows, 2)
        probs = jnp.exp(scores - block_logs[..., None])
        grad_values = grad_values + jnp.einsum(
            "rhqk,rqhd->rkhd",
            probs.astype(jnp.bfloat16),
            grad_block,
            preferred_element_type=jnp.float32,
        )
        grad_probs = jnp.einsum(
            "rqhd,rkhd->rhqk", grad_block, value_heads, preferred_element_type=jnp.float32
        )
        inner = jnp.sum(probs * grad_probs, axis=-1, keepdims=True)
        grad_scores = (probs * (grad_probs - inner)).astype(jnp.bfloat16)
        grad_query = (
            jnp.einsum(
                "rhqk,rkhd->rqhd", grad_scores, key_heads, preferred_element_type=jnp.float32
            )
            * scale
        )
        grad_keys = (
            grad_keys
            + jnp.einsum(
                "rhqk,rqhd->rkhd", grad_scores, query_block, preferred_element_type=jnp.float32
            )
            * scale
        )
        return ((grad_keys, grad_values), grad_query.astype(jnp.bfloat16))

    zeros_heads = jnp.zeros((row_count, seq_len, head_count, head_size), jnp.float32)
    starts = jnp.arange(seq_len // block_rows) * block_rows
    (grad_keys, grad_values), grad_queries = lax.scan(one_block, (zeros_heads, zeros_heads), starts)
    grad_queries = jnp.moveaxis(grad_queries, 0, 1).reshape(row_count, seq_len, width)
    grad_keys = grad_keys.reshape(row_count, seq_len, width).astype(jnp.bfloat16)
    grad_values = grad_values.reshape(row_count, seq_len, width).astype(jnp.bfloat16)
    return (grad_queries, grad_keys, grad_values)


def layer_forward(inputs, row_lengths, weights, slopes_here):
    gains, biases, w_proj, proj_bias, w_attn, w_first, first_bias, w_second, end_biases = weights
    normed, _, _ = layer_norm(inputs, gains[0], biases[0])
    whole_rows = gather_tokens(normed.astype(jnp.bfloat16))
    queries, key_rows, value_rows = project(whole_rows, w_proj, proj_bias)
    attended, log_totals = attention(queries, key_rows, value_rows, row_lengths, slopes_here)
    attn_part = jnp.dot(attended, w_attn, preferred_element_type=jnp.float32)
    after_attn = inputs + scatter_tokens(attn_part) + end_biases[0]
    middle, _, _ = layer_norm(after_attn, gains[1], biases[1])
    middle_rows = gather_tokens(middle.astype(jnp.bfloat16))
    pre_act = jnp.dot(middle_rows, w_first, preferred_element_type=jnp.float32) + first_bias
    hidden = jax.nn.gelu(pre_act, approximate=True).astype(jnp.bfloat16)
    ffn_part = jnp.dot(hidden, w_second, preferred_element_type=jnp.float32)
    result = after_attn + scatter_tokens(ffn_part) + end_biases[1]
    return (result, after_attn, attended, log_totals, whole_rows, middle_rows)


def layer_backward(grad_result, stored, row_lengths, weights, slopes_here):
    gains, biases, w_proj, proj_bias, w_attn, w_first, first_bias, w_second, end_biases = weights
    inputs = stored[0].astype(jnp.float32)
    after_attn = stored[1]
    attended = stored[2]
    log_totals = stored[3]
    normed, normal_one, factor_one = layer_norm(inputs, gains[0], biases[0])
    middle, normal_two, factor_two = layer_norm(after_attn, gains[1], biases[1])
    whole_rows = gather_tokens(normed.astype(jnp.bfloat16))
    middle_rows = gather_tokens(middle.astype(jnp.bfloat16))
    pre_act = jnp.dot(middle_rows, w_first, preferred_element_type=jnp.float32) + first_bias
    hidden, gelu_pull = jax.vjp(partial(jax.nn.gelu, approximate=True), pre_act)
    hidden = hidden.astype(jnp.bfloat16)
    grad_end_two = jnp.sum(grad_result, axis=(0, 1))
    grad_branch = gather_grads(grad_result.astype(jnp.bfloat16))
    grad_second = jnp.einsum("rlf,rld->fd", hidden, grad_branch, preferred_element_type=jnp.float32)
    grad_hidden = jnp.einsum(
        "rld,fd->rlf", grad_branch, w_second, preferred_element_type=jnp.float32
    )
    grad_pre = gelu_pull(grad_hidden)[0].astype(jnp.bfloat16)
    grad_first_bias = jnp.sum(grad_pre, axis=(0, 1), dtype=jnp.float32)
    grad_first = jnp.einsum(
        "rld,rlf->df", middle_rows, grad_pre, preferred_element_type=jnp.float32
    )
    grad_middle = scatter_grads(
        jnp.einsum("rlf,df->rld", grad_pre, w_first, preferred_element_type=jnp.float32)
    )
    grad_gain_two = jnp.sum(grad_middle * normal_two, axis=(0, 1))
    grad_bias_two = jnp.sum(grad_middle, axis=(0, 1))
    grad_after = grad_result + norm_back(grad_middle, normal_two, factor_two, gains[1])
    grad_end_one = jnp.sum(grad_after, axis=(0, 1))
    grad_attn_rows = gather_grads(grad_after.astype(jnp.bfloat16))
    grad_attn = jnp.einsum(
        "rle,rld->ed", attended, grad_attn_rows, preferred_element_type=jnp.float32
    )
    grad_attended = jnp.einsum(
        "rld,ed->rle", grad_attn_rows, w_attn, preferred_element_type=jnp.float32
    ).astype(jnp.bfloat16)
    queries, key_rows, value_rows = project(whole_rows, w_proj, proj_bias)
    grad_queries, grad_keys, grad_values = attention_back(
        queries, key_rows, value_rows, grad_attended, log_totals, row_lengths, slopes_here
    )
    stacked = jnp.stack([grad_queries, grad_keys, grad_values])
    grad_proj = jnp.einsum("rld,crle->cde", whole_rows, stacked, preferred_element_type=jnp.float32)
    grad_proj_bias = jnp.stack(
        [
            jnp.sum(grad_queries, axis=(0, 1), dtype=jnp.float32),
            jnp.sum(grad_values, axis=(0, 1), dtype=jnp.float32),
        ]
    )
    grad_normed = scatter_grads(
        jnp.einsum("crle,cde->rld", stacked, w_proj, preferred_element_type=jnp.float32)
    )
    grad_gain_one = jnp.sum(grad_normed * normal_one, axis=(0, 1))
    grad_bias_one = jnp.sum(grad_normed, axis=(0, 1))
    grad_inputs = grad_after + norm_back(grad_normed, normal_one, factor_one, gains[0])
    sharded = (grad_proj, grad_proj_bias, grad_attn, grad_first, grad_first_bias, grad_second)
    shared = (
        jnp.stack([grad_gain_one, grad_gain_two]),
        jnp.stack([grad_bias_one, grad_bias_two]),
        jnp.stack([grad_end_one, grad_end_two]),
    )
    return (grad_inputs, sharded, shared)


def on_device(
    ends_in, lengths, ln_gains, ln_biases, w_qkv, qv_bias, w_out, w_up, up_bias, w_down, out_biases
):
    section_index = lax.axis_index("section")
    weights = tuple(
        (
            stored[0]
            for stored in (
                ln_gains,
                ln_biases,
                w_qkv,
                qv_bias,
                w_out,
                w_up,
                up_bias,
                w_down,
                out_biases,
            )
        )
    )
    local_ends = ends_in[0]
    micro_count = local_ends.shape[0]
    heads_here = w_qkv.shape[-1] // (D // HEADS)
    first_head = lax.axis_index("tensor") * heads_here
    slopes_here = jnp.exp2(
        -8.0 * (first_head + jnp.arange(heads_here) + 1).astype(jnp.float32) / HEADS
    )
    padded = jnp.concatenate([local_ends, jnp.zeros_like(local_ends[:1])], axis=0)
    tick_list = jnp.arange(micro_count + 1)

    def forward_tick(received, item):
        arriving, tick_index = item
        entering = jnp.where(section_index == 0, arriving, received)
        slot_index = jnp.clip(tick_index - section_index, 0, micro_count - 1)
        row_lengths = lax.dynamic_index_in_dim(lengths, slot_index, 0, keepdims=False)
        result, after_attn, attended, log_totals, whole_rows, middle_rows = layer_forward(
            entering.astype(jnp.float32), row_lengths, weights, slopes_here
        )
        outgoing = shifted(result.astype(jnp.bfloat16), "section", 1)
        stored = (entering, after_attn, attended, log_totals)
        return (outgoing, (result, stored))

    _, (results, kept_all) = lax.scan(
        forward_tick, jnp.zeros_like(local_ends[0]), (padded, tick_list)
    )
    sharded_zero = (
        jnp.zeros(w_qkv.shape[1:], jnp.float32),
        jnp.zeros(qv_bias.shape[1:], jnp.float32),
        jnp.zeros(w_out.shape[1:], jnp.float32),
        jnp.zeros(w_up.shape[1:], jnp.float32),
        jnp.zeros(up_bias.shape[1:], jnp.float32),
        jnp.zeros(w_down.shape[1:], jnp.float32),
    )
    shared_zero = (
        jnp.zeros(ln_gains.shape[1:], jnp.float32),
        jnp.zeros(ln_biases.shape[1:], jnp.float32),
        jnp.zeros(out_biases.shape[1:], jnp.float32),
    )

    def backward_tick(carry, item):
        received, sharded_total, shared_total = carry
        arriving, tick_index = item
        grad_result = jnp.where(section_index == 1, arriving, received).astype(jnp.float32)
        slot_index = tick_index - 1 + section_index
        is_valid = ((slot_index >= 0) & (slot_index < micro_count)).astype(jnp.float32)
        slot_index = jnp.clip(slot_index, 0, micro_count - 1)
        stored = tuple(
            (
                lax.dynamic_index_in_dim(kept, slot_index + section_index, 0, keepdims=False)
                for kept in kept_all
            )
        )
        row_lengths = lax.dynamic_index_in_dim(lengths, slot_index, 0, keepdims=False)
        grad_inputs, sharded, shared = layer_backward(
            grad_result, stored, row_lengths, weights, slopes_here
        )
        outgoing = shifted(grad_inputs.astype(jnp.bfloat16), "section", -1)
        sharded = tuple((value * is_valid for value in sharded))
        shared = tuple((value * is_valid for value in shared))
        sharded_total = tuple((left + right for left, right in zip(sharded_total, sharded)))
        shared_total = tuple((left + right for left, right in zip(shared_total, shared)))
        return ((outgoing, sharded_total, shared_total), grad_inputs)

    start_carry = (jnp.zeros_like(local_ends[0]), sharded_zero, shared_zero)
    (_, sharded_total, shared_total), grads_in = lax.scan(
        backward_tick, start_carry, (padded, tick_list)
    )
    sharded_total = (
        lax.psum(sharded_total[0].astype(jnp.bfloat16), "dp").astype(jnp.float32),
        lax.psum(sharded_total[1].astype(jnp.bfloat16), "dp").astype(jnp.float32),
        lax.psum(sharded_total[2].astype(jnp.bfloat16), "dp").astype(jnp.float32),
        lax.psum(sharded_total[3].astype(jnp.bfloat16), "dp").astype(jnp.float32),
        lax.psum(sharded_total[4].astype(jnp.bfloat16), "dp").astype(jnp.float32),
        lax.psum(sharded_total[5].astype(jnp.bfloat16), "dp").astype(jnp.float32),
    )
    shared_total = lax.psum((shared_total[0], shared_total[1], shared_total[2]), ("dp", "tensor"))
    ends_local = jnp.where(section_index == 0, grads_in[1:], results[1:])
    return (
        ends_local[None],
        shared_total[0][None],
        shared_total[1][None],
        sharded_total[0][None],
        sharded_total[1][None],
        sharded_total[2][None],
        sharded_total[3][None],
        sharded_total[4][None],
        sharded_total[5][None],
        shared_total[2][None],
    )


bf16, f32 = jnp.bfloat16, jnp.float32
HEAD = D // HEADS
LOG2E = 1.4426950408889634
GROUP = 4
ST = ("section", "tensor")
MIB = 2**20


def one_row_a_chip(mesh):
    return mesh.shape["section"] == 2 and mesh.shape["tensor"] == GROUP


def core_of(segment):
    return (segment & 1) ^ (segment >> 1)


def place(core, chip):
    return core * GROUP + chip


CHIPS = range(GROUP)
FIRST_HOP = [(place(0, t), place(0, t ^ 1)) for t in CHIPS] + [(place(1, t), place(1, t ^ 2)) for t in CHIPS]
LAST_HOP = [(place(c, t), place(c, t ^ 3)) for c in range(2) for t in CHIPS]
SECOND_HOP = [(place(0, t), place(0, t ^ 2)) for t in CHIPS] + [(place(1, t), place(1, t ^ 1)) for t in CHIPS]


def hop(value, pairs):
    return lax.ppermute(value, ST, pairs)


def swap(value):
    return lax.ppermute(value, "section", [(0, 1), (1, 0)])


def half_of(value, axis, index):
    size = value.shape[axis] // 2
    return lax.dynamic_slice_in_dim(value, index * size, size, axis)


def dot_nn(left, right):
    return lax.dot_general(left, right, (((1,), (0,)), ((), ())), preferred_element_type=f32)


def dot_nt(left, right):
    return lax.dot_general(left, right, (((1,), (1,)), ((), ())), preferred_element_type=f32)


def dot_tn(left, right):
    return lax.dot_general(left, right, (((0,), (0,)), ((), ())), preferred_element_type=f32)


def three_parts(value):
    first = value.astype(bf16)
    rest = value - first.astype(f32)
    second = rest.astype(bf16)
    third = (rest - second.astype(f32)).astype(bf16)
    return first, second, third


def three_rounded(value):
    parts = []
    for _ in range(3):
        part = lax.reduce_precision(value, 8, 7)
        parts.append(part.astype(bf16))
        value = value - part
    return tuple(parts)


def key_columns(positions, length):
    high = (positions // 8 * 8).astype(f32)
    low = (positions % 8).astype(f32)
    mask = jnp.where(positions < length, 0.0, -1e30).astype(f32)
    one = jnp.ones_like(high)
    columns = jnp.stack([high, high, high, low, low, low, mask, one, one, one], axis=1)
    half = jnp.pad(columns, ((0, 0), (0, HEAD - 10)))
    return jnp.concatenate([half, half], axis=1).astype(bf16)


def query_columns(slopes):
    first, second, third = three_rounded(slopes * 8.0)
    one = jnp.ones_like(first)
    columns = jnp.stack([first, second, third, first, second, third, one], axis=1)
    half = jnp.pad(columns, ((0, 0), (0, HEAD - 7))).reshape(-1, 2, HEAD)
    row = jnp.concatenate([half[:, 1], half[:, 0]], axis=1).astype(f32)
    return jnp.broadcast_to(row[:, None, :], (row.shape[0], 8, 2 * HEAD))


def attend_kernel(seg, meta, q, kv, kvo, kcol, qcol, o, qx, qp, kp, vp):
    other = 1 - meta[0]
    lane = lax.broadcasted_iota(jnp.int32, (1, 128), 1)
    low = lane < 64
    base = qcol[0, 0:1, :].astype(bf16)
    scale = LOG2E / 8
    one = jnp.ones((1, 128), bf16)
    for h in range(2):
        mine = low if h == 0 else ~low
        qp[h] = jnp.where(mine, q[...], base)
        kp[h, 0 : 2 * seg] = jnp.where(mine, kv[0], kcol[0 : 2 * seg])
        kp[h, 2 * seg :] = jnp.where(mine, kvo[0], kcol[2 * seg :])
        vp[h, 0 : 2 * seg] = jnp.where(mine, kv[1], one)
        vp[h, 2 * seg :] = jnp.where(mine, kvo[1], one)

    apart, first, second = range(3)
    far = pl.multiple_of(2 * seg + other * seg, seg)
    keys_of = ([far], [0], [0, 2 * seg, seg])
    units = [(part, h) for part in (apart, first, second) for h in range(2)]

    def scores_of(part, h):
        start = pl.multiple_of(other * seg, seg) if part == apart else (part - first) * seg
        scores = [dot_nt(qp[h, pl.ds(start, seg)], kp[h, pl.ds(key, seg)]) for key in keys_of[part]]
        if part != apart:
            row = lax.broadcasted_iota(jnp.int32, (seg, seg), 0)
            column = lax.broadcasted_iota(jnp.int32, (seg, seg), 1)
            scores[-1] = jnp.where(column <= row, scores[-1], -1e30)
        return scores

    done = {}

    def weigh(part, h, scores):
        top = scores[0].max(axis=1, keepdims=True)
        for score in scores[1:]:
            top = jnp.maximum(top, score.max(axis=1, keepdims=True))
        if part != apart:
            use = other == part - first
            apart_top, apart_total = done[apart, h]
            apart_top = jnp.where(use, apart_top, -1e30)
            top = jnp.maximum(top, apart_top)
            weight = jnp.where(use, jnp.exp2((apart_top - top) * scale), 0.0)
        total = None
        for score, key in zip(scores, keys_of[part]):
            powers = jnp.exp2((score - top) * scale).astype(bf16)
            term = dot_nn(powers, vp[h, pl.ds(key, seg)])
            total = term if total is None else total + term
        done[part, h] = top, total if part == apart else total + weight * apart_total

    scores = scores_of(*units[0])
    for n, unit in enumerate(units):
        following = scores_of(*units[n + 1]) if n + 1 < len(units) else None
        weigh(*unit, scores)
        scores = following
    at = lane & 63
    for segment in range(2):
        rows = slice(segment * seg, (segment + 1) * seg)
        (top_low, total_low), (top_high, total_high) = done[first + segment, 0], done[first + segment, 1]
        number = jnp.where(low, total_low, total_high)
        sums = jnp.where(low, total_high, total_low)
        o[rows] = (number / pltpu.roll(sums, 64, 1)).astype(bf16)
        logs = jnp.where(low, top_high, top_low) + jnp.log(sums) * 8.0
        parts = three_parts(logs)
        qx[rows] = jnp.where(at == 7, -parts[0], jnp.where(at == 8, -parts[1], jnp.where(at == 9, -parts[2], base)))


def attend(meta, q, kv, kvo, kcol, qcol):
    rows, width = q.shape
    seg = rows // 2
    pairs = width // 128
    block = pl.BlockSpec((rows, 128), lambda i, m: (0, i))
    return pl.pallas_call(
        partial(attend_kernel, seg),
        grid_spec=pltpu.PrefetchScalarGridSpec(
            num_scalar_prefetch=1,
            grid=(pairs,),
            in_specs=[
                block,
                pl.BlockSpec((2, rows, 128), lambda i, m: (0, 0, i)),
                pl.BlockSpec((2, rows, 128), lambda i, m: (0, 0, m[1 + i])),
                pl.BlockSpec((2 * rows, 128), lambda i, m: (0, 0)),
                pl.BlockSpec((1, 8, 128), lambda i, m: (i, 0, 0)),
            ],
            out_specs=[block, block],
            scratch_shapes=[
                pltpu.VMEM((2, rows, 128), bf16),
                pltpu.VMEM((2, 2 * rows, 128), bf16),
                pltpu.VMEM((2, 2 * rows, 128), bf16),
            ],
        ),
        out_shape=[jax.ShapeDtypeStruct((rows, width), bf16)] * 2,
        compiler_params=pltpu.CompilerParams(vmem_limit_bytes=60 * MIB),
        cost_estimate=cost(
            flops=40 * 256 * seg * seg * pairs, bytes_accessed=rows * width * 14, transcendentals=10 * seg * seg * pairs
        ),
        name="attend",
    )(meta, q, kv, kvo, kcol, qcol)


def attend_back_kernel(
    seg, starts, meta, q, kv, kvo, kcol, qx, low_grad, o, *refs
):
    weights, (dq, dkv, dkvo, qp, kp, vp, dp, kt, qm, dm, aq, ak, av, both) = refs[: 2 * len(starts)], refs[2 * len(starts) :]
    pair = pl.program_id(0)

    @pl.when(pair % 2 == 0)
    def _():
        two = []
        for n in range(2):
            weight = weights[n][...]
            for ref, start in zip(weights[2 + n :: 2], starts[1:]):
                weight = jnp.where(pair + n < start, weight, ref[...])
            two.append(weight)
        grads = dot_nt(low_grad[...], jnp.concatenate(two, axis=0)).astype(bf16)
        both[0], both[1] = grads[:, :128], grads[:, 128:]

    do = both[pair % 2]
    other = 1 - meta[0]
    lane = lax.broadcasted_iota(jnp.int32, (1, 128), 1)
    low = lane < 64
    at = lane & 63
    scale = LOG2E / 8
    zero = jnp.zeros((1, 128), bf16)
    product = do.astype(f32) * o[...].astype(f32)
    for h in range(2):
        mine = low if h == 0 else ~low
        qp[h] = jnp.where(mine, q[...], qx[...])
        kp[h, 0 : 2 * seg] = jnp.where(mine, kv[0], kcol[0 : 2 * seg])
        kp[h, 2 * seg :] = jnp.where(mine, kvo[0], kcol[2 * seg :])
        vp[h, 0 : 2 * seg] = jnp.where(mine, kv[1], kcol[0 : 2 * seg])
        vp[h, 2 * seg :] = jnp.where(mine, kvo[1], kcol[2 * seg :])
        first, second, third = three_parts(jnp.sum(jnp.where(mine, product, 0.0), axis=1, keepdims=True))
        extra = jnp.where(at == 7, -first, jnp.where(at == 8, -second, jnp.where(at == 9, -third, zero)))
        dp[h] = jnp.where(mine, do, extra)
        qm[h] = jnp.where(mine, q[...], zero)
        dm[h] = jnp.where(mine, do, zero)
    kt[:, 0 : 2 * seg] = kv[0].T
    kt[:, 2 * seg :] = kvo[0].T
    aq[...] = jnp.zeros_like(aq)
    ak[...] = jnp.zeros_like(ak)
    av[...] = jnp.zeros_like(av)

    def block(query_start, query_count, key_start, key_count, masked):
        queries, keys = pl.ds(query_start, query_count), pl.ds(key_start, key_count)
        for h in range(2):
            probs = jnp.exp2(dot_nt(kp[h, keys], qp[h, queries]) * scale)
            if masked:
                row = lax.broadcasted_iota(jnp.int32, (key_count, query_count), 0)
                column = lax.broadcasted_iota(jnp.int32, (key_count, query_count), 1)
                probs = jnp.where(row <= column, probs, 0.0)
            grads = (probs * dot_nt(vp[h, keys], dp[h, queries])).astype(bf16)
            av[keys] += dot_nn(probs.astype(bf16), dm[h, queries])
            ak[keys] += dot_nn(grads, qm[h, queries])
            aq[h * 64 : (h + 1) * 64, queries] += dot_nn(kt[h * 64 : (h + 1) * 64, keys], grads)

    half = seg // 2
    for segment in range(2):
        start = segment * seg
        block(start, half, start, half, True)
        block(start + half, half, start, half, False)
        block(start + half, half, start + half, half, True)
    block(seg, seg, 0, seg, False)
    block(seg, seg, 2 * seg, seg, False)
    block(pl.multiple_of(other * seg, seg), seg, pl.multiple_of(2 * seg + other * seg, seg), seg, False)
    dq[...] = (aq[...] * 0.125).T.astype(bf16)
    dkv[0] = (ak[0 : 2 * seg] * 0.125).astype(bf16)
    dkvo[0] = (ak[2 * seg :] * 0.125).astype(bf16)
    dkv[1] = av[0 : 2 * seg].astype(bf16)
    dkvo[1] = av[2 * seg :].astype(bf16)


def attend_back(meta, q, kv, kvo, kcol, qx, low_grad, o, pieces):
    rows, width = q.shape
    seg = rows // 2
    pairs = width // 128
    block = pl.BlockSpec((rows, 128), lambda i, m: (0, i))
    mine = pl.BlockSpec((2, rows, 128), lambda i, m: (0, 0, i))
    theirs = pl.BlockSpec((2, rows, 128), lambda i, m: (0, 0, m[1 + i]))
    starts, at, weights = [], 0, []
    for piece in pieces:
        count = units_of(piece) // 128
        for n in range(2):
            place_of = lambda i, m, at=at, count=count, n=n: (3 * count + jnp.clip(i // 2 * 2 + n - at, 0, count - 1), 0)
            weights.append(pl.BlockSpec((128, piece.shape[1]), place_of))
        starts.append(at)
        at += count
    return pl.pallas_call(
        partial(attend_back_kernel, seg, starts),
        grid_spec=pltpu.PrefetchScalarGridSpec(
            num_scalar_prefetch=1,
            grid=(pairs,),
            in_specs=[block, mine, theirs, pl.BlockSpec((2 * rows, 128), lambda i, m: (0, 0))] + [block, fixed(low_grad.shape), block]
            + weights,
            out_specs=[block, mine, theirs],
            scratch_shapes=[
                pltpu.VMEM((2, rows, 128), bf16),
                pltpu.VMEM((2, 2 * rows, 128), bf16),
                pltpu.VMEM((2, 2 * rows, 128), bf16),
                pltpu.VMEM((2, rows, 128), bf16),
                pltpu.VMEM((128, 2 * rows), bf16),
                pltpu.VMEM((2, rows, 128), bf16),
                pltpu.VMEM((2, rows, 128), bf16),
                pltpu.VMEM((128, rows), f32),
                pltpu.VMEM((2 * rows, 128), f32),
                pltpu.VMEM((2 * rows, 128), f32),
                pltpu.VMEM((2, rows, 128), bf16),
            ],
        ),
        out_shape=[
            jax.ShapeDtypeStruct((rows, width), bf16),
            jax.ShapeDtypeStruct((2, rows, width), bf16),
            jax.ShapeDtypeStruct((2, rows, width), bf16),
        ],
        compiler_params=pltpu.CompilerParams(vmem_limit_bytes=60 * MIB),
        cost_estimate=cost(
            flops=100 * 256 * seg * seg * pairs + 512 * rows * low_grad.shape[1] * pairs, bytes_accessed=rows * width * 26, transcendentals=10 * seg * seg * pairs
        ),
        name="attend_back",
    )(meta, q, kv, kvo, kcol, qx, low_grad, o, *(piece for piece in pieces for _ in range(2)))


PART = 64


def cost(flops, bytes_accessed, transcendentals):
    return pl.CostEstimate(flops=flops // PART, bytes_accessed=bytes_accessed // PART, transcendentals=transcendentals // PART)


def fixed(shape):
    return pl.BlockSpec(shape, lambda *_: (0,) * len(shape), pipeline_mode=pl.Buffered(1))


BIAS_ROWS = 32


def units_of(piece):
    return (piece.shape[0] - BIAS_ROWS) // 4


def joined(refs, size=0, matrix=0):
    parts = [ref[matrix * ref.shape[0] // size : (matrix + 1) * ref.shape[0] // size] if size else ref[...] for ref in refs]
    return jnp.concatenate(parts, axis=0) if len(parts) > 1 else parts[0]


def project_kernel(first, a, bias, *refs):
    refs = list(refs)
    rows = a[...]
    if first:
        vectors, normed = refs.pop(0), refs.pop()
        rows = normed_rows(rows.astype(f32), vectors)
        normed[...] = rows
    pieces, (q, kv) = refs[:-2], refs[-2:]
    at = 0
    for piece in pieces:
        units = piece.shape[0] // 3
        result = dot_nt(rows, piece[...])
        for n in range(3):
            part = (result[:, n * units : (n + 1) * units] + bias[n, :, at : at + units]).astype(bf16)
            if n == 0:
                q[:, at : at + units] = part
            else:
                kv[n - 1, :, at : at + units] = part
        at += units


def project_heads(a, pieces, bias, vectors=None):
    rows, width = a.shape
    columns = sum(units_of(piece) for piece in pieces)
    tile = rows // 4
    slim = pl.BlockSpec((tile, width), lambda i: (i, 0))
    first = vectors is not None
    extra = [vectors] if first else []
    return pl.pallas_call(
        partial(project_kernel, first),
        grid=(rows // tile,),
        in_specs=[slim, fixed(bias.shape)]
        + [fixed(v.shape) for v in extra]
        + [pl.BlockSpec((3 * units_of(piece), width), lambda i: (0, 0), pipeline_mode=pl.Buffered(1)) for piece in pieces],
        out_specs=[pl.BlockSpec((tile, columns), lambda i: (i, 0)), pl.BlockSpec((2, tile, columns), lambda i: (0, i, 0))]
        + [slim] * len(extra),
        out_shape=[jax.ShapeDtypeStruct((rows, columns), bf16), jax.ShapeDtypeStruct((2, rows, columns), bf16)]
        + [jax.ShapeDtypeStruct((rows, width), bf16)] * len(extra),
        cost_estimate=cost(
            flops=6 * rows * width * columns, bytes_accessed=2 * rows * width + 6 * width * columns + 6 * rows * columns, transcendentals=0
        ),
        compiler_params=pltpu.CompilerParams(vmem_limit_bytes=60 * MIB),
        name="project",
    )(a, bias, *extra, *pieces)


def normalize(value):
    center = jnp.mean(value, axis=-1, keepdims=True)
    centred = value - center
    spread = jnp.mean(centred * centred, axis=-1, keepdims=True)
    factor = lax.rsqrt(spread + eps)
    return centred * factor, factor


def normed_rows(value, vectors):
    normal, _ = normalize(value)
    return (normal * vectors[1:2] + vectors[2:3]).astype(bf16)


def eight_rows(*rows):
    return jnp.concatenate([jnp.stack(rows), jnp.zeros((8 - len(rows), rows[0].shape[-1]), f32)])


STEPS = 4
GELU_A = 0.7978845608028654
GELU_B = 0.044715


def share_specs(pieces, steps):
    specs = [pl.BlockSpec((2, 2, pieces[0].shape[2] // steps, pieces[0].shape[3]), lambda i, m: (0, 0, i, 0))]
    for piece in pieces[1:]:
        specs.append(pl.BlockSpec((2, piece.shape[1] // steps, piece.shape[2]), lambda i, m: (0, i, 0)))
    return specs


def share(refs, matrix, core):
    own = refs[0]
    return jnp.concatenate([own[matrix, core], own[matrix, 1 - core]] + [ref[matrix] for ref in refs[1:]], axis=0)


def gelu_parts(u):
    square = u * u
    t = jnp.tanh(u * (GELU_A + (GELU_A * GELU_B) * square))
    half = 0.5 * u
    slope = 0.5 + 0.5 * t + (half - half * t * t) * (GELU_A + (3 * GELU_A * GELU_B) * square)
    return slope.astype(bf16), (half + half * t).astype(bf16)


def in_turn(count, first, second):
    value = first(0)
    for n in range(count):
        following = first(n + 1) if n + 1 < count else None
        second(n, value)
        value = following


def feed_kernel(counts, meta, *refs):
    heads, weights = refs[: counts[0]], refs[counts[0] : sum(counts)]
    x, vectors, bias, own, near, near_too, slope, hidden, after, middle, total = refs[sum(counts) :]
    core = meta[0]
    tile = total.shape[0] // 4

    @pl.when(pl.program_id(0) == 0)
    def _():
        for n in range(4):
            at = slice(n * tile, (n + 1) * tile)
            left = jnp.concatenate([ref[at] for ref in heads], axis=1)
            value = x[at].astype(f32) + vectors[0:1] + dot_nn(left, joined(weights))
            after[at] = value
            middle[at] = normed_rows(value, vectors)
            total[at] = value + vectors[3:4]

    refs = (own, near, near_too)
    up, down = share(refs, 0, core), share(refs, 1, core)
    rows_of = lambda n: slice(n * tile, (n + 1) * tile)

    def rest(n, u):
        slope[0, rows_of(n)], value = gelu_parts(u)
        hidden[0, rows_of(n)] = value
        total[rows_of(n)] += dot_nn(value, down)

    in_turn(4, lambda n: dot_nt(middle[rows_of(n)], up) + bias[0], rest)


def feed(meta, x, heads, heads_pieces, vectors, bias, pieces):
    rows, width = x.shape
    units = 3 * pieces[1].shape[1]
    steps = STEPS
    wide = units // steps
    per_step = pl.BlockSpec((1, rows, wide), lambda i, m: (i, 0, 0))
    whole = pl.BlockSpec((rows, width), lambda i, m: (0, 0))
    return pl.pallas_call(
        partial(feed_kernel, (len(heads), len(heads_pieces))),
        grid_spec=pltpu.PrefetchScalarGridSpec(
            num_scalar_prefetch=1,
            grid=(steps,),
            in_specs=[fixed(h.shape) for h in heads]
            + [pl.BlockSpec((units_of(p), width), lambda i, m: (3, 0), pipeline_mode=pl.Buffered(1)) for p in heads_pieces]
            + [fixed(x.shape), fixed(vectors.shape), pl.BlockSpec((1, 1, wide), lambda i, m: (i, 0, 0))]
            + share_specs(pieces[:3], steps),
            out_specs=[per_step, per_step, whole, whole, whole],
        ),
        out_shape=[jax.ShapeDtypeStruct((steps, rows, wide), bf16)] * 2
        + [jax.ShapeDtypeStruct((rows, width), kind) for kind in (f32, bf16, f32)],
        cost_estimate=cost(
            flops=2 * rows * width * (2 * units + width), bytes_accessed=4 * units * (rows + width) + 16 * rows * width, transcendentals=rows * units
        ),
        compiler_params=pltpu.CompilerParams(vmem_limit_bytes=60 * MIB),
        name="feed",
    )(meta, *heads, *heads_pieces, x, vectors, bias, *pieces[:3])


def feed_last_kernel(middle, so_far, vectors, bias, far, far_too, slope, hidden, out, normed, weights):
    steps = slope.shape[0]

    @pl.when(pl.program_id(0) == 0)
    def _():
        size = far.shape[1] // steps
        for n in range(2):
            for i in range(steps):
                weights[n, 2 * i * size : (2 * i + 1) * size] = far[n, i * size : (i + 1) * size]
                weights[n, (2 * i + 1) * size : (2 * i + 2) * size] = far_too[n, i * size : (i + 1) * size]

    wide = slope.shape[2]
    count = 2
    tile = middle.shape[0] // count
    rows_of = lambda n: slice(n * tile, (n + 1) * tile)

    def rest(n, u):
        slopes, values = gelu_parts(u)
        for i in range(steps):
            slope[i, rows_of(n)] = slopes[:, i * wide : (i + 1) * wide]
            hidden[i, rows_of(n)] = values[:, i * wide : (i + 1) * wide]
        value = (so_far[rows_of(n)] + dot_nn(values, weights[1])).astype(bf16)
        out[rows_of(n)] = value
        normed[rows_of(n)] = normed_rows(value.astype(f32), vectors)

    in_turn(count, lambda n: dot_nt(middle[rows_of(n)], weights[0]) + bias[...], rest)


def feed_last(middle, so_far, vectors, bias, pieces):
    rows, width = middle.shape
    units = pieces[1].shape[1]
    steps = STEPS
    wide = units // steps
    tile = rows // 2
    slim = pl.BlockSpec((tile, width), lambda i: (i, 0))
    per_step = pl.BlockSpec((steps, tile, wide), lambda i: (0, i, 0))
    return pl.pallas_call(
        feed_last_kernel,
        grid=(rows // tile,),
        in_specs=[slim, slim, fixed(vectors.shape), fixed(bias.shape), fixed(pieces[3].shape), fixed(pieces[4].shape)],
        out_specs=[per_step, per_step, slim, slim],
        out_shape=[jax.ShapeDtypeStruct((steps, rows, wide), bf16)] * 2 + [jax.ShapeDtypeStruct((rows, width), bf16)] * 2,
        scratch_shapes=[pltpu.VMEM((2, units, width), bf16)],
        cost_estimate=cost(
            flops=4 * rows * width * units, bytes_accessed=4 * units * (rows + width) + 10 * rows * width, transcendentals=rows * units
        ),
        compiler_params=pltpu.CompilerParams(vmem_limit_bytes=60 * MIB),
        name="feed_last",
    )(middle, so_far, vectors, bias, pieces[3], pieces[4])


def norm_back_rows(total, value, above, gain):
    normal, factor = normalize(value)
    scaled = total * gain
    first = jnp.mean(scaled, axis=-1, keepdims=True)
    second = jnp.mean(scaled * normal, axis=-1, keepdims=True)
    return above + factor * (scaled - first - normal * second), normal


def norm_back_all(total, value, above, gain, low, sums):
    tile = total.shape[0] // 4
    rows = []
    for n in range(4):
        at = slice(n * tile, (n + 1) * tile)
        part = total[at]
        top = above[at].astype(f32)
        grad, normal = norm_back_rows(part, value[at].astype(f32), top, gain)
        low[at] = grad.astype(bf16)
        rows.append([jnp.sum(v, axis=0, keepdims=True) for v in (part * normal, part, grad, top)])
    for n in range(4):
        sums[n : n + 1] = rows[0][n] + rows[1][n] + rows[2][n] + rows[3][n]


def feed_back_kernel(
    meta, above, middle, after, vectors, slope, slope_last, hidden, hidden_last, own, near, near_too, far, far_too,
    keep, send, bias_sums, low, sums, total
):
    core = meta[0]
    step = pl.program_id(0)
    refs = (own, near, near_too, far, far_too)
    up, down = share(refs, 0, core), share(refs, 1, core)
    part = up.shape[0] // 8

    def spread(n, value):
        value = value.astype(bf16)
        keep[n, 0, 0 : 2 * part] = value[2 * part : 4 * part]
        keep[n, 0, 2 * part : 3 * part] = value[6 * part : 7 * part]
        keep[n, 0, 3 * part :] = value[0:part]
        send[n, 0, 0 : 2 * part] = value[4 * part : 6 * part]
        send[n, 0, 2 * part : 3 * part] = value[7 * part :]
        send[n, 0, 3 * part :] = value[part : 2 * part]

    @pl.when(step == 0)
    def _():
        total[...] = jnp.zeros_like(total)

    slopes = jnp.concatenate([slope[0], slope_last[0]], axis=1)
    values = jnp.concatenate([hidden[0], hidden_last[0]], axis=1)
    grad = dot_nt(above[...], down) * slopes.astype(f32)
    bias_sums[0] = jnp.broadcast_to(jnp.sum(grad, axis=0, keepdims=True), bias_sums.shape[1:])
    low_grad = grad.astype(bf16)
    spread(1, dot_tn(values, above[...]))
    total[...] += dot_nn(low_grad, up)
    spread(0, dot_tn(low_grad, middle[...]))

    @pl.when(step == pl.num_programs(0) - 1)
    def _():
        norm_back_all(total, after, above, vectors[0:1], low, sums)


def feed_back(meta, above, middle, after, gain, slopes, values, pieces):
    rows, width = middle.shape
    units = 4 * pieces[1].shape[1]
    steps = STEPS
    wide = units // steps
    vectors = jnp.broadcast_to(gain[None], (8, width))
    per_step = [pl.BlockSpec((1, rows, v.shape[2]), lambda i, m: (i, 0, 0)) for v in slopes]
    grads = pl.BlockSpec((2, 1, wide // 2, width), lambda i, m: (0, i, 0, 0))
    return pl.pallas_call(
        feed_back_kernel,
        grid_spec=pltpu.PrefetchScalarGridSpec(
            num_scalar_prefetch=1,
            grid=(steps,),
            in_specs=[fixed(above.shape), fixed(middle.shape), fixed(after.shape), fixed(vectors.shape)] + per_step * 2
            + share_specs(pieces, steps),
            out_specs=[grads, grads, pl.BlockSpec((1, 8, wide), lambda i, m: (i, 0, 0)), pl.BlockSpec((rows, width), lambda i, m: (0, 0)), pl.BlockSpec((8, width), lambda i, m: (0, 0))],
            scratch_shapes=[pltpu.VMEM((rows, width), f32)],
        ),
        out_shape=[jax.ShapeDtypeStruct((2, steps, wide // 2, width), bf16)] * 2
        + [
            jax.ShapeDtypeStruct((steps, 8, wide), f32),
            jax.ShapeDtypeStruct((rows, width), bf16),
            jax.ShapeDtypeStruct((8, width), f32),
        ],
        cost_estimate=cost(
            flops=8 * rows * width * units, bytes_accessed=12 * units * (rows + width) + 14 * rows * width, transcendentals=0
        ),
        compiler_params=pltpu.CompilerParams(vmem_limit_bytes=60 * MIB),
        name="feed_back",
    )(meta, above, middle, after, vectors, *slopes, *values, *pieces)


def project_back_kernel(groups, first, last, meta, *refs):
    refs = list(refs)
    take = lambda n: [refs.pop(0) for _ in range(n)]
    dq, dkv, dkv_got, o, a, low = take(6)
    pieces = take(len(groups))
    so_far = None if first else refs.pop(0)
    if last:
        value, above, vectors = take(3)
    keep, send, bias_sums = take(3)
    outs = take(2) if last else take(1)
    lefts = refs.pop(0)
    total = refs.pop(0) if last else None
    step = pl.program_id(0)
    core = meta[0]

    @pl.when(step == 0)
    def _():
        bias_sums[0:1] = jnp.sum(dq[...].astype(f32), axis=0, keepdims=True)
        for n in range(2):
            value_n = dkv[n].astype(f32) + dkv_got[n].astype(f32)
            lefts[n] = value_n.astype(bf16)
            if n == 1:
                bias_sums[1:2] = jnp.sum(value_n, axis=0, keepdims=True)

    sides = (dq, lefts.at[0], lefts.at[1], o)
    term = None
    for c in range(4):
        value_c = dot_tn(sides[c][...], (low if c == 3 else a)[...]).astype(bf16)
        keep_at = send_at = at = 0
        for name, size in groups:
            if name == "own":
                half = size // 2
                one, two = value_c[at : at + half], value_c[at + half : at + size]
                keep[c, keep_at : keep_at + half] = jnp.where(core == 0, one, two)
                send[c, send_at : send_at + half] = jnp.where(core == 0, two, one)
                keep_at, send_at = keep_at + half, send_at + half
            elif name in ("near", "far"):
                keep[c, keep_at : keep_at + size] = value_c[at : at + size]
                keep_at += size
            else:
                send[c, send_at : send_at + size] = value_c[at : at + size]
                send_at += size
            at += size
        if c < 3:
            part = dot_nn(sides[c][...], joined(pieces, 3, c))
            term = part if term is None else term + part
    if not first:
        term = term + so_far[...].astype(f32)
    if not last:
        outs[0][...] = term.astype(bf16)
        return
    tile = term.shape[1]
    total[:, pl.ds(pl.multiple_of(step * tile, tile), tile)] = term

    @pl.when(step == pl.num_programs(0) - 1)
    def _():
        norm_back_all(total, value, above, vectors[0:1], outs[0], outs[1])


def project_back(meta, names, dq, dkv, dkv_got, o, a, low, pieces, so_far, norm):
    rows, width = a.shape
    columns = dq.shape[1]
    groups = [(name, units_of(piece)) for name, piece in zip(names, pieces)]
    tiles = 4
    tile = width // tiles
    slim = pl.BlockSpec((rows, tile), lambda i, m: (0, i))
    grads = pl.BlockSpec((4, columns // 2, tile), lambda i, m: (0, 0, i))
    args = [dq, dkv, dkv_got, o, a, low, *pieces]
    specs = [fixed(dq.shape), fixed(dkv.shape), fixed(dkv.shape), fixed(o.shape), slim, slim]
    specs += [pl.BlockSpec((3 * units_of(p), tile), lambda i, m: (0, i)) for p in pieces]
    if so_far is not None:
        args.append(so_far)
        specs.append(slim)
    out_specs = [grads, grads, pl.BlockSpec((8, columns), lambda i, m: (0, 0))]
    out_shape = [jax.ShapeDtypeStruct((4, columns // 2, width), bf16)] * 2 + [jax.ShapeDtypeStruct((8, columns), f32)]
    scratch = [pltpu.VMEM((2, rows, columns), bf16)]
    if norm is None:
        out_specs.append(slim)
        out_shape.append(jax.ShapeDtypeStruct((rows, width), bf16))
    else:
        value, above, gain = norm
        args += [value, above, jnp.broadcast_to(gain[None], (8, width))]
        specs += [fixed(value.shape), fixed(above.shape), fixed((8, width))]
        out_specs += [pl.BlockSpec((rows, width), lambda i, m: (0, 0)), pl.BlockSpec((8, width), lambda i, m: (0, 0))]
        out_shape += [jax.ShapeDtypeStruct((rows, width), bf16), jax.ShapeDtypeStruct((8, width), f32)]
        scratch.append(pltpu.VMEM((rows, width), f32))
    return pl.pallas_call(
        partial(project_back_kernel, groups, so_far is None, norm is not None),
        grid_spec=pltpu.PrefetchScalarGridSpec(
            num_scalar_prefetch=1, grid=(tiles,), in_specs=specs, out_specs=out_specs, scratch_shapes=scratch
        ),
        out_shape=out_shape,
        cost_estimate=cost(
            flops=14 * rows * width * columns, bytes_accessed=2 * (6 * rows * columns + 7 * width * columns + 6 * rows * width), transcendentals=0
        ),
        compiler_params=pltpu.CompilerParams(vmem_limit_bytes=60 * MIB),
        name="project_back",
    )(meta, *args)


def tie(values, *others):
    return lax.optimization_barrier((values, others))[0]


def plus(*values):
    if len(values) == 2:
        return values[0] + values[1]
    total = values[0].astype(f32)
    for value in values[1:]:
        total = total + value.astype(f32)
    return total.astype(bf16)


def meet_kernel(meta, keep_early, keep_late, got_early, got_late, far, own, early, late):
    core = meta[0]
    size = early.shape[1]
    for half, out, kept, got in ((1 - core, early, keep_early, got_early), (core, late, keep_late, got_late)):
        total = (kept[0, 0].astype(f32) + got[0, 0].astype(f32)).astype(bf16)
        out[0] = total[:size]
        far[0, half, 0] = total[size : size + size // 2]
        own[0, half, 0] = total[size + size // 2 :]


def meet(meta, keep, got):
    matrices, steps, units, width = keep.shape
    each = steps // 2
    view = lambda late: pl.BlockSpec(
        (1, 1, units, width), lambda n, j, m: (n, (m[0] if late else 1 - m[0]) * each + j, 0, 0)
    )
    halves = pl.BlockSpec((1, 2, 1, units // 4, width), lambda n, j, m: (n, 0, j, 0, 0))
    rows = pl.BlockSpec((1, units // 2, width), lambda n, j, m: (n, j, 0))
    both_shape = jax.ShapeDtypeStruct((matrices, 2, each, units // 4, width), bf16)
    rows_shape = jax.ShapeDtypeStruct((matrices, each * units // 2, width), bf16)
    far, own, early, late = pl.pallas_call(
        meet_kernel,
        grid_spec=pltpu.PrefetchScalarGridSpec(
            num_scalar_prefetch=1,
            grid=(matrices, each),
            in_specs=[view(False), view(True)] * 2,
            out_specs=[halves, halves, rows, rows],
        ),
        out_shape=[both_shape, both_shape, rows_shape, rows_shape],
        cost_estimate=cost(flops=keep.size, bytes_accessed=6 * keep.size, transcendentals=0),
        compiler_params=pltpu.CompilerParams(vmem_limit_bytes=60 * MIB),
        name="meet",
    )(meta, keep, keep, got, got)
    flat = lambda value: value.reshape(matrices, -1, width)
    return flat(far), flat(own), early, late


def exchanged(value, axis, distance):
    count = lax.axis_size(axis)
    return lax.ppermute(value, axis, [(n, n ^ distance) for n in range(count)])


def ordered(first, mine, other):
    return jnp.where(first, jnp.concatenate([mine, other], axis=1), jnp.concatenate([other, mine], axis=1))


class Send:
    def __init__(self, transfer, value):
        self.transfer, self.value = transfer, value


def hopping(value, pairs):
    return Send(lambda v: hop(v, pairs), value)


def swapping(value):
    return Send(swap, value)


def exchanging(value, axis, distance):
    return Send(lambda v: exchanged(v, axis, distance), value)


class Chain:
    def __init__(self, steps):
        self.steps, self.result, self.done = steps, None, False
        self.advance(None)

    def advance(self, value):
        self.pending, self.under_way = None, None
        try:
            self.pending, self.wait = self.steps.send(value)
        except StopIteration as stop:
            self.result, self.done = stop.value, True


def once(sends, wait):
    value = yield sends, wait
    return value


class Chains:
    def __init__(self):
        self.running = []

    def start(self, steps):
        chain = Chain(steps)
        self.running.append(chain)
        return chain

    def turn(self, values):
        self.running = [chain for chain in self.running if not chain.done]
        due = []
        for chain in self.running:
            chain.wait -= 1
            if chain.wait <= 0:
                due.append(chain)
        there = [lax.optimization_barrier((chain.under_way, values))[0] for chain in due]
        values = lax.optimization_barrier((values, [chain.under_way for chain in due]))[0]
        for chain, value in zip(due, there):
            chain.advance(value)
        return values

    def launch(self, values):
        chains = [chain for chain in self.running if chain.pending is not None]
        for chain in chains:
            sends = chain.pending if isinstance(chain.pending, list) else [chain.pending]
            values, sent = lax.optimization_barrier((values, [send.value for send in sends]))
            under_way = [send.transfer(value) for send, value in zip(sends, sent)]
            chain.under_way = under_way if isinstance(chain.pending, list) else under_way[0]
            chain.pending = None
        return values

    def stepped(self, values, new):
        values = self.turn(values)
        started = [self.start(make()) for make in new]
        return [self.launch(values), *started]

    def step(self, values, *new):
        values, *started = self.stepped(values, new)
        return (values, *started) if new else values


def summed_feed(meta, keep, send, waits):
    waits = iter(waits)
    got = yield swapping(send), next(waits)
    far, own, early, late = meet(meta, keep, got)
    relayed, early = yield [hopping(far, SECOND_HOP), hopping(early, FIRST_HOP)], next(waits)
    late, back = yield [hopping(plus(late, relayed), FIRST_HOP), swapping(early)], next(waits)
    return (yield from summed_over_line(plus(own, late, back), waits))


def summed_far(keep, send, waits):
    waits = iter(waits)
    got = yield swapping(send), next(waits)
    return (yield hopping(plus(keep, got), LAST_HOP), next(waits))


def summed_near(keep, send, core, waits):
    waits = iter(waits)
    got = yield swapping(send), next(waits)
    near = yield hopping(plus(keep, got), FIRST_HOP), next(waits)
    back = yield swapping(half_of(near, 1, 1 - core)), next(waits)
    return half_of(near, 1, core), back


def summed_over_line(total, waits):
    if lax.axis_size("dp") != 4:
        return lax.psum(total, "dp")
    line = lax.axis_index("dp")
    low, high = line & 1, line >> 1
    got = yield exchanging(half_of(total, 1, 1 - low), "dp", 1), next(waits)
    total = plus(half_of(total, 1, low), got)
    got = yield exchanging(half_of(total, 1, 1 - high), "dp", 2), next(waits)
    total = plus(half_of(total, 1, high), got)
    got = yield exchanging(total, "dp", 2), next(waits)
    total = ordered(high == 0, total, got)
    got = yield exchanging(total, "dp", 1), next(waits)
    return ordered(low == 0, total, got)


def ends_kernel(meta, *refs):
    out = refs[-1]
    for core in range(2):
        for distance in range(GROUP):

            @pl.when((meta[0] == core) & ((pl.program_id(1) ^ meta[1]) == distance))
            def _(ref=refs[core * GROUP + distance]):
                out[0] = ref[...].astype(f32)


def ends_rows(meta, first, second):
    rows, width = first[0].shape
    tile = rows // 2
    return pl.pallas_call(
        ends_kernel,
        grid_spec=pltpu.PrefetchScalarGridSpec(
            num_scalar_prefetch=1,
            grid=(rows // tile, GROUP),
            in_specs=[pl.BlockSpec((tile, width), lambda j, n, m: (j, 0))] * (2 * GROUP),
            out_specs=pl.BlockSpec((1, tile, width), lambda j, n, m: (n, j, 0)),
        ),
        out_shape=jax.ShapeDtypeStruct((GROUP, rows, width), f32),
        cost_estimate=cost(flops=GROUP * rows * width, bytes_accessed=16 * GROUP * rows * width, transcendentals=0),
        compiler_params=pltpu.CompilerParams(vmem_limit_bytes=60 * MIB),
        name="ends_rows",
    )(meta, *first, *second)


def feed_out_kernel(meta, lower, upper, to_lower, to_upper, up, down):
    for core, mine, other in ((0, lower, to_lower), (1, upper, to_upper)):
        for same, ref in ((True, mine), (False, other)):

            @pl.when((meta[0] == core) & ((pl.program_id(1) == core) == same))
            def _(ref=ref):
                up[...] = ref[0].astype(f32).T
                down[...] = ref[1].astype(f32)


def feed_out(meta, lower, upper, to_lower, to_upper):
    _, units, width = lower.shape
    tile = units // 2
    return pl.pallas_call(
        feed_out_kernel,
        grid_spec=pltpu.PrefetchScalarGridSpec(
            num_scalar_prefetch=1,
            grid=(units // tile, 2),
            in_specs=[pl.BlockSpec((2, tile, width), lambda j, h, m: (0, j, 0))] * 4,
            out_specs=[
                pl.BlockSpec((width, tile), lambda j, h, m: (0, h * 2 + j)),
                pl.BlockSpec((tile, width), lambda j, h, m: (h * 2 + j, 0)),
            ],
        ),
        out_shape=[jax.ShapeDtypeStruct((width, 2 * units), f32), jax.ShapeDtypeStruct((2 * units, width), f32)],
        cost_estimate=cost(flops=4 * units * width, bytes_accessed=32 * units * width, transcendentals=0),
        compiler_params=pltpu.CompilerParams(vmem_limit_bytes=60 * MIB),
        name="feed_out",
    )(meta, lower, upper, to_lower, to_upper)


def handed_over(steps, pairs, pause=0):
    total = yield from steps
    if pause:
        yield [], pause
    got = yield Send(lambda v: lax.ppermute(v, "section", pairs), total), 1
    return total, got


UP, DOWN = [(0, 1)], [(1, 0)]


def summed_everywhere(value):
    for axis in ("section", "tensor", "dp"):
        count = lax.axis_size(axis)
        if count & (count - 1):
            value = lax.psum(value, axis)
            continue
        distance = 1
        while distance < count:
            got = yield exchanging(value, axis, distance), 1
            value = value + got
            distance *= 2
    return value


def in_order(own, near, near_too, far, far_too, core, chip):
    first = core == 0
    last = jnp.concatenate([jnp.where(first, far, far_too), jnp.where(first, far_too, far)], axis=-1)
    by_distance = jnp.stack([own, jnp.where(first, near, near_too), jnp.where(first, near_too, near), last])
    rows = [lax.dynamic_index_in_dim(by_distance, quarter ^ chip, 0, keepdims=False) for quarter in CHIPS]
    return jnp.concatenate(rows, axis=-1)


PIECES = ("own", "near", "near_too", "far", "far_too")
GROUPS = (("own",), ("near", "near_too"), ("far", "far_too"))
OWN, NEAR, FAR = range(3)


def on_row(
    ends_in, lengths, ln_gains, ln_biases, w_qkv, qv_bias, w_out, w_up, up_bias, w_down, out_biases
):
    core = lax.axis_index("section")
    chip = lax.axis_index("tensor")
    first_core = core == 0
    micro, rows_here, seg = ends_in.shape[1:4]
    ends = ends_in.reshape(micro * rows_here, seg, D)
    lo_segment, hi_segment = core, 3 - core
    n_qv = qv_bias.shape[-1]
    n_up = up_bias.shape[-1]

    def row_from(section):
        return [
            hopping(
                lax.dynamic_index_in_dim(ends, chip ^ k, 0, keepdims=False),
                [(place(section, t), place(core_of(t), t ^ k)) for t in CHIPS if k or core_of(t) != section],
            )
            for k in CHIPS
        ]

    def chosen_rows(section, got):
        here = lax.dynamic_index_in_dim(ends, chip, 0, keepdims=False)
        got = [jnp.where(core == section, here, got[0]), *got[1:]]

        def pick(k):
            return jnp.where(k == 0, got[0], jnp.where(k == 1, got[1], jnp.where(k == 2, got[2], got[3])))

        return jnp.concatenate([pick(chip ^ lo_segment), pick(chip ^ hi_segment)])

    def segment_of(row, distance):
        return jnp.where(chip ^ distance == lo_segment, row[:seg], row[seg:])

    def row_to(section, row, distances):
        got = []
        for k in distances:
            pairs = [(place(core_of(t), t ^ k), place(section, t)) for t in CHIPS if k or core_of(t) != section]
            got.append(hopping(segment_of(row, k), pairs))
        return got

    def both(mine):
        theirs = swap(mine)
        return (jnp.where(first_core, mine, theirs), jnp.where(first_core, theirs, mine))

    chains = Chains()
    bias = jnp.concatenate([qv_bias[0].reshape(-1), up_bias[0]])
    bias_rows = -(-bias.shape[0] // D)
    bias = jnp.pad(bias, (0, bias_rows * D - bias.shape[0])).reshape(-1, D)
    extra = jnp.concatenate([bias, ln_gains[0], ln_biases[0], out_biases[0]])
    extra_rows = extra.shape[0]
    extra = jnp.concatenate(three_rounded(extra))
    extra = jnp.pad(extra, ((0, BIAS_ROWS - extra.shape[0]), (0, 0)))

    def extra_of(pack):
        rows = pack[-BIAS_ROWS:].astype(f32)
        return (rows[:extra_rows] + rows[extra_rows : 2 * extra_rows]) + rows[2 * extra_rows : 3 * extra_rows]

    pack = jnp.concatenate([jnp.swapaxes(w_qkv[0], 1, 2).reshape(-1, D), w_out[0], extra])
    sends = row_from(0)
    attention_own = both(pack)
    x = chosen_rows(0, [send.transfer(send.value) for send in sends])
    feed_mine = tie(jnp.concatenate([w_up[0].T[None], w_down]), x)
    feed_own = both(feed_mine)

    def gathered_heads(own, pieces, waits):
        pieces["own"] = own
        near = yield hopping(own, FIRST_HOP), waits[0]
        pieces["near"], pieces["near_too"] = near, swap(near)
        heads = half_of(near[: 4 * n_qv].reshape(4, n_qv, D), 1, core).reshape(-1, D)
        far = yield hopping(jnp.concatenate([heads, near[4 * n_qv :]]), SECOND_HOP), waits[1]
        pieces["far"], pieces["far_too"] = far, swap(far)

    def gathered_feed(own, pieces, waits):
        near = yield hopping(own, FIRST_HOP), waits[0]
        pieces += [own.reshape(2, 2, -1, D), near, swap(near)]
        far = yield hopping(half_of(near, 1, core), SECOND_HOP), waits[1]
        pieces += [far, swap(far)]

    attention, feeding = ({}, {}), ([], [])
    x, attention_own = tie((x, attention_own))

    def bias_of(name, layer, start, size):
        part = extra_of(attention[layer][name])[:bias_rows].reshape(-1)[start : start + size]
        if name == "far":
            part = half_of(part, 0, core)
        if name == "far_too":
            part = half_of(part, 0, 1 - core)
        return part

    six = [extra_of(own)[bias_rows:] for own in attention_own]
    gains, shifts, end_biases = ([layer_six[n : n + 2] for layer_six in six] for n in (0, 2, 4))

    length = lax.dynamic_index_in_dim(lengths.reshape(-1), chip, 0, keepdims=False)
    segments = jnp.stack([lo_segment, hi_segment, 1 - core, 2 + core])
    positions = (segments[:, None] * seg + jnp.arange(seg)[None]).reshape(-1)
    kcol = key_columns(positions, length)
    heads_here = n_qv // HEAD
    quarters = {"own": chip, "near": chip ^ (1 + core), "near_too": chip ^ (2 - core), "far": chip ^ 3, "far_too": chip ^ 3}
    pairs_of = {name: n_qv // 128 // (2 if name.startswith("far") else 1) for name in PIECES}
    across = {"own": "own", "near": "near_too", "near_too": "near", "far": "far_too", "far_too": "far"}

    def head_slopes(name):
        head = quarters[name] * heads_here + jnp.arange(heads_here)
        if name == "far":
            head = half_of(head, 0, core)
        if name == "far_too":
            head = half_of(head, 0, 1 - core)
        return jnp.exp2(-8.0 * (head + 1).astype(f32) / HEADS)

    slopes = {name: head_slopes(name) for name in PIECES}

    def group_meta(names):
        starts, at = {}, 0
        for name in names:
            starts[name] = at
            at += pairs_of[name]
        table = [starts[across[name]] + n for name in names for n in range(pairs_of[name])]
        return jnp.concatenate([core[None].astype(jnp.int32), jnp.array(table, jnp.int32)])

    groups = [
        [
            dict(names=names, meta=group_meta(names), qcol=query_columns(jnp.concatenate([slopes[name] for name in names])))
            for names in GROUPS
        ]
        for layer in range(2)
    ]

    def pieces_of(layer, index):
        return [attention[layer][name] for name in groups[layer][index]["names"]]

    def heads_bias(layer, index):
        names = groups[layer][index]["names"]
        return jnp.stack(
            [
                jnp.concatenate([bias_of(name, layer, 0, n_qv) for name in names]),
                jnp.zeros((sum(pairs_of[name] for name in names) * 128,), f32),
                jnp.concatenate([bias_of(name, layer, n_qv, n_qv) for name in names]),
            ]
        )[:, None]

    meta = core[None].astype(jnp.int32)

    def into_heads(layer, index, normed):
        q, kv = project_heads(normed, pieces_of(layer, index), heads_bias(layer, index))
        return q, kv, swap(kv)

    def attended(layer, index, projected):
        group = groups[layer][index]
        return tuple(projected) + tuple(attend(group["meta"], *projected, kcol, group["qcol"]))

    def fed(layer, x, saved):
        vectors = eight_rows(end_biases[layer][0], gains[layer][1], shifts[layer][1], end_biases[layer][1])
        pieces = [p for index in range(len(saved)) for p in pieces_of(layer, index)]
        bias = [bias_of("own", layer, 2 * n_qv, n_up)]
        bias = [half_of(bias[0], 0, core), half_of(bias[0], 0, 1 - core)]
        bias += [bias_of(name, layer, 2 * n_qv, n_up) for name in ("near", "near_too")]
        bias = jnp.concatenate([part.reshape(STEPS, -1) for part in bias], axis=1)[:, None]
        return feed(meta, x, [v[3] for v in saved], pieces, vectors, bias, feeding[layer])

    def fed_last(layer, middle, total):
        following = min(layer + 1, 1)
        vectors = eight_rows(jnp.zeros((D,), f32), gains[following][0], shifts[following][0])
        bias = [bias_of(name, layer, 2 * n_qv, n_up).reshape(STEPS, -1) for name in ("far", "far_too")]
        return feed_last(middle, total, vectors, jnp.concatenate(bias, axis=1).reshape(1, -1), feeding[layer])

    kept = [None, None]
    chains.start(gathered_heads(attention_own[0], attention[0], (1, 1)))
    x = chains.launch(x)
    normed = None
    for layer in range(2):
        saved = [None] * 3
        if layer == 0:
            first_vectors = eight_rows(jnp.zeros((D,), f32), gains[0][0], shifts[0][0])
            q, kv, normed = project_heads(x, pieces_of(0, OWN), heads_bias(0, OWN), first_vectors)
            projected, feed_own = lax.optimization_barrier(((q, kv, swap(kv)), feed_own))
        else:
            projected = into_heads(layer, OWN, normed)
        saved[OWN] = attended(layer, OWN, projected)
        (normed, saved[OWN], feed_own), *_ = chains.stepped(
            (normed, saved[OWN], feed_own),
            [] if layer else [lambda: gathered_feed(feed_own[0], feeding[0], (2, 1))],
        )
        saved[NEAR] = attended(layer, NEAR, into_heads(layer, NEAR, normed))
        normed, saved[NEAR] = chains.step((normed, saved[NEAR]))
        saved[FAR] = attended(layer, FAR, into_heads(layer, FAR, normed))
        saved = chains.step(saved)
        slope, hidden, after, middle, total = fed(layer, x, saved)
        (total, attention_own, ends), following = chains.step(
            (total, attention_own, ends),
            lambda: once(row_from(1), 1) if layer else gathered_heads(attention_own[1], attention[1], (2, 1)),
        )
        slope_last, hidden_last, result, normed_next = fed_last(layer, middle, total)
        kept[layer] = (x, normed, saved, after, middle, (slope, slope_last), (hidden, hidden_last))
        if layer == 0:
            (x, normed, feed_own), _ = chains.step(
                (result, normed_next, feed_own), lambda: gathered_feed(feed_own[1], feeding[1], (3, 1))
            )
    x, *sent_back = chains.step(result, lambda: once(row_to(1, result, (0, 1)), 1))
    grad = chosen_rows(1, following.result)

    def heads_gradients(layer, index, low):
        group = groups[layer][index]
        q, kv, kvo, o, qx = kept[layer][2][index]
        return attend_back(group["meta"], q, kv, kvo, kcol, qx, low, o, pieces_of(layer, index))

    def weight_gradients(layer, index, grads, low, so_far, last):
        group = groups[layer][index]
        norm = (kept[layer][0], low, gains[layer][0]) if last else None
        return project_back(
            meta, group["names"], *grads, kept[layer][2][index][3], kept[layer][1], low, pieces_of(layer, index), so_far, norm
        )

    def sums_of(layer, results, unit_sums, sums_one, sums_two):
        parts = {}
        for index, group in enumerate(groups[layer]):
            at = 0
            for name in group["names"]:
                size = pairs_of[name] * 128
                parts[name] = results[index][2][0:2, at : at + size]
                at += size
        unit_sums = unit_sums[:, 0]
        part = unit_sums.shape[1] // 8

        def unit_part(start, count):
            return unit_sums[:, start * part : (start + count) * part].reshape(-1)

        own_keep, own_send = unit_part(0, 1), unit_part(1, 1)
        own = jnp.concatenate([jnp.where(first_core, own_keep, own_send), jnp.where(first_core, own_send, own_keep)])
        return jnp.concatenate(
            [
                jnp.stack([sums_one[0], sums_two[0], sums_one[1], sums_two[1], sums_two[2], sums_two[3]]),
                in_order(*[parts[name] for name in PIECES], core, chip),
                in_order(own, unit_part(2, 2), unit_part(4, 2), unit_part(6, 1), unit_part(7, 1), core, chip).reshape(-1, D),
            ]
        )

    def feed_gradients(layer, grad):
        _, _, _, after, middle, slope, hidden = kept[layer]
        return feed_back(meta, grad, middle, after, gains[layer][1], slope, hidden, feeding[layer])

    def backward(layer, grad, others, new, late):
        keep, send, unit_sums, low, sums_two = feed_gradients(layer, grad)
        (low, keep, send, others), feed_sums, *started = chains.step(
            (low, keep, send, others),
            lambda: handed_over(
                summed_feed(meta, keep, send, (1, 2, 1, 1, 2, 1, 1) if layer else (1, 2, 1, 1, 2, 2, 1)), UP if layer else DOWN, 4 if layer else 0
            ),
            *(lambda make=make: make(others) for make in new),
        )

        results = [None] * 3
        dq_far, dkv_far, sent_far = heads_gradients(layer, FAR, low)
        (low, sent_far), got_far = chains.step((low, sent_far), lambda: once(swapping(sent_far), 1))
        dq_near, dkv_near, sent_near = heads_gradients(layer, NEAR, low)
        (low, sent_near), got_near = chains.step((low, sent_near), lambda: once(swapping(sent_near), 1))
        results[FAR] = weight_gradients(layer, FAR, (dq_far, dkv_far, got_far.result), low, None, False)
        (low, results[FAR]), far_sum, *started_late = chains.stepped(
            (low, results[FAR]), [lambda: summed_far(*results[FAR][:2], (1, 1)), *late]
        )
        results[NEAR] = weight_gradients(layer, NEAR, (dq_near, dkv_near, got_near.result), low, results[FAR][3], False)
        (low, results[NEAR]), near_sum = chains.step(
            (low, results[NEAR]), lambda: summed_near(*results[NEAR][:2], core, (1, 2, 1))
        )
        dq_own, dkv_own, sent_own = heads_gradients(layer, OWN, low)
        (low, sent_own), got_own = chains.step((low, sent_own), lambda: once(swapping(sent_own), 1))
        low, dq_own, dkv_own = chains.step((low, dq_own, dkv_own))
        results[OWN] = weight_gradients(layer, OWN, (dq_own, dkv_own, got_own.result), low, results[NEAR][3], True)
        grad, sums_one = results[OWN][3:]
        sums = sums_of(layer, results, unit_sums, sums_one, sums_two)
        return grad, results[OWN], sums, feed_sums, near_sum, far_sum, started + started_late

    grad, own, sums_upper, upper_feed, near_sum, far_sum, again = backward(
        1, grad, x, [lambda row: once(row_to(1, row, (2, 3)), 1)], []
    )
    sent_back += again
    (grad, own), own_sum = chains.step((grad, own), lambda: once(swapping(own[1]), 1))

    def summed_heads(pairs, keep, own_sum, near_sum, far_sum):
        total = plus(keep, own_sum.result, *near_sum.result, far_sum.result)
        return handed_over(summed_over_line(total, iter((1, 1, 1, 1))), pairs)

    upper_parts = own[0], own_sum, near_sum, far_sum
    grad, own, sums_lower, lower_feed, near_sum, far_sum, (upper_heads,) = backward(
        0, grad, (), [lambda _: summed_heads(UP, *upper_parts)], []
    )
    (grad, sums_lower, own), own_sum, zero, both_sums = chains.step(
        (grad, sums_lower, own),
        lambda: once(swapping(own[1]), 1),
        lambda: once(row_to(0, grad, (0,)), 1),
        lambda: summed_everywhere(jnp.stack([sums_lower, sums_upper])),
    )
    grad, lower_heads, three, one = chains.step(
        grad,
        lambda: summed_heads(DOWN, own[0], own_sum, near_sum, far_sum),
        lambda: once(row_to(0, grad, (3,)), 1),
        lambda: once(row_to(0, grad, (1,)), 1),
    )
    grad, two = chains.step(grad, lambda: once(row_to(0, grad, (2,)), 1))
    grad = chains.step(grad)
    first_rows = [zero, one, two, three]

    def feed_outputs():
        (lower, to_lower), (upper, to_upper) = lower_feed.result, upper_feed.result
        return feed_out(meta, lower, upper, to_lower, to_upper)

    def ends_outputs():
        place_here = jnp.stack([core, chip]).astype(jnp.int32)
        first, second = [chain.result[0] for chain in first_rows], [*sent_back[0].result, *sent_back[1].result]
        own_core = core_of(chip)
        first[0] = jnp.where(own_core == 0, segment_of(grad, 0), first[0])
        second[0] = jnp.where(own_core == 1, segment_of(result, 0), second[0])
        rows = ends_rows(place_here, first, second)
        return rows.reshape(1, micro, rows_here, seg, D)

    ready, waiting = {}, {"feed": (feed_outputs, [lower_feed, upper_feed]), "ends": (ends_outputs, first_rows)}
    while any(not chain.done for chain in chains.running):
        for name in list(waiting):
            make, needed = waiting[name]
            if all(chain.done for chain in needed):
                ready[name] = make()
                del waiting[name]
        ready, grad = chains.step((ready, grad))
    for name, (make, _) in waiting.items():
        ready[name] = make()
    ends_out, (grad_up, grad_down) = ready["ends"], ready["feed"]
    (lower, to_lower), (upper, to_upper) = lower_heads.result, upper_heads.result
    attention_grads = jnp.where(
        first_core, jnp.concatenate([lower, to_lower], axis=1), jnp.concatenate([to_upper, upper], axis=1)
    ).astype(f32)
    both_sums = both_sums.result
    sums = jnp.where(first_core, both_sums[0], both_sums[1])
    grad_qv = lax.dynamic_slice_in_dim(sums[6:8], chip * n_qv, n_qv, 1)[None]
    grad_up_bias = lax.dynamic_slice_in_dim(sums[8:].reshape(-1), chip * n_up, n_up, 0)[None]
    return (
        ends_out,
        sums[0:2][None],
        sums[2:4][None],
        jnp.swapaxes(attention_grads[:3], 1, 2)[None],
        grad_qv,
        attention_grads[3:],
        grad_up[None],
        grad_up_bias,
        grad_down[None],
        sums[4:6][None],
    )


def solution(mesh):
    return jax.shard_map(
        on_row if one_row_a_chip(mesh) else on_device,
        mesh=mesh,
        in_specs=(
            P("section", None, "dp", "tensor", None),
            P(None, "dp"),
            P("section", None, None),
            P("section", None, None),
            P("section", None, None, "tensor"),
            P("section", None, "tensor"),
            P("section", "tensor", None),
            P("section", None, "tensor"),
            P("section", "tensor"),
            P("section", "tensor", None),
            P("section", None, None),
        ),
        out_specs=(
            P("section", None, "dp", "tensor", None),
            P("section", None, None),
            P("section", None, None),
            P("section", None, None, "tensor"),
            P("section", None, "tensor"),
            P("section", "tensor", None),
            P("section", None, "tensor"),
            P("section", "tensor"),
            P("section", "tensor", None),
            P("section", None, None),
        ),
        check_vma=False,
    )
```
